32 devices in a mesh: groups: 2 (over y), replica: 4 (over z), tensor: 4 (over x, core).
Axes of the slice: x: 2, y: 2, z: 4, core: 2. Of those that a mesh axis runs over, the one named last changes fastest.
Arguments:
- queries: bfloat16 [1024, 2, 4096], P(('groups', 'replica'), None, 'tensor'), parts along dimension 0, may hold values from -8 to 8
- recent_keys: bfloat16 [1024, 2, 1024], P(('groups', 'replica'), None, 'tensor'), parts along dimension 0, may hold values from -12 to 12
- recent_values: bfloat16 [1024, 2, 1024], P(('groups', 'replica'), None, 'tensor'), parts along dimension 0, may hold values from -24 to 24
- prefix_key_value: bfloat16 [8, 2, 4096, 1024], P(('groups', 'replica'), None, None, 'tensor'), parts along dimension 0, may hold values from -6 to 6
- prefix_length_each: int32 [1024], P(('groups', 'replica')), parts along dimension 0, may hold values from 512 to 4096, as said below
- batch_adapter_index: int32 [128], P(('groups', 'replica')), parts along dimension 0, may hold values from 0 to 63, as said below
- adapter_table_row: int32 [128], P('groups'), parts along dimension 0, may hold values from 0 to 63, as said below
- down_weight_table: bfloat16 [64, 16, 4096], P('replica', None, 'tensor'), may hold values from -2 to 2
- up_weight_table: bfloat16 [64, 16, 8192], P('replica', None, 'tensor'), may hold values from -1.5 to 1.5
- output_weight: bfloat16 [4096, 8192], P('tensor'), may hold values from -2 to 2
Outputs:
- block_out: bfloat16 [1024, 2, 8192], P(('groups', 'replica'), None, 'tensor'), parts along dimension 0
The draws below stay inside these ranges and needn't reach their ends.
There are 2 independent parts, one for each index of `groups`. The reference program is written for one: setup_inputs(seed, part) draws one part's arguments, and reference() takes and returns one part's arrays. A program takes and returns all parts, laid end to end along the dimension named above; an argument that names none is the same for every part. Nothing has to cross between parts.
Inputs may be any that keep to these rules, and one draw needn't show every extreme that they name: `prefix_length_each`: the largest length equals 4096 in every draw. adapter_table_row is a permutation of 0 to 63; rows k * 16 to (k + 1) * 16 - 1 of the tables lie on replica k. `batch_adapter_index`: of the 16 fork batches of one replica, at most 8 name adapters whose table rows lie on one replica; every draw reaches 8. An adapter may serve several batches.
All inputs are finite; a program needn't handle non-finite values.
Results may differ from the reference program's by a relative error of at most 0.0095.
Values may be sent and summed in bfloat16 or wider, within the bound.
No kernel may reach another device: no remote copies, remote signals or barrier semaphores. Data moves between devices by JAX's collectives and lax.ppermute only.
A program may use at most 192 MiB of HBM per device.

```python
import math
import jax
import jax.numpy as jnp
from jax import lax

MODEL_WIDTH = 8192
HD = 128
KVH = 8
GROUP = 4
ADAPTER_RANK = 16
DECODE_STEPS = 2
PREFIX = 4096
BATCH_FORKS = 8
REPLICA_BATCHES = 16
ADAPT_DEV = 16
QUERY_FEATURES = 4096
FORKS_DEV = 128
FORKS = 512
ADAPTER_TOTAL = 64
N_REPLICA = 4


def shared_rows(key):
    return jax.random.permutation(jax.random.fold_in(key, 17), ADAPTER_TOTAL).astype(jnp.int32)


def draw_queries(key, part):
    key = jax.random.fold_in(key, 5)
    first_key = jax.random.fold_in(key, 0)
    drawn = jnp.clip(jax.random.normal(first_key, (FORKS, DECODE_STEPS, QUERY_FEATURES), jnp.float32), -6.0, 6.0)
    return drawn.astype(jnp.bfloat16)


def draw_prefix_key_value(key, part):
    key = jax.random.fold_in(key, 3)
    first_key, second_key = jax.random.split(key)
    values = jnp.clip(jax.random.normal(second_key, (N_REPLICA, PREFIX, KVH * HD), jnp.float32), -6.0, 6.0)
    key_rows = jnp.clip(jax.random.normal(first_key, (N_REPLICA, PREFIX, KVH * HD), jnp.float32), -6.0, 6.0)
    return jnp.stack([key_rows, values], axis=1).astype(jnp.bfloat16)


def draw_prefix_length_each(key, part):
    key = jax.random.fold_in(key, 7)
    cap_key, raw_key, place_key = jax.random.split(key, 3)
    lowest = PREFIX // 8
    replica_caps = jax.random.randint(cap_key, (N_REPLICA, 1), lowest, PREFIX + 1)
    raw_bits = jax.random.randint(raw_key, (N_REPLICA, FORKS_DEV), 0, 1 << 20)
    lengths = (lowest + raw_bits % (replica_caps - lowest + 1)).reshape(FORKS)
    longest_at = jax.random.randint(place_key, (), 0, FORKS)
    return lengths.at[longest_at].set(PREFIX).astype(jnp.int32)


def draw_adapter_table_row(key, part):
    mapping = shared_rows(key)
    return mapping


def pick_owners(sub_key):
    return jax.random.permutation(sub_key, N_REPLICA)


def pick_order(sub_key):
    return jax.random.permutation(sub_key, REPLICA_BATCHES)


def draw_batch_adapter_index(key, part):
    mapping = shared_rows(key)
    inverse = jnp.argsort(mapping).astype(jnp.int32)
    key = jax.random.fold_in(key, 11)
    owner_key, flag_key, local_key, order_key = jax.random.split(key, 4)
    capacity = max(2, 2 * REPLICA_BATCHES // N_REPLICA)
    group_count = REPLICA_BATCHES // capacity
    owner_order = jax.vmap(pick_owners)(jax.random.split(owner_key, N_REPLICA))
    flag_bits = jax.random.randint(flag_key, (N_REPLICA, REPLICA_BATCHES), 0, 2)
    group_of = jnp.arange(REPLICA_BATCHES) // capacity
    flag_bits = jnp.where(group_of[None, :] == 0, 1, flag_bits)
    first_owner = owner_order[:, group_of]
    other_owner = owner_order[:, group_count + group_of]
    owner_of = jnp.where(flag_bits == 1, first_owner, other_owner)
    local_pick = jax.random.randint(local_key, (N_REPLICA, REPLICA_BATCHES), 0, ADAPT_DEV)
    chosen = inverse[owner_of * ADAPT_DEV + local_pick]
    slot_order = jax.vmap(pick_order)(jax.random.split(order_key, N_REPLICA))
    chosen = jnp.take_along_axis(chosen, slot_order, axis=1)
    return chosen.reshape(N_REPLICA * REPLICA_BATCHES).astype(jnp.int32)


def block_levels(key, dims, pieces, smallest, top_value):
    def one(axis_at, blocks):
        heights = jax.random.uniform(jax.random.fold_in(jax.random.fold_in(key, 6), axis_at), (blocks,), jnp.float32, smallest / len(pieces), top_value / len(pieces))
        return jnp.repeat(jnp.exp(heights), dims[axis_at] // blocks).reshape((-1,) + (1,) * (len(dims) - axis_at - 1))

    gain = one(*pieces[0])
    for cut in pieces[1:]:
        gain = gain * one(*cut)
    return gain


def scatter_about(key, dims, width, reach, shards=(), kind=jnp.bfloat16):
    entries = jax.random.normal(key, dims, jnp.float32) * width
    if len(shards) > 0:
        entries = block_levels(key, dims, shards, -0.22, 0.18) * entries
    return jnp.clip(entries, min=-reach, max=reach).astype(kind)


def setup_inputs(seed: int = 0, part: int = 0) -> dict:
    key_list = jax.random.split(jax.random.key(seed), 11)
    part_keys = jax.random.split(jax.random.fold_in(key_list[10], part), 11)
    queries = draw_queries(jax.random.fold_in(jax.random.fold_in(key_list[10], part), 71), part)
    recent_keys = scatter_about(part_keys[1], (FORKS, DECODE_STEPS, KVH * HD), 2.0, 12.0, ((0, 4), (2, 4)))
    recent_values = scatter_about(part_keys[2], (FORKS, DECODE_STEPS, KVH * HD), 4.0, 24.0, ((0, 4), (2, 4)))
    prefix_key_value = draw_prefix_key_value(jax.random.fold_in(jax.random.fold_in(key_list[10], part), 71), part)
    prefix_length_each = draw_prefix_length_each(jax.random.fold_in(jax.random.fold_in(key_list[10], part), 71), part)
    batch_adapter_index = draw_batch_adapter_index(jax.random.fold_in(jax.random.fold_in(key_list[10], part), 71), part)
    adapter_table_row = draw_adapter_table_row(jax.random.fold_in(jax.random.fold_in(key_list[10], part), 71), part)
    down_weight_table = scatter_about(key_list[7], (ADAPTER_TOTAL, ADAPTER_RANK, QUERY_FEATURES), (QUERY_FEATURES // 512) ** -0.5, 2.0, ((0, 4), (2, 4)))
    up_weight_table = scatter_about(key_list[8], (ADAPTER_TOTAL, ADAPTER_RANK, MODEL_WIDTH), ADAPTER_RANK ** -0.5, 1.5, ((0, 4), (2, 4)))
    output_weight = scatter_about(key_list[9], (QUERY_FEATURES, MODEL_WIDTH), (QUERY_FEATURES // 512) ** -0.5, 2.0, ((0, 4),))
    return {"queries": queries, "recent_keys": recent_keys, "recent_values": recent_values, "prefix_key_value": prefix_key_value, "prefix_length_each": prefix_length_each, "batch_adapter_index": batch_adapter_index, "adapter_table_row": adapter_table_row, "down_weight_table": down_weight_table, "up_weight_table": up_weight_table, "output_weight": output_weight}


def replica_pass(packed):
    query_rows, new_key, new_value, cache, lengths = packed
    forks_total = query_rows.shape[0]
    score_scale = 1.0 / math.sqrt(HD)
    query_heads = query_rows.astype(jnp.float32).reshape(forks_total, DECODE_STEPS, KVH, GROUP, HD).transpose(2, 0, 1, 3, 4)
    key_rows = cache[0].astype(jnp.float32).reshape(PREFIX, KVH, HD).transpose(1, 0, 2)
    value_rows = cache[1].astype(jnp.float32).reshape(PREFIX, KVH, HD).transpose(1, 0, 2)
    fresh_keys = new_key.astype(jnp.float32).reshape(forks_total, DECODE_STEPS, KVH, HD).transpose(2, 0, 1, 3)
    fresh_values = new_value.astype(jnp.float32).reshape(forks_total, DECODE_STEPS, KVH, HD).transpose(2, 0, 1, 3)
    visible = jnp.arange(PREFIX, dtype=jnp.int32)[None, :] < lengths[:, None]
    causal = jnp.arange(DECODE_STEPS)[None, :] <= jnp.arange(DECODE_STEPS)[:, None]

    def head_pass(inner):
        head_query, head_keys, head_values, head_fresh_keys, head_fresh_values = inner
        scores = jnp.einsum('fsgd,pd->fsgp', head_query, head_keys) * score_scale
        scores = jnp.where(visible[:, None, None, :], scores, -jnp.inf)
        own_scores = jnp.einsum('fsgd,ftd->fsgt', head_query, head_fresh_keys) * score_scale
        own_scores = jnp.where(causal[None, :, None, :], own_scores, -jnp.inf)
        top_score = jnp.maximum(lax.optimization_barrier(jnp.max(scores, axis=-1)), lax.optimization_barrier(jnp.max(own_scores, axis=-1)))
        weights = jnp.exp(scores - top_score[..., None])
        own_weights = jnp.exp(own_scores - top_score[..., None])
        totals = lax.optimization_barrier(jnp.sum(weights, axis=-1)) + lax.optimization_barrier(jnp.sum(own_weights, axis=-1))
        rounded = lax.optimization_barrier((weights.astype(jnp.bfloat16), own_weights.astype(jnp.bfloat16)))
        mixture = jnp.einsum('fsgp,pd->fsgd', rounded[0].astype(jnp.float32), head_values)
        mixture = mixture + jnp.einsum('fsgt,ftd->fsgd', rounded[1].astype(jnp.float32), head_fresh_values)
        return mixture / totals[..., None]
    heads_out = lax.map(head_pass, (query_heads, key_rows, value_rows, fresh_keys, fresh_values))
    return heads_out.transpose(1, 2, 0, 3, 4).reshape(forks_total, DECODE_STEPS, QUERY_FEATURES).astype(jnp.bfloat16)

def reference(queries, recent_keys, recent_values, prefix_key_value, prefix_length_each, batch_adapter_index, adapter_table_row, down_weight_table, up_weight_table, output_weight):
    attended = lax.map(replica_pass, (queries.reshape(N_REPLICA, FORKS_DEV, DECODE_STEPS, QUERY_FEATURES), recent_keys.reshape(N_REPLICA, FORKS_DEV, DECODE_STEPS, KVH * HD), recent_values.reshape(N_REPLICA, FORKS_DEV, DECODE_STEPS, KVH * HD), prefix_key_value, prefix_length_each.reshape(N_REPLICA, FORKS_DEV)))
    flat_rows = attended.reshape(FORKS * DECODE_STEPS, QUERY_FEATURES)
    base_output = jnp.dot(flat_rows, output_weight, preferred_element_type=jnp.float32)
    adapter_table_count = adapter_table_row[batch_adapter_index]
    picked_down_weight = down_weight_table[adapter_table_count].astype(jnp.float32)
    picked_up_weight = up_weight_table[adapter_table_count].astype(jnp.float32)
    grouped = attended.reshape(N_REPLICA * REPLICA_BATCHES, BATCH_FORKS * DECODE_STEPS, QUERY_FEATURES).astype(jnp.float32)
    rank_activation = jnp.einsum('brq,bkq->brk', grouped, picked_down_weight, precision=lax.Precision.HIGHEST)
    adapter_output = jnp.einsum('yzh,yhf->yzf', rank_activation, picked_up_weight, precision=lax.Precision.HIGHEST)
    final_output = base_output.reshape(N_REPLICA * REPLICA_BATCHES, BATCH_FORKS * DECODE_STEPS, MODEL_WIDTH) + adapter_output
    return final_output.reshape(FORKS, DECODE_STEPS, MODEL_WIDTH).astype(jnp.bfloat16)
```

```python
import functools
import math

import jax
import jax.numpy as jnp
from jax import lax
from jax.experimental import pallas as pl
from jax.experimental.pallas import tpu as pltpu
from jax.sharding import PartitionSpec as P

HD = 128
NEG = -1e30
LOG2_SCALE = math.log2(math.e) / math.sqrt(HD)
BF16, F32 = jnp.bfloat16, jnp.float32
VMEM = pl.BlockSpec(memory_space=pltpu.VMEM)
SMEM = pl.BlockSpec(memory_space=pltpu.SMEM)
PARAMS = pltpu.CompilerParams(vmem_limit_bytes=58 * 1024 * 1024)


def attention_kernel(
    unit_heads, key_block, q_ref, rk_ref, rv_ref, kv_ref, lens_ref, o_ref,
    s_a, s_b, vaug, mx_a, mx_b, mb, acc, lensb, qs,
):
    steps, forks, width = q_ref.shape
    heads = width // HD
    heads_kv = rk_ref.shape[2] // HD
    group = heads // heads_kv
    head_rows = steps * forks
    rows = unit_heads * head_rows
    units = heads // unit_heads
    prefix = kv_ref.shape[2]
    longest = jnp.max(lens_ref[...])
    blocks = (longest + (key_block - 1)) // key_block
    lens = jnp.broadcast_to(lens_ref[...], (head_rows, HD))
    for i in range(unit_heads):
        lensb[i * head_rows : (i + 1) * head_rows, :] = lens
    for v in range(heads_kv):
        vaug[v, :, 0:HD] = kv_ref[0, 1, :, v * HD : (v + 1) * HD]
        vaug[v, :, HD : 2 * HD] = jnp.ones((prefix, HD), BF16)
    for h in range(heads):
        qs[h * head_rows : (h + 1) * head_rows, :] = q_ref[:, :, h * HD : (h + 1) * HD].reshape(head_rows, HD)
    score_refs, max_refs = (s_a, s_b), (mx_a, mx_b)

    def own_scores(u, t):
        parts = []
        for i in range(unit_heads):
            h = u * unit_heads + i
            v = h // group
            k = rk_ref[t, :, v * HD : (v + 1) * HD].astype(F32)
            for s in range(steps):
                if t <= s:
                    at = h * head_rows + s * forks
                    parts.append(jnp.sum(qs[at : at + forks, :].astype(F32) * k, axis=1, keepdims=True))
                else:
                    parts.append(jnp.full((forks, 1), NEG, F32))
        return jnp.concatenate(parts, axis=0)

    def score_block(u, j, s_ref, mx_ref):
        v = (u * unit_heads) // group
        keys = kv_ref[0, 0, pl.ds(pl.multiple_of(j * key_block, key_block), key_block), v * HD : (v + 1) * HD]
        s = lax.dot_general(
            qs[u * rows : (u + 1) * rows, :], keys, (((1,), (1,)), ((), ())), preferred_element_type=F32
        )
        top = mx_ref[...]
        left = lensb[...] - j * key_block
        lane = lax.broadcasted_iota(jnp.int32, (rows, HD), 1)
        for c in range(key_block // HD):
            part = jnp.where(lane + c * HD < left, s[:, c * HD : (c + 1) * HD], NEG)
            top = jnp.maximum(top, part)
            s_ref[j, :, c * HD : (c + 1) * HD] = part
        mx_ref[...] = top

    def value_block(u, j, s_ref):
        v = (u * unit_heads) // group
        top = mb[...]
        parts = [
            jnp.exp2((s_ref[j, :, c * HD : (c + 1) * HD] - top) * LOG2_SCALE).astype(BF16)
            for c in range(key_block // HD)
        ]
        values = vaug[v, pl.ds(pl.multiple_of(j * key_block, key_block), key_block), :]
        acc[...] += jnp.dot(jnp.concatenate(parts, axis=1), values, preferred_element_type=F32)

    for u in range(units + 1):
        done = u - 1
        if u < units:
            max_refs[u % 2][...] = jnp.full((rows, HD), NEG, F32)
        if u > 0:
            own = [own_scores(done, t) for t in range(steps)]
            top = jnp.max(max_refs[done % 2][...], axis=1, keepdims=True)
            for o in own:
                top = jnp.maximum(top, o)
            mb[...] = jnp.broadcast_to(top, (rows, HD))
            acc[...] = jnp.zeros_like(acc)

        @pl.loop(0, blocks)
        def _(j):
            if u < units:
                score_block(u, j, score_refs[u % 2], max_refs[u % 2])
            if u > 0:
                value_block(done, j, score_refs[done % 2])

        if u > 0:
            weights = [jnp.exp2((o - top) * LOG2_SCALE) for o in own]
            total = acc[:, HD : 2 * HD]
            for w in weights:
                total = total + w
            for i in range(unit_heads):
                h = done * unit_heads + i
                v = h // group
                at = slice(i * head_rows, (i + 1) * head_rows)
                mixed = acc[at, 0:HD]
                for t in range(steps):
                    value = rv_ref[t, :, v * HD : (v + 1) * HD].astype(F32)
                    value = jnp.concatenate([value] * steps, axis=0)
                    mixed = mixed + weights[t][at].astype(BF16).astype(F32) * value
                o_ref[:, h * HD : (h + 1) * HD] = (mixed / total[at]).astype(BF16)


def attention(q, rk, rv, kv, lens):
    steps, forks, width = q.shape
    prefix = kv.shape[2]
    heads_kv = rk.shape[2] // HD
    unit_heads = 2
    key_block = prefix
    rows = unit_heads * steps * forks
    return pl.pallas_call(
        functools.partial(attention_kernel, unit_heads, key_block),
        out_shape=jax.ShapeDtypeStruct((steps * forks, width), BF16),
        in_specs=[VMEM] * 5,
        out_specs=VMEM,
        scratch_shapes=[pltpu.VMEM((prefix // key_block, rows, key_block), F32)] * 2
        + [pltpu.VMEM((heads_kv, prefix, 2 * HD), BF16)]
        + [pltpu.VMEM((rows, HD), F32)] * 3
        + [
            pltpu.VMEM((rows, 2 * HD), F32),
            pltpu.VMEM((rows, HD), jnp.int32),
            pltpu.VMEM((width // HD * steps * forks, HD), BF16),
        ],
        compiler_params=PARAMS,
        cost_estimate=pl.CostEstimate(flops=2 * 10**10, bytes_accessed=6 * 2**20, transcendentals=0),
        name="attention",
    )(q, rk, rv, kv, lens)


def project(attended, weight, column_group, width, add, dtype):
    rows, depth = attended.shape
    tile = 1024 if width % 1024 == 0 else width
    tiles = width // tile

    def kernel(group_ref, a_ref, w_ref, *rest):
        o_ref = rest[-1]
        part = jnp.dot(a_ref[...], w_ref[...], preferred_element_type=F32)
        if len(rest) == 2:
            part = part + rest[0][...].astype(F32)
        o_ref[...] = part.astype(o_ref.dtype)

    in_specs = [
        pl.BlockSpec((rows, depth), lambda i, g: (0, 0)),
        pl.BlockSpec((depth, tile), lambda i, g: (0, g[0] * tiles + i)),
    ]
    operands = [attended, weight]
    if add is not None:
        in_specs.append(pl.BlockSpec((rows, tile), lambda i, g: (0, i)))
        operands.append(add)
    return pl.pallas_call(
        kernel,
        out_shape=jax.ShapeDtypeStruct((rows, width), dtype),
        grid_spec=pltpu.PrefetchScalarGridSpec(
            num_scalar_prefetch=1,
            grid=(tiles,),
            in_specs=in_specs,
            out_specs=pl.BlockSpec((rows, tile), lambda i, g: (0, i)),
        ),
        compiler_params=PARAMS,
        cost_estimate=pl.CostEstimate(
            flops=2 * rows * depth * width, bytes_accessed=2 * depth * width, transcendentals=0
        ),
        name="project",
    )(column_group.reshape(1), *operands)


def pack(down, up, rows_all, place, capacity):
    replicas, batches = rows_all.shape
    stored = down.shape[0]

    def kernel(rows_ref, place_ref, down_ref, up_ref, *outs):
        me = place_ref[0]
        for d in range(1, replicas):
            to = lax.rem(me + d, replicas)
            down_out, up_out = outs[2 * (d - 1)], outs[2 * (d - 1) + 1]

            def step(b, count):
                row = rows_ref[to, b] - me * stored
                mine = (row >= 0) & (row < stored)

                @pl.when(mine)
                def _():
                    down_out[count] = down_ref[row]
                    up_out[count] = up_ref[row]

                return count + mine.astype(jnp.int32)

            lax.fori_loop(0, batches, step, jnp.int32(0))

    shapes = []
    for _ in range(1, replicas):
        shapes.append(jax.ShapeDtypeStruct((capacity,) + down.shape[1:], BF16))
        shapes.append(jax.ShapeDtypeStruct((capacity,) + up.shape[1:], BF16))
    outs = pl.pallas_call(
        kernel,
        out_shape=shapes,
        in_specs=[SMEM, SMEM, VMEM, VMEM],
        out_specs=[VMEM] * len(shapes),
        compiler_params=PARAMS,
        name="pack",
    )(rows_all, place, down, up)
    return outs[0::2], outs[1::2]


def collect(rows_ref, place_ref, replicas, table_refs, selected):
    stored = table_refs[0].shape[0]
    batches = selected.shape[0]
    me = place_ref[0]
    for d in range(replicas):
        owner = lax.rem(me + (replicas - d), replicas)
        source = table_refs[d]

        def step(b, count):
            row = rows_ref[b] - owner * stored
            there = (row >= 0) & (row < stored)

            @pl.when(there)
            def _():
                selected[b] = source[row if d == 0 else count]

            return count + there.astype(jnp.int32)

        lax.fori_loop(0, batches, step, jnp.int32(0))


def batch_mask(rows, forks, batches, rank):
    batch_forks = forks // batches
    row = lax.broadcasted_iota(jnp.int32, (rows, batches * rank), 0)
    column = lax.broadcasted_iota(jnp.int32, (rows, batches * rank), 1)
    return lax.rem(row, forks) // batch_forks == column // rank


def low_rank(attended, forks, own_rows, place, tables):
    replicas = len(tables)
    rows, depth = attended.shape
    batches = own_rows.shape[0]
    rank = tables[0].shape[1]

    def kernel(rows_ref, place_ref, a_ref, *rest):
        o_ref, selected = rest[-2], rest[-1]
        collect(rows_ref, place_ref, replicas, rest[:replicas], selected)
        every = lax.dot_general(
            a_ref[...],
            selected[...].reshape(batches * rank, depth),
            (((1,), (1,)), ((), ())),
            preferred_element_type=F32,
        )
        every = jnp.where(batch_mask(rows, forks, batches, rank), every, 0.0)
        total = every[:, 0:HD]
        for c in range(1, batches * rank // HD):
            total = total + every[:, c * HD : (c + 1) * HD]
        o_ref[...] = total

    return pl.pallas_call(
        kernel,
        out_shape=jax.ShapeDtypeStruct((rows, HD), F32),
        in_specs=[SMEM, SMEM] + [VMEM] * (1 + replicas),
        out_specs=VMEM,
        scratch_shapes=[pltpu.VMEM((batches, rank, depth), BF16)],
        compiler_params=PARAMS,
        name="low_rank",
    )(own_rows, place, attended, *tables)


def finish(base, received, ranks, forks, own_rows, place, tables):
    replicas = len(tables)
    rows, width = base.shape
    batches = own_rows.shape[0]
    rank = tables[0].shape[1]
    n_received, n_ranks = len(received), len(ranks)
    steps = rows // forks

    def kernel(rows_ref, place_ref, base_ref, *rest):
        received_refs = rest[:n_received]
        rank_refs = rest[n_received : n_received + n_ranks]
        table_refs = rest[n_received + n_ranks : -2]
        o_ref, selected = rest[-2], rest[-1]
        collect(rows_ref, place_ref, replicas, table_refs, selected)
        total = rank_refs[0][...]
        for r in rank_refs[1:]:
            total = total + r[...]
        spread = jnp.concatenate([total] * (batches * rank // HD), axis=1)
        spread = jnp.where(batch_mask(rows, forks, batches, rank), spread, 0.0)
        high = spread.astype(BF16)
        low = (spread - high.astype(F32)).astype(BF16)
        up = selected[...].reshape(batches * rank, width)
        tile = 512
        for c in range(width // tile):
            at = slice(c * tile, (c + 1) * tile)
            out = jnp.dot(high, up[:, at], preferred_element_type=F32)
            out = out + jnp.dot(low, up[:, at], preferred_element_type=F32)
            out = out + base_ref[:, at]
            for r in received_refs:
                out = out + r[:, at].astype(F32)
            o_ref[:, at] = out.astype(BF16)

    return pl.pallas_call(
        kernel,
        out_shape=jax.ShapeDtypeStruct((rows, width), BF16),
        in_specs=[SMEM, SMEM] + [VMEM] * (1 + n_received + n_ranks + replicas),
        out_specs=VMEM,
        scratch_shapes=[pltpu.VMEM((batches, rank, width), BF16)],
        compiler_params=PARAMS,
        name="finish",
    )(own_rows, place, base, *received, *ranks, *tables)


def lookup(wanted, adapter_table_row):
    matches = wanted[..., None] == jnp.arange(adapter_table_row.shape[0], dtype=jnp.int32)
    return jnp.sum(jnp.where(matches, adapter_table_row, 0), axis=-1)


def body(
    replicas,
    chips,
    queries,
    recent_keys,
    recent_values,
    prefix_key_value,
    prefix_length_each,
    batch_adapter_index,
    adapter_table_row,
    down_weight_table,
    up_weight_table,
    output_weight,
):
    forks, steps, _ = queries.shape
    batches = batch_adapter_index.shape[0]
    capacity = max(2, 2 * batches // replicas)
    model_width = output_weight.shape[1]
    width = model_width // (2 * chips)
    replica = lax.axis_index("replica").astype(jnp.int32)
    tensor = lax.axis_index("tensor").astype(jnp.int32)
    chip, core = tensor // 2, lax.rem(tensor, 2)
    place = replica.reshape(1)

    own_rows = lookup(batch_adapter_index, adapter_table_row)
    rows_all = lax.all_gather(own_rows, "replica")
    down_parts, up_parts = pack(down_weight_table, up_weight_table, rows_all, place, capacity)

    def shift(d):
        return [(z, (z + d) % replicas) for z in range(replicas)]

    downs = [lax.ppermute(down_parts[d - 1], "replica", shift(d)) for d in range(1, replicas)]
    ups = [lax.ppermute(up_parts[d - 1], "replica", shift(d)) for d in range(1, replicas)]

    lens = jnp.concatenate([prefix_length_each] * steps)[:, None]
    attended = attention(
        queries.transpose(1, 0, 2),
        recent_keys.transpose(1, 0, 2),
        recent_values.transpose(1, 0, 2),
        prefix_key_value,
        lens,
    )

    swap = [(t, t ^ 1) for t in range(2 * chips)]

    def along(e):
        return [(t, (t + 2 * e) % (2 * chips)) for t in range(2 * chips)]

    order = list(range(1, chips)) + [0]
    groups = [lax.rem(chip + e, chips) * 2 for e in order]
    halves = [
        lax.ppermute(project(attended, output_weight, g + 1 - core, width, None, BF16), "tensor", swap)
        for g in groups
    ]
    received = []
    for e, g, half in zip(order, groups, halves):
        if e:
            part = project(attended, output_weight, g + core, width, half, BF16)
            received.append(lax.ppermute(part, "tensor", along(e)))
        else:
            base = project(attended, output_weight, g + core, width, half, F32)

    rank_part = low_rank(attended, forks, own_rows, place, [down_weight_table] + downs)
    rank_chip = rank_part + lax.ppermute(rank_part, "tensor", swap)
    ranks = [rank_chip] + [lax.ppermute(rank_chip, "tensor", along(e)) for e in range(1, chips)]
    out = finish(base, received, ranks, forks, own_rows, place, [up_weight_table] + ups)
    return out.reshape(steps, forks, width).transpose(1, 0, 2)


def solution(mesh):
    placed = (
        P(("groups", "replica"), None, "tensor"),
        P(("groups", "replica"), None, "tensor"),
        P(("groups", "replica"), None, "tensor"),
        P(("groups", "replica"), None, None, "tensor"),
        P(("groups", "replica")),
        P(("groups", "replica")),
        P("groups"),
        P("replica", None, "tensor"),
        P("replica", None, "tensor"),
        P("tensor", None),
    )
    return jax.shard_map(
        functools.partial(body, mesh.shape["replica"], mesh.shape["tensor"] // 2),
        mesh=mesh,
        in_specs=placed,
        out_specs=P(("groups", "replica"), None, "tensor"),
        check_vma=False,
    )
```

```python
import functools
import math

import jax
import jax.numpy as jnp
from jax import lax
from jax.experimental import pallas as pl
from jax.experimental.pallas import tpu as pltpu
from jax.sharding import PartitionSpec as P

HD = 128
NEG = -1e30
LOG2_SCALE = math.log2(math.e) / math.sqrt(HD)
BF16, F32 = jnp.bfloat16, jnp.float32
VMEM = pl.BlockSpec(memory_space=pltpu.VMEM)
SMEM = pl.BlockSpec(memory_space=pltpu.SMEM)
PARAMS = pltpu.CompilerParams(vmem_limit_bytes=58 * 1024 * 1024)


def attention_kernel(
    unit_heads, key_block, q_ref, rk_ref, rv_ref, kv_ref, lens_ref, o_ref,
    s_a, s_b, vaug, mx_a, mx_b, mb, acc, lensb, qs,
):
    steps, forks, width = q_ref.shape
    heads = width // HD
    heads_kv = rk_ref.shape[2] // HD
    group = heads // heads_kv
    head_rows = steps * forks
    rows = unit_heads * head_rows
    units = heads // unit_heads
    prefix = kv_ref.shape[2]
    longest = jnp.max(lens_ref[...])
    blocks = (longest + (key_block - 1)) // key_block
    lens = jnp.broadcast_to(lens_ref[...], (head_rows, HD))
    for i in range(unit_heads):
        lensb[i * head_rows : (i + 1) * head_rows, :] = lens
    for v in range(heads_kv):
        vaug[v, :, 0:HD] = kv_ref[0, 1, :, v * HD : (v + 1) * HD]
        vaug[v, :, HD : 2 * HD] = jnp.ones((prefix, HD), BF16)
    for h in range(heads):
        qs[h * head_rows : (h + 1) * head_rows, :] = q_ref[:, :, h * HD : (h + 1) * HD].reshape(head_rows, HD)
    score_refs, max_refs = (s_a, s_b), (mx_a, mx_b)

    def own_scores(u, t):
        parts = []
        for i in range(unit_heads):
            h = u * unit_heads + i
            v = h // group
            k = rk_ref[t, :, v * HD : (v + 1) * HD].astype(F32)
            for s in range(steps):
                if t <= s:
                    at = h * head_rows + s * forks
                    parts.append(jnp.sum(qs[at : at + forks, :].astype(F32) * k, axis=1, keepdims=True))
                else:
                    parts.append(jnp.full((forks, 1), NEG, F32))
        return jnp.concatenate(parts, axis=0)

    def score_block(u, j, s_ref, mx_ref):
        v = (u * unit_heads) // group
        keys = kv_ref[0, 0, pl.ds(pl.multiple_of(j * key_block, key_block), key_block), v * HD : (v + 1) * HD]
        s = lax.dot_general(
            qs[u * rows : (u + 1) * rows, :], keys, (((1,), (1,)), ((), ())), preferred_element_type=F32
        )
        top = mx_ref[...]
        left = lensb[...] - j * key_block
        lane = lax.broadcasted_iota(jnp.int32, (rows, HD), 1)
        for c in range(key_block // HD):
            part = jnp.where(lane + c * HD < left, s[:, c * HD : (c + 1) * HD], NEG)
            top = jnp.maximum(top, part)
            s_ref[j, :, c * HD : (c + 1) * HD] = part
        mx_ref[...] = top

    def value_block(u, j, s_ref):
        v = (u * unit_heads) // group
        top = mb[...]
        parts = [
            jnp.exp2((s_ref[j, :, c * HD : (c + 1) * HD] - top) * LOG2_SCALE).astype(BF16)
            for c in range(key_block // HD)
        ]
        values = vaug[v, pl.ds(pl.multiple_of(j * key_block, key_block), key_block), :]
        acc[...] += jnp.dot(jnp.concatenate(parts, axis=1), values, preferred_element_type=F32)

    for u in range(units + 1):
        done = u - 1
        if u < units:
            max_refs[u % 2][...] = jnp.full((rows, HD), NEG, F32)
        if u > 0:
            own = [own_scores(done, t) for t in range(steps)]
            top = jnp.max(max_refs[done % 2][...], axis=1, keepdims=True)
            for o in own:
                top = jnp.maximum(top, o)
            mb[...] = jnp.broadcast_to(top, (rows, HD))
            acc[...] = jnp.zeros_like(acc)

        @pl.loop(0, blocks)
        def _(j):
            if u < units:
                score_block(u, j, score_refs[u % 2], max_refs[u % 2])
            if u > 0:
                value_block(done, j, score_refs[done % 2])

        if u > 0:
            weights = [jnp.exp2((o - top) * LOG2_SCALE) for o in own]
            total = acc[:, HD : 2 * HD]
            for w in weights:
                total = total + w
            for i in range(unit_heads):
                h = done * unit_heads + i
                v = h // group
                at = slice(i * head_rows, (i + 1) * head_rows)
                mixed = acc[at, 0:HD]
                for t in range(steps):
                    value = rv_ref[t, :, v * HD : (v + 1) * HD].astype(F32)
                    value = jnp.concatenate([value] * steps, axis=0)
                    mixed = mixed + weights[t][at].astype(BF16).astype(F32) * value
                o_ref[:, h * HD : (h + 1) * HD] = (mixed / total[at]).astype(BF16)


def attention(q, rk, rv, kv, lens):
    steps, forks, width = q.shape
    prefix = kv.shape[2]
    heads_kv = rk.shape[2] // HD
    unit_heads = 2
    key_block = prefix
    rows = unit_heads * steps * forks
    return pl.pallas_call(
        functools.partial(attention_kernel, unit_heads, key_block),
        out_shape=jax.ShapeDtypeStruct((steps * forks, width), BF16),
        in_specs=[VMEM] * 5,
        out_specs=VMEM,
        scratch_shapes=[pltpu.VMEM((prefix // key_block, rows, key_block), F32)] * 2
        + [pltpu.VMEM((heads_kv, prefix, 2 * HD), BF16)]
        + [pltpu.VMEM((rows, HD), F32)] * 3
        + [
            pltpu.VMEM((rows, 2 * HD), F32),
            pltpu.VMEM((rows, HD), jnp.int32),
            pltpu.VMEM((width // HD * steps * forks, HD), BF16),
        ],
        compiler_params=PARAMS,
        cost_estimate=pl.CostEstimate(flops=2 * 10**10, bytes_accessed=6 * 2**20, transcendentals=0),
        name="attention",
    )(q, rk, rv, kv, lens)


def project(attended, weight, column_group, width, add, dtype):
    rows, depth = attended.shape
    tile = 1024 if width % 1024 == 0 else width
    tiles = width // tile

    def kernel(group_ref, a_ref, w_ref, *rest):
        o_ref = rest[-1]
        part = jnp.dot(a_ref[...], w_ref[...], preferred_element_type=F32)
        if len(rest) == 2:
            part = part + rest[0][...].astype(F32)
        o_ref[...] = part.astype(o_ref.dtype)

    in_specs = [
        pl.BlockSpec((rows, depth), lambda i, g: (0, 0)),
        pl.BlockSpec((depth, tile), lambda i, g: (0, g[0] * tiles + i)),
    ]
    operands = [attended, weight]
    if add is not None:
        in_specs.append(pl.BlockSpec((rows, tile), lambda i, g: (0, i)))
        operands.append(add)
    return pl.pallas_call(
        kernel,
        out_shape=jax.ShapeDtypeStruct((rows, width), dtype),
        grid_spec=pltpu.PrefetchScalarGridSpec(
            num_scalar_prefetch=1,
            grid=(tiles,),
            in_specs=in_specs,
            out_specs=pl.BlockSpec((rows, tile), lambda i, g: (0, i)),
        ),
        compiler_params=PARAMS,
        cost_estimate=pl.CostEstimate(
            flops=2 * rows * depth * width, bytes_accessed=2 * depth * width, transcendentals=0
        ),
        name="project",
    )(column_group.reshape(1), *operands)


def pack(down, up, rows_all, place, capacity):
    replicas, batches = rows_all.shape
    stored, rank, up_width = up.shape
    width = up_width + down.shape[2]

    def kernel(rows_ref, place_ref, down_ref, up_ref, *outs):
        me = place_ref[0]
        for d in range(1, replicas):
            to = lax.rem(me + d, replicas)
            out = outs[d - 1]

            def step(b, count):
                row = rows_ref[to, b] - me * stored
                mine = (row >= 0) & (row < stored)

                @pl.when(mine)
                def _():
                    out[count, :, 0:up_width] = up_ref[row]
                    out[count, :, up_width:width] = down_ref[row]

                return count + mine.astype(jnp.int32)

            lax.fori_loop(0, batches, step, jnp.int32(0))

    return pl.pallas_call(
        kernel,
        out_shape=[jax.ShapeDtypeStruct((capacity, rank, width), BF16)] * (replicas - 1),
        in_specs=[SMEM, SMEM, VMEM, VMEM],
        out_specs=[VMEM] * (replicas - 1),
        compiler_params=PARAMS,
        name="pack",
    )(rows_all, place, down, up)


def collect(rows_ref, place_ref, replicas, table_refs, selected):
    stored = table_refs[0].shape[0]
    batches = selected.shape[0]
    me = place_ref[0]
    for d in range(replicas):
        owner = lax.rem(me + (replicas - d), replicas)
        source = table_refs[d]

        def step(b, count):
            row = rows_ref[b] - owner * stored
            there = (row >= 0) & (row < stored)

            @pl.when(there)
            def _():
                selected[b] = source[row if d == 0 else count]

            return count + there.astype(jnp.int32)

        lax.fori_loop(0, batches, step, jnp.int32(0))


def whole(shape):
    return pl.BlockSpec(shape, lambda i: (0,) * len(shape))


def columns(packed, width, block):
    shape = packed.shape[:-1] + (width,)
    return pl.BlockSpec(shape, lambda i: (0,) * (len(shape) - 1) + (block,))


def batch_mask(rows, forks, batches, rank):
    batch_forks = forks // batches
    row = lax.broadcasted_iota(jnp.int32, (rows, batches * rank), 0)
    column = lax.broadcasted_iota(jnp.int32, (rows, batches * rank), 1)
    return lax.rem(row, forks) // batch_forks == column // rank


def low_rank(attended, forks, own_rows, place, tables):
    replicas = len(tables)
    rows, depth = attended.shape
    batches = own_rows.shape[0]
    rank = tables[0].shape[1]

    def kernel(rows_ref, place_ref, a_ref, *rest):
        o_ref, selected = rest[-2], rest[-1]
        collect(rows_ref, place_ref, replicas, rest[:replicas], selected)
        every = lax.dot_general(
            a_ref[...],
            selected[...].reshape(batches * rank, depth),
            (((1,), (1,)), ((), ())),
            preferred_element_type=F32,
        )
        every = jnp.where(batch_mask(rows, forks, batches, rank), every, 0.0)
        total = every[:, 0:HD]
        for c in range(1, batches * rank // HD):
            total = total + every[:, c * HD : (c + 1) * HD]
        o_ref[...] = total

    return pl.pallas_call(
        kernel,
        out_shape=jax.ShapeDtypeStruct((rows, HD), F32),
        grid=(1,),
        in_specs=[SMEM, SMEM, whole(attended.shape), whole(tables[0].shape)]
        + [columns(t, depth, (t.shape[2] - depth) // depth) for t in tables[1:]],
        out_specs=whole((rows, HD)),
        scratch_shapes=[pltpu.VMEM((batches, rank, depth), BF16)],
        compiler_params=PARAMS,
        name="low_rank",
    )(own_rows, place, attended, *tables)


def finish(base, received, ranks, forks, own_rows, place, tables):
    replicas = len(tables)
    rows, width = base.shape
    batches = own_rows.shape[0]
    rank = tables[0].shape[1]
    n_received, n_ranks = len(received), len(ranks)
    steps = rows // forks

    def kernel(rows_ref, place_ref, base_ref, *rest):
        received_refs = rest[:n_received]
        rank_refs = rest[n_received : n_received + n_ranks]
        table_refs = rest[n_received + n_ranks : -2]
        o_ref, selected = rest[-2], rest[-1]
        collect(rows_ref, place_ref, replicas, table_refs, selected)
        total = rank_refs[0][...]
        for r in rank_refs[1:]:
            total = total + r[...]
        spread = jnp.concatenate([total] * (batches * rank // HD), axis=1)
        spread = jnp.where(batch_mask(rows, forks, batches, rank), spread, 0.0)
        high = spread.astype(BF16)
        low = (spread - high.astype(F32)).astype(BF16)
        up = selected[...].reshape(batches * rank, width)
        tile = 512
        for c in range(width // tile):
            at = slice(c * tile, (c + 1) * tile)
            out = jnp.dot(high, up[:, at], preferred_element_type=F32)
            out = out + jnp.dot(low, up[:, at], preferred_element_type=F32)
            out = out + base_ref[:, at]
            for r in received_refs:
                out = out + r[:, at].astype(F32)
            o_ref[:, at] = out.astype(BF16)

    return pl.pallas_call(
        kernel,
        out_shape=jax.ShapeDtypeStruct((rows, width), BF16),
        grid=(1,),
        in_specs=[SMEM, SMEM]
        + [whole(x.shape) for x in (base, *received, *ranks, tables[0])]
        + [columns(t, width, 0) for t in tables[1:]],
        out_specs=whole((rows, width)),
        scratch_shapes=[pltpu.VMEM((batches, rank, width), BF16)],
        compiler_params=PARAMS,
        name="finish",
    )(own_rows, place, base, *received, *ranks, *tables)


def lookup(wanted, adapter_table_row):
    matches = wanted[..., None] == jnp.arange(adapter_table_row.shape[0], dtype=jnp.int32)
    return jnp.sum(jnp.where(matches, adapter_table_row, 0), axis=-1)


def body(
    replicas,
    chips,
    queries,
    recent_keys,
    recent_values,
    prefix_key_value,
    prefix_length_each,
    batch_adapter_index,
    adapter_table_row,
    down_weight_table,
    up_weight_table,
    output_weight,
):
    forks, steps, _ = queries.shape
    batches = batch_adapter_index.shape[0]
    capacity = max(2, 2 * batches // replicas)
    model_width = output_weight.shape[1]
    width = model_width // (2 * chips)
    replica = lax.axis_index("replica").astype(jnp.int32)
    tensor = lax.axis_index("tensor").astype(jnp.int32)
    chip, core = tensor // 2, lax.rem(tensor, 2)
    place = replica.reshape(1)

    own_rows = lookup(batch_adapter_index, adapter_table_row)
    rows_all = lax.all_gather(own_rows, "replica")
    parts = pack(down_weight_table, up_weight_table, rows_all, place, capacity)
    queries = lax.optimization_barrier((queries, *parts))[0]
    arrived = [
        lax.ppermute(parts[d - 1], "replica", [(z, (z + d) % replicas) for z in range(replicas)])
        for d in range(1, replicas)
    ]

    lens = jnp.concatenate([prefix_length_each] * steps)[:, None]
    attended = attention(
        queries.transpose(1, 0, 2),
        recent_keys.transpose(1, 0, 2),
        recent_values.transpose(1, 0, 2),
        prefix_key_value,
        lens,
    )

    swap = [(t, t ^ 1) for t in range(2 * chips)]

    def along(e):
        return [(t, (t + 2 * e) % (2 * chips)) for t in range(2 * chips)]

    order = list(range(1, chips)) + [0]
    groups = [lax.rem(chip + e, chips) * 2 for e in order]
    halves = [
        lax.ppermute(project(attended, output_weight, g + 1 - core, width, None, BF16), "tensor", swap)
        for g in groups
    ]
    received = []
    for e, g, half in zip(order, groups, halves):
        if e:
            part = project(attended, output_weight, g + core, width, half, BF16)
            received.append(lax.ppermute(part, "tensor", along(e)))
        else:
            base = project(attended, output_weight, g + core, width, half, F32)

    rank_part = low_rank(attended, forks, own_rows, place, [down_weight_table] + arrived)
    rank_chip = rank_part + lax.ppermute(rank_part, "tensor", swap)
    ranks = [rank_chip] + [lax.ppermute(rank_chip, "tensor", along(e)) for e in range(1, chips)]
    out = finish(base, received, ranks, forks, own_rows, place, [up_weight_table] + arrived)
    return out.reshape(steps, forks, width).transpose(1, 0, 2)


def solution(mesh):
    placed = (
        P(("groups", "replica"), None, "tensor"),
        P(("groups", "replica"), None, "tensor"),
        P(("groups", "replica"), None, "tensor"),
        P(("groups", "replica"), None, None, "tensor"),
        P(("groups", "replica")),
        P(("groups", "replica")),
        P("groups"),
        P("replica", None, "tensor"),
        P("replica", None, "tensor"),
        P("tensor", None),
    )
    return jax.shard_map(
        functools.partial(body, mesh.shape["replica"], mesh.shape["tensor"] // 2),
        mesh=mesh,
        in_specs=placed,
        out_specs=P(("groups", "replica"), None, "tensor"),
        check_vma=False,
    )
```

```python
import functools
import math

import jax
import jax.numpy as jnp
from jax import lax
from jax.experimental import pallas as pl
from jax.experimental.pallas import tpu as pltpu
from jax.sharding import PartitionSpec as P

HD = 128
NEG = -1e30
LOG2_SCALE = math.log2(math.e) / math.sqrt(HD)
BF16, F32 = jnp.bfloat16, jnp.float32
VMEM = pl.BlockSpec(memory_space=pltpu.VMEM)
SMEM = pl.BlockSpec(memory_space=pltpu.SMEM)
PARAMS = pltpu.CompilerParams(vmem_limit_bytes=58 * 1024 * 1024)


def attention_kernel(
    unit_heads, key_block, q_ref, rk_ref, rv_ref, kv_ref, lens_ref, o_ref,
    s_a, s_b, vaug, mx_a, mx_b, mb, acc, lensb, qs,
):
    steps, forks, width = q_ref.shape
    heads = width // HD
    heads_kv = rk_ref.shape[2] // HD
    group = heads // heads_kv
    head_rows = steps * forks
    rows = unit_heads * head_rows
    units = heads // unit_heads
    prefix = kv_ref.shape[2]
    longest = jnp.max(lens_ref[...])
    blocks = (longest + (key_block - 1)) // key_block
    lens = jnp.broadcast_to(lens_ref[...], (head_rows, HD))
    for i in range(unit_heads):
        lensb[i * head_rows : (i + 1) * head_rows, :] = lens
    for v in range(heads_kv):
        vaug[v, :, 0:HD] = kv_ref[0, 1, :, v * HD : (v + 1) * HD]
        vaug[v, :, HD : 2 * HD] = jnp.ones((prefix, HD), BF16)
    for h in range(heads):
        qs[h * head_rows : (h + 1) * head_rows, :] = q_ref[:, :, h * HD : (h + 1) * HD].reshape(head_rows, HD)
    score_refs, max_refs = (s_a, s_b), (mx_a, mx_b)

    def own_scores(u, t):
        parts = []
        for i in range(unit_heads):
            h = u * unit_heads + i
            v = h // group
            k = rk_ref[t, :, v * HD : (v + 1) * HD].astype(F32)
            for s in range(steps):
                if t <= s:
                    at = h * head_rows + s * forks
                    parts.append(jnp.sum(qs[at : at + forks, :].astype(F32) * k, axis=1, keepdims=True))
                else:
                    parts.append(jnp.full((forks, 1), NEG, F32))
        return jnp.concatenate(parts, axis=0)

    def score_block(u, j, s_ref, mx_ref):
        v = (u * unit_heads) // group
        keys = kv_ref[0, 0, pl.ds(pl.multiple_of(j * key_block, key_block), key_block), v * HD : (v + 1) * HD]
        s = lax.dot_general(
            qs[u * rows : (u + 1) * rows, :], keys, (((1,), (1,)), ((), ())), preferred_element_type=F32
        )
        top = mx_ref[...]
        left = lensb[...] - j * key_block
        lane = lax.broadcasted_iota(jnp.int32, (rows, HD), 1)
        for c in range(key_block // HD):
            part = jnp.where(lane + c * HD < left, s[:, c * HD : (c + 1) * HD], NEG)
            top = jnp.maximum(top, part)
            s_ref[j, :, c * HD : (c + 1) * HD] = part
        mx_ref[...] = top

    def value_block(u, j, s_ref):
        v = (u * unit_heads) // group
        top = mb[...]
        parts = [
            jnp.exp2((s_ref[j, :, c * HD : (c + 1) * HD] - top) * LOG2_SCALE).astype(BF16)
            for c in range(key_block // HD)
        ]
        values = vaug[v, pl.ds(pl.multiple_of(j * key_block, key_block), key_block), :]
        acc[...] += jnp.dot(jnp.concatenate(parts, axis=1), values, preferred_element_type=F32)

    for u in range(units + 1):
        done = u - 1
        if u < units:
            max_refs[u % 2][...] = jnp.full((rows, HD), NEG, F32)
        if u > 0:
            own = [own_scores(done, t) for t in range(steps)]
            top = jnp.max(max_refs[done % 2][...], axis=1, keepdims=True)
            for o in own:
                top = jnp.maximum(top, o)
            mb[...] = jnp.broadcast_to(top, (rows, HD))
            acc[...] = jnp.zeros_like(acc)

        @pl.loop(0, blocks)
        def _(j):
            if u < units:
                score_block(u, j, score_refs[u % 2], max_refs[u % 2])
            if u > 0:
                value_block(done, j, score_refs[done % 2])

        if u > 0:
            weights = [jnp.exp2((o - top) * LOG2_SCALE) for o in own]
            total = acc[:, HD : 2 * HD]
            for w in weights:
                total = total + w
            for i in range(unit_heads):
                h = done * unit_heads + i
                v = h // group
                at = slice(i * head_rows, (i + 1) * head_rows)
                mixed = acc[at, 0:HD]
                for t in range(steps):
                    value = rv_ref[t, :, v * HD : (v + 1) * HD].astype(F32)
                    value = jnp.concatenate([value] * steps, axis=0)
                    mixed = mixed + weights[t][at].astype(BF16).astype(F32) * value
                o_ref[:, h * HD : (h + 1) * HD] = (mixed / total[at]).astype(BF16)


def attention(q, rk, rv, kv, lens):
    steps, forks, width = q.shape
    prefix = kv.shape[2]
    heads_kv = rk.shape[2] // HD
    unit_heads = 2
    key_block = prefix
    rows = unit_heads * steps * forks
    return pl.pallas_call(
        functools.partial(attention_kernel, unit_heads, key_block),
        out_shape=jax.ShapeDtypeStruct((steps * forks, width), BF16),
        in_specs=[VMEM] * 5,
        out_specs=VMEM,
        scratch_shapes=[pltpu.VMEM((prefix // key_block, rows, key_block), F32)] * 2
        + [pltpu.VMEM((heads_kv, prefix, 2 * HD), BF16)]
        + [pltpu.VMEM((rows, HD), F32)] * 3
        + [
            pltpu.VMEM((rows, 2 * HD), F32),
            pltpu.VMEM((rows, HD), jnp.int32),
            pltpu.VMEM((width // HD * steps * forks, HD), BF16),
        ],
        compiler_params=PARAMS,
        cost_estimate=pl.CostEstimate(flops=2 * 10**10, bytes_accessed=6 * 2**20, transcendentals=0),
        name="attention",
    )(q, rk, rv, kv, lens)


def project(attended, weight, column_group, width, add, dtype):
    rows, depth = attended.shape
    tile = 1024 if width % 1024 == 0 else width
    tiles = width // tile

    def kernel(group_ref, a_ref, w_ref, *rest):
        o_ref = rest[-1]
        part = jnp.dot(a_ref[...], w_ref[...], preferred_element_type=F32)
        if len(rest) == 2:
            part = part + rest[0][...].astype(F32)
        o_ref[...] = part.astype(o_ref.dtype)

    in_specs = [
        pl.BlockSpec((rows, depth), lambda i, g: (0, 0)),
        pl.BlockSpec((depth, tile), lambda i, g: (0, g[0] * tiles + i)),
    ]
    operands = [attended, weight]
    if add is not None:
        in_specs.append(pl.BlockSpec((rows, tile), lambda i, g: (0, i)))
        operands.append(add)
    return pl.pallas_call(
        kernel,
        out_shape=jax.ShapeDtypeStruct((rows, width), dtype),
        grid_spec=pltpu.PrefetchScalarGridSpec(
            num_scalar_prefetch=1,
            grid=(tiles,),
            in_specs=in_specs,
            out_specs=pl.BlockSpec((rows, tile), lambda i, g: (0, i)),
        ),
        compiler_params=PARAMS,
        cost_estimate=pl.CostEstimate(
            flops=2 * rows * depth * width, bytes_accessed=2 * depth * width, transcendentals=0
        ),
        name="project",
    )(column_group.reshape(1), *operands)


def pack(down, up, rows_all, place, capacity):
    replicas, batches = rows_all.shape
    stored, rank, up_width = up.shape
    width = up_width + down.shape[2]

    def kernel(rows_ref, place_ref, down_ref, up_ref, out):
        me = place_ref[0]
        for to in range(replicas):

            def step(b, count):
                row = rows_ref[to, b] - me * stored
                mine = (row >= 0) & (row < stored)

                @pl.when(mine)
                def _():
                    out[to, count, :, 0:up_width] = up_ref[row]
                    out[to, count, :, up_width:width] = down_ref[row]

                return count + mine.astype(jnp.int32)

            lax.fori_loop(0, batches, step, jnp.int32(0))

    return pl.pallas_call(
        kernel,
        out_shape=jax.ShapeDtypeStruct((replicas, capacity, rank, width), BF16),
        in_specs=[SMEM, SMEM, VMEM, VMEM],
        out_specs=VMEM,
        compiler_params=PARAMS,
        name="pack",
    )(rows_all, place, down, up)


def collect(rows_ref, stored, arrived_ref, selected):
    batches = selected.shape[0]
    for owner in range(arrived_ref.shape[0]):

        def step(b, count):
            row = rows_ref[b] - owner * stored
            there = (row >= 0) & (row < stored)

            @pl.when(there)
            def _():
                selected[b] = arrived_ref[owner, count]

            return count + there.astype(jnp.int32)

        lax.fori_loop(0, batches, step, jnp.int32(0))


def whole(shape):
    return pl.BlockSpec(shape, lambda i: (0,) * len(shape))


def columns(packed, width, block):
    shape = packed.shape[:-1] + (width,)
    return pl.BlockSpec(shape, lambda i: (0,) * (len(shape) - 1) + (block,))


def batch_mask(rows, forks, batches, rank):
    batch_forks = forks // batches
    row = lax.broadcasted_iota(jnp.int32, (rows, batches * rank), 0)
    column = lax.broadcasted_iota(jnp.int32, (rows, batches * rank), 1)
    return lax.rem(row, forks) // batch_forks == column // rank


def low_rank(attended, forks, own_rows, stored, arrived):
    rows, depth = attended.shape
    batches = own_rows.shape[0]
    rank = arrived.shape[2]

    def kernel(rows_ref, a_ref, arrived_ref, o_ref, selected):
        collect(rows_ref, stored, arrived_ref, selected)
        every = lax.dot_general(
            a_ref[...],
            selected[...].reshape(batches * rank, depth),
            (((1,), (1,)), ((), ())),
            preferred_element_type=F32,
        )
        every = jnp.where(batch_mask(rows, forks, batches, rank), every, 0.0)
        total = every[:, 0:HD]
        for c in range(1, batches * rank // HD):
            total = total + every[:, c * HD : (c + 1) * HD]
        o_ref[...] = total

    return pl.pallas_call(
        kernel,
        out_shape=jax.ShapeDtypeStruct((rows, HD), F32),
        grid=(1,),
        in_specs=[SMEM, whole(attended.shape), columns(arrived, depth, (arrived.shape[3] - depth) // depth)],
        out_specs=whole((rows, HD)),
        scratch_shapes=[pltpu.VMEM((batches, rank, depth), BF16)],
        compiler_params=PARAMS,
        name="low_rank",
    )(own_rows, attended, arrived)


def finish(base, received, ranks, forks, own_rows, stored, arrived):
    rows, width = base.shape
    batches = own_rows.shape[0]
    rank = arrived.shape[2]
    n_received = len(received)
    tile = min(width, 1024)

    def kernel(rows_ref, base_ref, *rest):
        received_refs, rank_refs = rest[:n_received], rest[n_received:-3]
        arrived_ref, o_ref, selected = rest[-3:]
        collect(rows_ref, stored, arrived_ref, selected)
        total = rank_refs[0][...]
        for r in rank_refs[1:]:
            total = total + r[...]
        spread = jnp.concatenate([total] * (batches * rank // HD), axis=1)
        spread = jnp.where(batch_mask(rows, forks, batches, rank), spread, 0.0)
        high = spread.astype(BF16)
        low = (spread - high.astype(F32)).astype(BF16)
        up = selected[...].reshape(batches * rank, tile)
        out = jnp.dot(high, up, preferred_element_type=F32)
        out = out + jnp.dot(low, up, preferred_element_type=F32)
        out = out + base_ref[...]
        for r in received_refs:
            out = out + r[...].astype(F32)
        o_ref[...] = out.astype(BF16)

    by_tile = pl.BlockSpec((rows, tile), lambda i: (0, i))
    return pl.pallas_call(
        kernel,
        out_shape=jax.ShapeDtypeStruct((rows, width), BF16),
        grid=(width // tile,),
        in_specs=[SMEM, by_tile]
        + [by_tile] * n_received
        + [whole(r.shape) for r in ranks]
        + [pl.BlockSpec(arrived.shape[:3] + (tile,), lambda i: (0, 0, 0, i))],
        out_specs=by_tile,
        scratch_shapes=[pltpu.VMEM((batches, rank, tile), BF16)],
        compiler_params=PARAMS,
        name="finish",
    )(own_rows, base, *received, *ranks, arrived)


def lookup(wanted, adapter_table_row):
    matches = wanted[..., None] == jnp.arange(adapter_table_row.shape[0], dtype=jnp.int32)
    return jnp.sum(jnp.where(matches, adapter_table_row, 0), axis=-1)


def body(
    replicas,
    chips,
    queries,
    recent_keys,
    recent_values,
    prefix_key_value,
    prefix_length_each,
    batch_adapter_index,
    adapter_table_row,
    down_weight_table,
    up_weight_table,
    output_weight,
):
    forks, steps, _ = queries.shape
    batches = batch_adapter_index.shape[0]
    capacity = max(2, 2 * batches // replicas)
    model_width = output_weight.shape[1]
    width = model_width // (2 * chips)
    replica = lax.axis_index("replica").astype(jnp.int32)
    tensor = lax.axis_index("tensor").astype(jnp.int32)
    chip, core = tensor // 2, lax.rem(tensor, 2)
    place = replica.reshape(1)

    own_rows = lookup(batch_adapter_index, adapter_table_row)
    rows_all = lax.all_gather(own_rows, "replica")
    parts = pack(down_weight_table, up_weight_table, rows_all, place, capacity)
    queries = lax.optimization_barrier((queries, parts))[0]
    arrived = lax.all_to_all(parts, "replica", 0, 0)

    lens = jnp.concatenate([prefix_length_each] * steps)[:, None]
    attended = attention(
        queries.transpose(1, 0, 2),
        recent_keys.transpose(1, 0, 2),
        recent_values.transpose(1, 0, 2),
        prefix_key_value,
        lens,
    )

    swap = [(t, t ^ 1) for t in range(2 * chips)]

    def along(e):
        return [(t, (t + 2 * e) % (2 * chips)) for t in range(2 * chips)]

    order = list(range(1, chips)) + [0]
    groups = [lax.rem(chip + e, chips) * 2 for e in order]
    halves = [
        lax.ppermute(project(attended, output_weight, g + 1 - core, width, None, BF16), "tensor", swap)
        for g in groups
    ]
    received = []
    for e, g, half in zip(order, groups, halves):
        if e:
            part = project(attended, output_weight, g + core, width, half, BF16)
            received.append(lax.ppermute(part, "tensor", along(e)))
        else:
            base = project(attended, output_weight, g + core, width, half, F32)

    rank_part = low_rank(attended, forks, own_rows, down_weight_table.shape[0], arrived)
    rank_chip = rank_part + lax.ppermute(rank_part, "tensor", swap)
    ranks = [rank_chip] + [lax.ppermute(rank_chip, "tensor", along(e)) for e in range(1, chips)]
    out = finish(base, received, ranks, forks, own_rows, up_weight_table.shape[0], arrived)
    return out.reshape(steps, forks, width).transpose(1, 0, 2)


def solution(mesh):
    placed = (
        P(("groups", "replica"), None, "tensor"),
        P(("groups", "replica"), None, "tensor"),
        P(("groups", "replica"), None, "tensor"),
        P(("groups", "replica"), None, None, "tensor"),
        P(("groups", "replica")),
        P(("groups", "replica")),
        P("groups"),
        P("replica", None, "tensor"),
        P("replica", None, "tensor"),
        P("tensor", None),
    )
    return jax.shard_map(
        functools.partial(body, mesh.shape["replica"], mesh.shape["tensor"] // 2),
        mesh=mesh,
        in_specs=placed,
        out_specs=P(("groups", "replica"), None, "tensor"),
        check_vma=False,
    )
```

```python
import functools
import math

import jax
import jax.numpy as jnp
from jax import lax
from jax.experimental import pallas as pl
from jax.experimental.pallas import tpu as pltpu
from jax.sharding import PartitionSpec as P

HD = 128
NEG = -1e30
LOG2_SCALE = math.log2(math.e) / math.sqrt(HD)
BF16, F32 = jnp.bfloat16, jnp.float32
VMEM = pl.BlockSpec(memory_space=pltpu.VMEM)
SMEM = pl.BlockSpec(memory_space=pltpu.SMEM)
HBM = pl.BlockSpec(memory_space=pl.ANY)
SMALL_PARAMS = pltpu.CompilerParams(vmem_limit_bytes=20 * 1024 * 1024)
PARAMS = pltpu.CompilerParams(vmem_limit_bytes=58 * 1024 * 1024)


def attention_kernel(
    unit_heads, key_block, q_ref, rk_ref, rv_ref, kv_ref, lens_ref, o_ref,
    s_a, s_b, vaug, mx_a, mx_b, mb, acc, lensb, qs,
):
    steps, forks, width = q_ref.shape
    heads = width // HD
    heads_kv = rk_ref.shape[2] // HD
    group = heads // heads_kv
    head_rows = steps * forks
    rows = unit_heads * head_rows
    units = heads // unit_heads
    prefix = kv_ref.shape[2]
    longest = jnp.max(lens_ref[...])
    blocks = (longest + (key_block - 1)) // key_block
    lens = jnp.broadcast_to(lens_ref[...], (head_rows, HD))
    for i in range(unit_heads):
        lensb[i * head_rows : (i + 1) * head_rows, :] = lens
    for v in range(heads_kv):
        vaug[v, :, 0:HD] = kv_ref[0, 1, :, v * HD : (v + 1) * HD]
        vaug[v, :, HD : 2 * HD] = jnp.ones((prefix, HD), BF16)
    for h in range(heads):
        qs[h * head_rows : (h + 1) * head_rows, :] = q_ref[:, :, h * HD : (h + 1) * HD].reshape(head_rows, HD)
    score_refs, max_refs = (s_a, s_b), (mx_a, mx_b)

    def own_scores(u, t):
        parts = []
        for i in range(unit_heads):
            h = u * unit_heads + i
            v = h // group
            k = rk_ref[t, :, v * HD : (v + 1) * HD].astype(F32)
            for s in range(steps):
                if t <= s:
                    at = h * head_rows + s * forks
                    parts.append(jnp.sum(qs[at : at + forks, :].astype(F32) * k, axis=1, keepdims=True))
                else:
                    parts.append(jnp.full((forks, 1), NEG, F32))
        return jnp.concatenate(parts, axis=0)

    def score_block(u, j, s_ref, mx_ref):
        v = (u * unit_heads) // group
        keys = kv_ref[0, 0, pl.ds(pl.multiple_of(j * key_block, key_block), key_block), v * HD : (v + 1) * HD]
        s = lax.dot_general(
            qs[u * rows : (u + 1) * rows, :], keys, (((1,), (1,)), ((), ())), preferred_element_type=F32
        )
        top = mx_ref[...]
        left = lensb[...] - j * key_block
        lane = lax.broadcasted_iota(jnp.int32, (rows, HD), 1)
        for c in range(key_block // HD):
            part = jnp.where(lane + c * HD < left, s[:, c * HD : (c + 1) * HD], NEG)
            top = jnp.maximum(top, part)
            s_ref[j, :, c * HD : (c + 1) * HD] = part
        mx_ref[...] = top

    def value_block(u, j, s_ref):
        v = (u * unit_heads) // group
        top = mb[...]
        parts = [
            jnp.exp2((s_ref[j, :, c * HD : (c + 1) * HD] - top) * LOG2_SCALE).astype(BF16)
            for c in range(key_block // HD)
        ]
        values = vaug[v, pl.ds(pl.multiple_of(j * key_block, key_block), key_block), :]
        acc[...] += jnp.dot(jnp.concatenate(parts, axis=1), values, preferred_element_type=F32)

    for u in range(units + 1):
        done = u - 1
        if u < units:
            max_refs[u % 2][...] = jnp.full((rows, HD), NEG, F32)
        if u > 0:
            own = [own_scores(done, t) for t in range(steps)]
            top = jnp.max(max_refs[done % 2][...], axis=1, keepdims=True)
            for o in own:
                top = jnp.maximum(top, o)
            mb[...] = jnp.broadcast_to(top, (rows, HD))
            acc[...] = jnp.zeros_like(acc)

        @pl.loop(0, blocks)
        def _(j):
            if u < units:
                score_block(u, j, score_refs[u % 2], max_refs[u % 2])
            if u > 0:
                value_block(done, j, score_refs[done % 2])

        if u > 0:
            weights = [jnp.exp2((o - top) * LOG2_SCALE) for o in own]
            total = acc[:, HD : 2 * HD]
            for w in weights:
                total = total + w
            for i in range(unit_heads):
                h = done * unit_heads + i
                v = h // group
                at = slice(i * head_rows, (i + 1) * head_rows)
                mixed = acc[at, 0:HD]
                for t in range(steps):
                    value = rv_ref[t, :, v * HD : (v + 1) * HD].astype(F32)
                    value = jnp.concatenate([value] * steps, axis=0)
                    mixed = mixed + weights[t][at].astype(BF16).astype(F32) * value
                o_ref[:, h * HD : (h + 1) * HD] = (mixed / total[at]).astype(BF16)


def attention(q, rk, rv, kv, lens):
    steps, forks, width = q.shape
    prefix = kv.shape[2]
    heads_kv = rk.shape[2] // HD
    unit_heads = 2
    key_block = prefix
    rows = unit_heads * steps * forks
    return pl.pallas_call(
        functools.partial(attention_kernel, unit_heads, key_block),
        out_shape=jax.ShapeDtypeStruct((steps * forks, width), BF16),
        in_specs=[VMEM] * 5,
        out_specs=VMEM,
        scratch_shapes=[pltpu.VMEM((prefix // key_block, rows, key_block), F32)] * 2
        + [pltpu.VMEM((heads_kv, prefix, 2 * HD), BF16)]
        + [pltpu.VMEM((rows, HD), F32)] * 3
        + [
            pltpu.VMEM((rows, 2 * HD), F32),
            pltpu.VMEM((rows, HD), jnp.int32),
            pltpu.VMEM((width // HD * steps * forks, HD), BF16),
        ],
        compiler_params=PARAMS,
        cost_estimate=pl.CostEstimate(flops=2 * 10**10, bytes_accessed=6 * 2**20, transcendentals=0),
        name="attention",
    )(q, rk, rv, kv, lens)


def project(attended, weight, column_group, width, add, dtype):
    rows, depth = attended.shape
    tile = 1024 if width % 1024 == 0 else width
    tiles = width // tile

    def kernel(group_ref, a_ref, w_ref, *rest):
        o_ref = rest[-1]
        part = jnp.dot(a_ref[...], w_ref[...], preferred_element_type=F32)
        for r in rest[:-1]:
            part = part + r[...].astype(F32)
        o_ref[...] = part.astype(o_ref.dtype)

    in_specs = [
        pl.BlockSpec((rows, depth), lambda i, g: (0, 0)),
        pl.BlockSpec((depth, tile), lambda i, g: (0, g[0] * tiles + i)),
    ]
    operands = [attended, weight]
    in_specs += [pl.BlockSpec((rows, tile), lambda i, g: (0, i))] * len(add)
    operands += add
    return pl.pallas_call(
        kernel,
        out_shape=jax.ShapeDtypeStruct((rows, width), dtype),
        grid_spec=pltpu.PrefetchScalarGridSpec(
            num_scalar_prefetch=1,
            grid=(tiles,),
            in_specs=in_specs,
            out_specs=pl.BlockSpec((rows, tile), lambda i, g: (0, i)),
        ),
        compiler_params=PARAMS,
        cost_estimate=pl.CostEstimate(
            flops=2 * rows * depth * width, bytes_accessed=2 * depth * width, transcendentals=0
        ),
        name="project",
    )(column_group.reshape(1), *operands)


def pack(down, up, rows_all, place, capacity):
    replicas, batches = rows_all.shape
    stored, rank, up_width = up.shape
    width = up_width + down.shape[2]

    def kernel(rows_ref, place_ref, down_ref, up_ref, out, sems):
        me = place_ref[0]

        def each(act):
            for to in range(replicas):

                def step(b, count):
                    row = rows_ref[to, b] - me * stored
                    mine = (row >= 0) & (row < stored)

                    @pl.when(mine)
                    def _():
                        slot = out.at[to, count]
                        act(pltpu.make_async_copy(up_ref.at[row], slot.at[:, 0:up_width], sems.at[0, to, count]))
                        act(pltpu.make_async_copy(down_ref.at[row], slot.at[:, up_width:width], sems.at[1, to, count]))

                    return count + mine.astype(jnp.int32)

                lax.fori_loop(0, batches, step, jnp.int32(0))

        each(lambda copy: copy.start())
        each(lambda copy: copy.wait())

    return pl.pallas_call(
        kernel,
        out_shape=jax.ShapeDtypeStruct((replicas, capacity, rank, width), BF16),
        in_specs=[SMEM, SMEM, HBM, HBM],
        out_specs=HBM,
        scratch_shapes=[pltpu.SemaphoreType.DMA((2, replicas, capacity))],
        compiler_params=PARAMS,
        name="pack",
    )(rows_all, place, down, up)


def collect(rows_ref, stored, arrived_ref, selected):
    batches = selected.shape[0]
    for owner in range(arrived_ref.shape[0]):

        def step(b, count):
            row = rows_ref[b] - owner * stored
            there = (row >= 0) & (row < stored)

            @pl.when(there)
            def _():
                selected[b] = arrived_ref[owner, count]

            return count + there.astype(jnp.int32)

        lax.fori_loop(0, batches, step, jnp.int32(0))


def whole(shape):
    return pl.BlockSpec(shape, lambda i: (0,) * len(shape))


def columns(packed, width, block):
    shape = packed.shape[:-1] + (width,)
    return pl.BlockSpec(shape, lambda i: (0,) * (len(shape) - 1) + (block,))


def batch_mask(rows, forks, batches, rank):
    batch_forks = forks // batches
    row = lax.broadcasted_iota(jnp.int32, (rows, batches * rank), 0)
    column = lax.broadcasted_iota(jnp.int32, (rows, batches * rank), 1)
    return lax.rem(row, forks) // batch_forks == column // rank


def low_rank(attended, forks, own_rows, stored, arrived):
    rows, depth = attended.shape
    batches = own_rows.shape[0]
    rank = arrived.shape[2]

    def kernel(rows_ref, a_ref, arrived_ref, o_ref, selected):
        collect(rows_ref, stored, arrived_ref, selected)
        every = lax.dot_general(
            a_ref[...],
            selected[...].reshape(batches * rank, depth),
            (((1,), (1,)), ((), ())),
            preferred_element_type=F32,
        )
        every = jnp.where(batch_mask(rows, forks, batches, rank), every, 0.0)
        total = every[:, 0:HD]
        for c in range(1, batches * rank // HD):
            total = total + every[:, c * HD : (c + 1) * HD]
        o_ref[...] = total

    return pl.pallas_call(
        kernel,
        out_shape=jax.ShapeDtypeStruct((rows, HD), F32),
        grid=(1,),
        in_specs=[SMEM, whole(attended.shape), columns(arrived, depth, (arrived.shape[3] - depth) // depth)],
        out_specs=whole((rows, HD)),
        scratch_shapes=[pltpu.VMEM((batches, rank, depth), BF16)],
        compiler_params=SMALL_PARAMS,
        name="low_rank",
    )(own_rows, attended, arrived)


def finish(base, ranks, forks, own_rows, stored, arrived):
    rows, width = base.shape
    batches = own_rows.shape[0]
    rank = arrived.shape[2]
    tile = min(width, 1024)
    steps = rows // forks

    def kernel(rows_ref, base_ref, *rest):
        rank_refs = rest[:-3]
        arrived_ref, o_ref, selected = rest[-3:]
        collect(rows_ref, stored, arrived_ref, selected)
        total = rank_refs[0][...]
        for r in rank_refs[1:]:
            total = total + r[...]
        spread = jnp.concatenate([total] * (batches * rank // HD), axis=1)
        spread = jnp.where(batch_mask(rows, forks, batches, rank), spread, 0.0)
        high = spread.astype(BF16)
        low = (spread - high.astype(F32)).astype(BF16)
        up = selected[...].reshape(batches * rank, tile)
        out = jnp.dot(high, up, preferred_element_type=F32)
        out = out + jnp.dot(low, up, preferred_element_type=F32)
        out = out + base_ref[...]
        out = out.astype(BF16)
        for s in range(steps):
            o_ref[:, s, :] = out[s * forks : (s + 1) * forks, :]

    by_tile = pl.BlockSpec((rows, tile), lambda i: (0, i))
    return pl.pallas_call(
        kernel,
        out_shape=jax.ShapeDtypeStruct((forks, steps, width), BF16),
        grid=(width // tile,),
        in_specs=[SMEM, by_tile]
        + [whole(r.shape) for r in ranks]
        + [pl.BlockSpec(arrived.shape[:3] + (tile,), lambda i: (0, 0, 0, i))],
        out_specs=pl.BlockSpec((forks, steps, tile), lambda i: (0, 0, i)),
        scratch_shapes=[pltpu.VMEM((batches, rank, tile), BF16)],
        compiler_params=SMALL_PARAMS,
        name="finish",
    )(own_rows, base, *ranks, arrived)


def lookup(wanted, adapter_table_row):
    matches = wanted[..., None] == jnp.arange(adapter_table_row.shape[0], dtype=jnp.int32)
    return jnp.sum(jnp.where(matches, adapter_table_row, 0), axis=-1)


def body(
    replicas,
    chips,
    queries,
    recent_keys,
    recent_values,
    prefix_key_value,
    prefix_length_each,
    batch_adapter_index,
    adapter_table_row,
    down_weight_table,
    up_weight_table,
    output_weight,
):
    forks, steps, _ = queries.shape
    batches = batch_adapter_index.shape[0]
    capacity = max(2, 2 * batches // replicas)
    model_width = output_weight.shape[1]
    width = model_width // (2 * chips)
    replica = lax.axis_index("replica").astype(jnp.int32)
    tensor = lax.axis_index("tensor").astype(jnp.int32)
    chip, core = tensor // 2, lax.rem(tensor, 2)
    place = replica.reshape(1)

    own_rows = lookup(batch_adapter_index, adapter_table_row)
    rows_all = lax.all_to_all(jnp.broadcast_to(own_rows, (replicas, batches)), "replica", 0, 0)
    parts = pack(down_weight_table, up_weight_table, rows_all, place, capacity)
    queries = lax.optimization_barrier((queries, parts))[0]
    arrived = lax.all_to_all(parts, "replica", 0, 0)

    lens = jnp.concatenate([prefix_length_each] * steps)[:, None]
    attended = attention(
        queries.transpose(1, 0, 2),
        recent_keys.transpose(1, 0, 2),
        recent_values.transpose(1, 0, 2),
        prefix_key_value,
        lens,
    )

    swap = [(t, t ^ 1) for t in range(2 * chips)]

    def along(e):
        return [(t, (t + 2 * e) % (2 * chips)) for t in range(2 * chips)]

    order = list(range(1, chips)) + [0]
    groups = [lax.rem(chip + e, chips) * 2 for e in order]
    halves = [
        lax.ppermute(project(attended, output_weight, g + 1 - core, width, [], BF16), "tensor", swap)
        for g in groups
    ]
    received = []
    for e, g, half in zip(order, groups, halves):
        if e:
            part = project(attended, output_weight, g + core, width, [half], BF16)
            received.append(lax.ppermute(part, "tensor", along(e)))
        else:
            base = project(attended, output_weight, g + core, width, [half] + received, F32)

    rank_part = low_rank(attended, forks, own_rows, down_weight_table.shape[0], arrived)
    ranks = [rank_part] + [
        lax.ppermute(rank_part, "tensor", [(t, t ^ e) for t in range(2 * chips)]) for e in range(1, 2 * chips)
    ]
    return finish(base, ranks, forks, own_rows, up_weight_table.shape[0], arrived)


def solution(mesh):
    placed = (
        P(("groups", "replica"), None, "tensor"),
        P(("groups", "replica"), None, "tensor"),
        P(("groups", "replica"), None, "tensor"),
        P(("groups", "replica"), None, None, "tensor"),
        P(("groups", "replica")),
        P(("groups", "replica")),
        P("groups"),
        P("replica", None, "tensor"),
        P("replica", None, "tensor"),
        P("tensor", None),
    )
    return jax.shard_map(
        functools.partial(body, mesh.shape["replica"], mesh.shape["tensor"] // 2),
        mesh=mesh,
        in_specs=placed,
        out_specs=P(("groups", "replica"), None, "tensor"),
        check_vma=False,
    )
```

```python
import functools
import math

import jax
import jax.numpy as jnp
from jax import lax
from jax.experimental import pallas as pl
from jax.experimental.pallas import tpu as pltpu
from jax.sharding import PartitionSpec as P

HD = 128
NEG = -1e30
LOG2_SCALE = math.log2(math.e) / math.sqrt(HD)
BF16, F32 = jnp.bfloat16, jnp.float32
VMEM = pl.BlockSpec(memory_space=pltpu.VMEM)
SMEM = pl.BlockSpec(memory_space=pltpu.SMEM)
SMALL_PARAMS = pltpu.CompilerParams(vmem_limit_bytes=20 * 1024 * 1024)
PARAMS = pltpu.CompilerParams(vmem_limit_bytes=58 * 1024 * 1024)


def attention_kernel(
    unit_heads, key_block, q_ref, rk_ref, rv_ref, kv_ref, lens_ref, o_ref,
    s_a, s_b, vaug, mx_a, mx_b, mb, acc, lensb, qs,
):
    steps, forks, width = q_ref.shape
    heads = width // HD
    heads_kv = rk_ref.shape[2] // HD
    group = heads // heads_kv
    head_rows = steps * forks
    rows = unit_heads * head_rows
    units = heads // unit_heads
    prefix = kv_ref.shape[2]
    longest = jnp.max(lens_ref[...])
    blocks = (longest + (key_block - 1)) // key_block
    lens = jnp.broadcast_to(lens_ref[...], (head_rows, HD))
    for i in range(unit_heads):
        lensb[i * head_rows : (i + 1) * head_rows, :] = lens
    for v in range(heads_kv):
        vaug[v, :, 0:HD] = kv_ref[0, 1, :, v * HD : (v + 1) * HD]
        vaug[v, :, HD : 2 * HD] = jnp.ones((prefix, HD), BF16)
    for h in range(heads):
        qs[h * head_rows : (h + 1) * head_rows, :] = q_ref[:, :, h * HD : (h + 1) * HD].reshape(head_rows, HD)
    score_refs, max_refs = (s_a, s_b), (mx_a, mx_b)

    def own_scores(u, t):
        parts = []
        for i in range(unit_heads):
            h = u * unit_heads + i
            v = h // group
            k = rk_ref[t, :, v * HD : (v + 1) * HD].astype(F32)
            for s in range(steps):
                if t <= s:
                    at = h * head_rows + s * forks
                    parts.append(jnp.sum(qs[at : at + forks, :].astype(F32) * k, axis=1, keepdims=True))
                else:
                    parts.append(jnp.full((forks, 1), NEG, F32))
        return jnp.concatenate(parts, axis=0)

    def score_block(u, j, s_ref, mx_ref):
        v = (u * unit_heads) // group
        keys = kv_ref[0, 0, pl.ds(pl.multiple_of(j * key_block, key_block), key_block), v * HD : (v + 1) * HD]
        s = lax.dot_general(
            qs[u * rows : (u + 1) * rows, :], keys, (((1,), (1,)), ((), ())), preferred_element_type=F32
        )
        top = mx_ref[...]
        left = lensb[...] - j * key_block
        lane = lax.broadcasted_iota(jnp.int32, (rows, HD), 1)
        for c in range(key_block // HD):
            part = jnp.where(lane + c * HD < left, s[:, c * HD : (c + 1) * HD], NEG)
            top = jnp.maximum(top, part)
            s_ref[j, :, c * HD : (c + 1) * HD] = part
        mx_ref[...] = top

    def value_block(u, j, s_ref):
        v = (u * unit_heads) // group
        top = mb[...]
        parts = [
            jnp.exp2((s_ref[j, :, c * HD : (c + 1) * HD] - top) * LOG2_SCALE).astype(BF16)
            for c in range(key_block // HD)
        ]
        values = vaug[v, pl.ds(pl.multiple_of(j * key_block, key_block), key_block), :]
        acc[...] += jnp.dot(jnp.concatenate(parts, axis=1), values, preferred_element_type=F32)

    for u in range(units + 1):
        done = u - 1
        if u < units:
            max_refs[u % 2][...] = jnp.full((rows, HD), NEG, F32)
        if u > 0:
            own = [own_scores(done, t) for t in range(steps)]
            top = jnp.max(max_refs[done % 2][...], axis=1, keepdims=True)
            for o in own:
                top = jnp.maximum(top, o)
            mb[...] = jnp.broadcast_to(top, (rows, HD))
            acc[...] = jnp.zeros_like(acc)

        @pl.loop(0, blocks)
        def _(j):
            if u < units:
                score_block(u, j, score_refs[u % 2], max_refs[u % 2])
            if u > 0:
                value_block(done, j, score_refs[done % 2])

        if u > 0:
            weights = [jnp.exp2((o - top) * LOG2_SCALE) for o in own]
            total = acc[:, HD : 2 * HD]
            for w in weights:
                total = total + w
            for i in range(unit_heads):
                h = done * unit_heads + i
                v = h // group
                at = slice(i * head_rows, (i + 1) * head_rows)
                mixed = acc[at, 0:HD]
                for t in range(steps):
                    value = rv_ref[t, :, v * HD : (v + 1) * HD].astype(F32)
                    value = jnp.concatenate([value] * steps, axis=0)
                    mixed = mixed + weights[t][at].astype(BF16).astype(F32) * value
                o_ref[:, h * HD : (h + 1) * HD] = (mixed / total[at]).astype(BF16)


def attention(q, rk, rv, kv, lens):
    steps, forks, width = q.shape
    prefix = kv.shape[2]
    heads_kv = rk.shape[2] // HD
    unit_heads = 2
    key_block = prefix
    rows = unit_heads * steps * forks
    return pl.pallas_call(
        functools.partial(attention_kernel, unit_heads, key_block),
        out_shape=jax.ShapeDtypeStruct((steps * forks, width), BF16),
        in_specs=[VMEM] * 5,
        out_specs=VMEM,
        scratch_shapes=[pltpu.VMEM((prefix // key_block, rows, key_block), F32)] * 2
        + [pltpu.VMEM((heads_kv, prefix, 2 * HD), BF16)]
        + [pltpu.VMEM((rows, HD), F32)] * 3
        + [
            pltpu.VMEM((rows, 2 * HD), F32),
            pltpu.VMEM((rows, HD), jnp.int32),
            pltpu.VMEM((width // HD * steps * forks, HD), BF16),
        ],
        compiler_params=PARAMS,
        cost_estimate=pl.CostEstimate(flops=2 * 10**10, bytes_accessed=6 * 2**20, transcendentals=0),
        name="attention",
    )(q, rk, rv, kv, lens)


def project(attended, weight, column_group, width, add, dtype):
    rows, depth = attended.shape
    tile = 1024 if width % 1024 == 0 else width
    tiles = width // tile

    def kernel(group_ref, a_ref, w_ref, *rest):
        o_ref = rest[-1]
        part = jnp.dot(a_ref[...], w_ref[...], preferred_element_type=F32)
        for r in rest[:-1]:
            part = part + r[...].astype(F32)
        o_ref[...] = part.astype(o_ref.dtype)

    in_specs = [
        pl.BlockSpec((rows, depth), lambda i, g: (0, 0)),
        pl.BlockSpec((depth, tile), lambda i, g: (0, g[0] * tiles + i)),
    ]
    operands = [attended, weight]
    in_specs += [pl.BlockSpec((rows, tile), lambda i, g: (0, i))] * len(add)
    operands += add
    return pl.pallas_call(
        kernel,
        out_shape=jax.ShapeDtypeStruct((rows, width), dtype),
        grid_spec=pltpu.PrefetchScalarGridSpec(
            num_scalar_prefetch=1,
            grid=(tiles,),
            in_specs=in_specs,
            out_specs=pl.BlockSpec((rows, tile), lambda i, g: (0, i)),
        ),
        compiler_params=PARAMS,
        cost_estimate=pl.CostEstimate(
            flops=2 * rows * depth * width, bytes_accessed=2 * depth * width, transcendentals=0
        ),
        name="project",
    )(column_group.reshape(1), *operands)


def pack(tables, rows_all, place, capacity):
    replicas, batches = rows_all.shape
    stored, rank, _ = tables[0].shape
    widths = [t.shape[2] for t in tables]

    def kernel(rows_ref, place_ref, *refs):
        out = refs[-1]
        to = pl.program_id(0)

        def step(b, count):
            row = rows_ref[to, b] - place_ref[0] * stored
            mine = (row >= 0) & (row < stored)

            @pl.when(mine)
            def _():
                at = 0
                for ref, width in zip(refs, widths):
                    out[0, count, :, at : at + width] = ref[row]
                    at += width

            return count + mine.astype(jnp.int32)

        lax.fori_loop(0, batches, step, jnp.int32(0))

    return pl.pallas_call(
        kernel,
        out_shape=jax.ShapeDtypeStruct((replicas, capacity, rank, sum(widths)), BF16),
        grid=(replicas,),
        in_specs=[SMEM, SMEM] + [whole(t.shape) for t in tables],
        out_specs=pl.BlockSpec((1, capacity, rank, sum(widths)), lambda i: (i, 0, 0, 0)),
        compiler_params=PARAMS,
        name="pack",
    )(rows_all, place, *tables)


def partner_rows(rows, place, received):
    nearest = received[0]
    batches = rows.shape[0]

    def kernel(rows_ref, place_ref, *refs):
        out = refs[-1]

        @pl.loop(0, batches)
        def _(b):
            pick(rows_ref[b], place_ref, refs[:-1], lambda value: out.__setitem__(b, value))

    return pl.pallas_call(
        kernel,
        out_shape=jax.ShapeDtypeStruct((batches,) + nearest.shape[1:], BF16),
        in_specs=[SMEM, SMEM] + [VMEM] * len(received),
        out_specs=VMEM,
        compiler_params=SMALL_PARAMS,
        name="partner_rows",
    )(rows, place, *received)


def pick(row, place_ref, refs, put):
    stored = refs[0].shape[0]
    me = place_ref[0]
    owner, at = row // stored, lax.rem(row, stored)
    apart = owner ^ me
    middle = (me == 1) | (me == 2)
    for ref, where in zip(
        refs,
        (
            apart == 1,
            middle & (apart == 3),
            middle & (apart == 2),
            jnp.logical_not(middle) & (apart == 2),
            jnp.logical_not(middle) & (apart == 3),
        ),
    ):

        @pl.when(where)
        def _():
            put(ref[at])


def low_rank_of_halves(attended, forks, own_rows, place, table, received, partner):
    rows, depth = attended.shape
    batches = own_rows.shape[0]
    stored, rank, _ = table.shape
    half = depth // 2

    def kernel(rows_ref, place_ref, a_ref, table_ref, *refs):
        partner_ref, o_ref, mine, other = refs[-4:]
        here = pl.multiple_of(place_ref[1] * half, half)
        there = pl.multiple_of((1 - place_ref[1]) * half, half)

        @pl.loop(0, batches)
        def _(b):
            row = rows_ref[b]
            own = row // stored == place_ref[0]
            at = lax.rem(row, stored)

            @pl.when(own)
            def _():
                mine[b] = table_ref[at, :, pl.ds(here, half)]
                other[b] = table_ref[at, :, pl.ds(there, half)]

            @pl.when(jnp.logical_not(own))
            def _():
                other[b] = partner_ref[b]

            pick(row, place_ref, refs[:-4], lambda value: mine.__setitem__(b, value))

        every = jnp.zeros((rows, batches * rank), F32)
        for at, selected in ((here, mine), (there, other)):
            every = every + lax.dot_general(
                a_ref[:, pl.ds(at, half)],
                selected[...].reshape(batches * rank, half),
                (((1,), (1,)), ((), ())),
                preferred_element_type=F32,
            )
        o_ref[...] = fold(every, rows, forks, batches, rank)

    return pl.pallas_call(
        kernel,
        out_shape=jax.ShapeDtypeStruct((rows, HD), F32),
        in_specs=[SMEM, SMEM] + [VMEM] * (3 + len(received)),
        out_specs=VMEM,
        scratch_shapes=[pltpu.VMEM((batches, rank, half), BF16)] * 2,
        compiler_params=SMALL_PARAMS,
        name="low_rank",
    )(own_rows, place, attended, table, *received, partner)


def collect(rows_ref, stored, arrived_ref, selected):
    batches = selected.shape[0]
    for owner in range(arrived_ref.shape[0]):

        def step(b, count):
            row = rows_ref[b] - owner * stored
            there = (row >= 0) & (row < stored)

            @pl.when(there)
            def _():
                selected[b] = arrived_ref[owner, count]

            return count + there.astype(jnp.int32)

        lax.fori_loop(0, batches, step, jnp.int32(0))


def whole(shape):
    return pl.BlockSpec(shape, lambda i: (0,) * len(shape))


def columns(packed, width, block):
    shape = packed.shape[:-1] + (width,)
    return pl.BlockSpec(shape, lambda i: (0,) * (len(shape) - 1) + (block,))


def batch_mask(rows, forks, batches, rank):
    batch_forks = forks // batches
    row = lax.broadcasted_iota(jnp.int32, (rows, batches * rank), 0)
    column = lax.broadcasted_iota(jnp.int32, (rows, batches * rank), 1)
    return lax.rem(row, forks) // batch_forks == column // rank


def fold(every, rows, forks, batches, rank):
    every = jnp.where(batch_mask(rows, forks, batches, rank), every, 0.0)
    total = every[:, 0:HD]
    for c in range(1, batches * rank // HD):
        total = total + every[:, c * HD : (c + 1) * HD]
    return total


def low_rank(attended, forks, own_rows, stored, arrived):
    rows, depth = attended.shape
    batches = own_rows.shape[0]
    rank = arrived.shape[2]

    def kernel(rows_ref, a_ref, arrived_ref, o_ref, selected):
        collect(rows_ref, stored, arrived_ref, selected)
        every = lax.dot_general(
            a_ref[...],
            selected[...].reshape(batches * rank, depth),
            (((1,), (1,)), ((), ())),
            preferred_element_type=F32,
        )
        o_ref[...] = fold(every, rows, forks, batches, rank)

    return pl.pallas_call(
        kernel,
        out_shape=jax.ShapeDtypeStruct((rows, HD), F32),
        grid=(1,),
        in_specs=[SMEM, whole(attended.shape), columns(arrived, depth, (arrived.shape[3] - depth) // depth)],
        out_specs=whole((rows, HD)),
        scratch_shapes=[pltpu.VMEM((batches, rank, depth), BF16)],
        compiler_params=SMALL_PARAMS,
        name="low_rank",
    )(own_rows, attended, arrived)


def finish(base, ranks, forks, own_rows, stored, arrived):
    rows, width = base.shape
    batches = own_rows.shape[0]
    rank = arrived.shape[2]
    tile = min(width, 1024)
    steps = rows // forks

    def kernel(rows_ref, base_ref, *rest):
        rank_refs = rest[:-3]
        arrived_ref, o_ref, selected = rest[-3:]
        collect(rows_ref, stored, arrived_ref, selected)
        total = rank_refs[0][...]
        for r in rank_refs[1:]:
            total = total + r[...]
        spread = jnp.concatenate([total] * (batches * rank // HD), axis=1)
        spread = jnp.where(batch_mask(rows, forks, batches, rank), spread, 0.0)
        high = spread.astype(BF16)
        low = (spread - high.astype(F32)).astype(BF16)
        up = selected[...].reshape(batches * rank, tile)
        out = jnp.dot(high, up, preferred_element_type=F32)
        out = out + jnp.dot(low, up, preferred_element_type=F32)
        out = out + base_ref[...]
        out = out.astype(BF16)
        for s in range(steps):
            o_ref[:, s, :] = out[s * forks : (s + 1) * forks, :]

    by_tile = pl.BlockSpec((rows, tile), lambda i: (0, i))
    return pl.pallas_call(
        kernel,
        out_shape=jax.ShapeDtypeStruct((forks, steps, width), BF16),
        grid=(width // tile,),
        in_specs=[SMEM, by_tile]
        + [whole(r.shape) for r in ranks]
        + [pl.BlockSpec(arrived.shape[:3] + (tile,), lambda i: (0, 0, 0, i))],
        out_specs=pl.BlockSpec((forks, steps, tile), lambda i: (0, 0, i)),
        scratch_shapes=[pltpu.VMEM((batches, rank, tile), BF16)],
        compiler_params=SMALL_PARAMS,
        name="finish",
    )(own_rows, base, *ranks, arrived)


def lookup(wanted, adapter_table_row):
    matches = wanted[..., None] == jnp.arange(adapter_table_row.shape[0], dtype=jnp.int32)
    return jnp.sum(jnp.where(matches, adapter_table_row, 0), axis=-1)


def body(
    groups,
    replicas,
    chips,
    queries,
    recent_keys,
    recent_values,
    prefix_key_value,
    prefix_length_each,
    batch_adapter_index,
    adapter_table_row,
    down_weight_table,
    up_weight_table,
    output_weight,
):
    forks, steps, _ = queries.shape
    batches = batch_adapter_index.shape[0]
    capacity = max(2, 2 * batches // replicas)
    model_width = output_weight.shape[1]
    width = model_width // (2 * chips)
    replica = lax.axis_index("replica").astype(jnp.int32)
    tensor = lax.axis_index("tensor").astype(jnp.int32)
    chip, core = tensor // 2, lax.rem(tensor, 2)
    place = replica.reshape(1)

    own_rows = lookup(batch_adapter_index, adapter_table_row)
    by_halves = replicas == 4 and groups == 2
    stored = down_weight_table.shape[0]
    if by_halves:
        group = lax.axis_index("groups").astype(jnp.int32)
        place = jnp.stack([replica, group])
        half = down_weight_table.shape[2] // 2
        mine = lax.dynamic_slice_in_dim(down_weight_table, group * half, half, axis=2)
        nearest = lax.ppermute(mine, "replica", [(0, 1), (1, 0), (2, 3), (3, 2)])
        middle = lax.ppermute(mine, "replica", [(1, 2), (2, 1)])
        far = lax.ppermute(mine, "replica", [(0, 2), (3, 1)])
        onward = [(1, 0), (2, 3)]
        received = [nearest, middle, far, lax.ppermute(middle, "replica", onward), lax.ppermute(far, "replica", onward)]
        rows_all = lax.all_gather(own_rows, ("groups", "replica"))
        partner_named = lax.dynamic_index_in_dim(rows_all, (1 - group) * replicas + replica, keepdims=False)
        rows_all = lax.dynamic_slice_in_dim(rows_all, group * replicas, replicas, axis=0)
        parts = pack([up_weight_table], rows_all, place, capacity)
    else:
        rows_all = lax.all_gather(own_rows, "replica")
        parts = pack([up_weight_table, down_weight_table], rows_all, place, capacity)
    queries = lax.optimization_barrier((queries, parts))[0]
    arrived = lax.all_to_all(parts, "replica", 0, 0)

    lens = jnp.concatenate([prefix_length_each] * steps)[:, None]
    attended = attention(
        queries.transpose(1, 0, 2),
        recent_keys.transpose(1, 0, 2),
        recent_values.transpose(1, 0, 2),
        prefix_key_value,
        lens,
    )

    if by_halves:
        attended, *received = lax.optimization_barrier((attended, *received))

    swap = [(t, t ^ 1) for t in range(2 * chips)]

    def along(e):
        return [(t, (t + 2 * e) % (2 * chips)) for t in range(2 * chips)]

    order = list(range(1, chips)) + [0]
    starts = [lax.rem(chip + e, chips) * 2 for e in order]
    halves = [
        lax.ppermute(project(attended, output_weight, g + 1 - core, width, [], BF16), "tensor", swap)
        for g in starts
    ]
    sums = []
    for e, g, half in zip(order, starts, halves):
        if e:
            part = project(attended, output_weight, g + core, width, [half], BF16)
            sums.append(lax.ppermute(part, "tensor", along(e)))
        else:
            base = project(attended, output_weight, g + core, width, [half] + sums, F32)

    if by_halves:
        partner = lax.ppermute(partner_rows(partner_named, place, received), "groups", [(0, 1), (1, 0)])
        rank_part = low_rank_of_halves(attended, forks, own_rows, place, down_weight_table, received, partner)
    else:
        rank_part = low_rank(attended, forks, own_rows, stored, arrived)
    ranks = [rank_part] + [
        lax.ppermute(rank_part, "tensor", [(t, t ^ e) for t in range(2 * chips)]) for e in range(1, 2 * chips)
    ]
    return finish(base, ranks, forks, own_rows, stored, arrived)


def solution(mesh):
    placed = (
        P(("groups", "replica"), None, "tensor"),
        P(("groups", "replica"), None, "tensor"),
        P(("groups", "replica"), None, "tensor"),
        P(("groups", "replica"), None, None, "tensor"),
        P(("groups", "replica")),
        P(("groups", "replica")),
        P("groups"),
        P("replica", None, "tensor"),
        P("replica", None, "tensor"),
        P("tensor", None),
    )
    return jax.shard_map(
        functools.partial(body, mesh.shape["groups"], mesh.shape["replica"], mesh.shape["tensor"] // 2),
        mesh=mesh,
        in_specs=placed,
        out_specs=P(("groups", "replica"), None, "tensor"),
        check_vma=False,
    )
```

```python
import functools
import math

import jax
import jax.numpy as jnp
from jax import lax
from jax.experimental import pallas as pl
from jax.experimental.pallas import tpu as pltpu
from jax.sharding import PartitionSpec as P

HD = 128
NEG = -1e30
LOG2_SCALE = math.log2(math.e) / math.sqrt(HD)
BF16, F32 = jnp.bfloat16, jnp.float32
VMEM = pl.BlockSpec(memory_space=pltpu.VMEM)
SMEM = pl.BlockSpec(memory_space=pltpu.SMEM)
PARAMS = pltpu.CompilerParams(vmem_limit_bytes=58 * 1024 * 1024)


def attention_kernel(
    unit_heads, key_block, q_ref, rk_ref, rv_ref, kv_ref, lens_ref, o_ref,
    s_a, s_b, vaug, mx_a, mx_b, mb, acc, lensb, qs,
):
    steps, forks, width = q_ref.shape
    heads = width // HD
    heads_kv = rk_ref.shape[2] // HD
    group = heads // heads_kv
    head_rows = steps * forks
    rows = unit_heads * head_rows
    units = heads // unit_heads
    prefix = kv_ref.shape[2]
    longest = jnp.max(lens_ref[...])
    blocks = (longest + (key_block - 1)) // key_block
    lens = jnp.broadcast_to(lens_ref[...], (head_rows, HD))
    for i in range(unit_heads):
        lensb[i * head_rows : (i + 1) * head_rows, :] = lens
    for v in range(heads_kv):
        vaug[v, :, 0:HD] = kv_ref[0, 1, :, v * HD : (v + 1) * HD]
        vaug[v, :, HD : 2 * HD] = jnp.ones((prefix, HD), BF16)
    for h in range(heads):
        qs[h * head_rows : (h + 1) * head_rows, :] = q_ref[:, :, h * HD : (h + 1) * HD].reshape(head_rows, HD)
    score_refs, max_refs = (s_a, s_b), (mx_a, mx_b)

    def own_scores(u, t):
        parts = []
        for i in range(unit_heads):
            h = u * unit_heads + i
            v = h // group
            k = rk_ref[t, :, v * HD : (v + 1) * HD].astype(F32)
            for s in range(steps):
                if t <= s:
                    at = h * head_rows + s * forks
                    parts.append(jnp.sum(qs[at : at + forks, :].astype(F32) * k, axis=1, keepdims=True))
                else:
                    parts.append(jnp.full((forks, 1), NEG, F32))
        return jnp.concatenate(parts, axis=0)

    def score_block(u, j, s_ref, mx_ref):
        v = (u * unit_heads) // group
        keys = kv_ref[0, 0, pl.ds(pl.multiple_of(j * key_block, key_block), key_block), v * HD : (v + 1) * HD]
        s = lax.dot_general(
            qs[u * rows : (u + 1) * rows, :], keys, (((1,), (1,)), ((), ())), preferred_element_type=F32
        )
        top = mx_ref[...]
        left = lensb[...] - j * key_block
        lane = lax.broadcasted_iota(jnp.int32, (rows, HD), 1)
        for c in range(key_block // HD):
            part = jnp.where(lane + c * HD < left, s[:, c * HD : (c + 1) * HD], NEG)
            top = jnp.maximum(top, part)
            s_ref[j, :, c * HD : (c + 1) * HD] = part
        mx_ref[...] = top

    def value_block(u, j, s_ref):
        v = (u * unit_heads) // group
        top = mb[...]
        parts = [
            jnp.exp2((s_ref[j, :, c * HD : (c + 1) * HD] - top) * LOG2_SCALE).astype(BF16)
            for c in range(key_block // HD)
        ]
        values = vaug[v, pl.ds(pl.multiple_of(j * key_block, key_block), key_block), :]
        acc[...] += jnp.dot(jnp.concatenate(parts, axis=1), values, preferred_element_type=F32)

    for u in range(units + 1):
        done = u - 1
        if u < units:
            max_refs[u % 2][...] = jnp.full((rows, HD), NEG, F32)
        if u > 0:
            own = [own_scores(done, t) for t in range(steps)]
            top = jnp.max(max_refs[done % 2][...], axis=1, keepdims=True)
            for o in own:
                top = jnp.maximum(top, o)
            mb[...] = jnp.broadcast_to(top, (rows, HD))
            acc[...] = jnp.zeros_like(acc)

        @pl.loop(0, blocks)
        def _(j):
            if u < units:
                score_block(u, j, score_refs[u % 2], max_refs[u % 2])
            if u > 0:
                value_block(done, j, score_refs[done % 2])

        if u > 0:
            weights = [jnp.exp2((o - top) * LOG2_SCALE) for o in own]
            total = acc[:, HD : 2 * HD]
            for w in weights:
                total = total + w
            for i in range(unit_heads):
                h = done * unit_heads + i
                v = h // group
                at = slice(i * head_rows, (i + 1) * head_rows)
                mixed = acc[at, 0:HD]
                for t in range(steps):
                    value = rv_ref[t, :, v * HD : (v + 1) * HD].astype(F32)
                    value = jnp.concatenate([value] * steps, axis=0)
                    mixed = mixed + weights[t][at].astype(BF16).astype(F32) * value
                o_ref[:, h * HD : (h + 1) * HD] = (mixed / total[at]).astype(BF16)


def attention(q, rk, rv, kv, lens):
    steps, forks, width = q.shape
    prefix = kv.shape[2]
    heads_kv = rk.shape[2] // HD
    unit_heads = 2
    key_block = prefix
    rows = unit_heads * steps * forks
    return pl.pallas_call(
        functools.partial(attention_kernel, unit_heads, key_block),
        out_shape=jax.ShapeDtypeStruct((steps * forks, width), BF16),
        in_specs=[VMEM] * 5,
        out_specs=VMEM,
        scratch_shapes=[pltpu.VMEM((prefix // key_block, rows, key_block), F32)] * 2
        + [pltpu.VMEM((heads_kv, prefix, 2 * HD), BF16)]
        + [pltpu.VMEM((rows, HD), F32)] * 3
        + [
            pltpu.VMEM((rows, 2 * HD), F32),
            pltpu.VMEM((rows, HD), jnp.int32),
            pltpu.VMEM((width // HD * steps * forks, HD), BF16),
        ],
        compiler_params=PARAMS,
        cost_estimate=pl.CostEstimate(flops=2 * 10**10, bytes_accessed=6 * 2**20, transcendentals=0),
        name="attention",
    )(q, rk, rv, kv, lens)


def project(attended, weight, column_group, width, add, dtype):
    rows, depth = attended.shape
    tile = 512 if width % 512 == 0 else width
    tiles = width // tile

    def kernel(group_ref, a_ref, w_ref, *rest):
        o_ref = rest[-1]
        part = jnp.dot(a_ref[...], w_ref[...], preferred_element_type=F32)
        for r in rest[:-1]:
            part = part + r[...].astype(F32)
        o_ref[...] = part.astype(o_ref.dtype)

    in_specs = [
        pl.BlockSpec((rows, depth), lambda i, g: (0, 0)),
        pl.BlockSpec((depth, tile), lambda i, g: (0, g[0] * tiles + i)),
    ]
    operands = [attended, weight]
    in_specs += [pl.BlockSpec((rows, tile), lambda i, g: (0, i))] * len(add)
    operands += add
    return pl.pallas_call(
        kernel,
        out_shape=jax.ShapeDtypeStruct((rows, width), dtype),
        grid_spec=pltpu.PrefetchScalarGridSpec(
            num_scalar_prefetch=1,
            grid=(tiles,),
            in_specs=in_specs,
            out_specs=pl.BlockSpec((rows, tile), lambda i, g: (0, i)),
        ),
        compiler_params=PARAMS,
        cost_estimate=pl.CostEstimate(
            flops=2 * rows * depth * width, bytes_accessed=2 * depth * width, transcendentals=0
        ),
        name="project",
    )(column_group.reshape(1), *operands)


def add(a, b):
    rows, width = a.shape
    spec = pl.BlockSpec((rows // 4, width), lambda i: (i, 0))

    def kernel(a_ref, b_ref, o_ref):
        o_ref[...] = (a_ref[...].astype(F32) + b_ref[...].astype(F32)).astype(o_ref.dtype)

    return pl.pallas_call(
        kernel,
        out_shape=jax.ShapeDtypeStruct((rows, width), BF16),
        grid=(4,),
        in_specs=[spec, spec],
        out_specs=spec,
        compiler_params=PARAMS,
        name="add",
    )(a, b)


def pack(tables, rows_all, place, capacity, relative):
    replicas, batches = rows_all.shape
    stored, rank, _ = tables[0].shape
    widths = [t.shape[2] for t in tables]

    def kernel(rows_ref, place_ref, *refs):
        out = refs[-1]
        to = pl.program_id(0)

        def step(b, count):
            row = rows_ref[to ^ place_ref[0] if relative else to, b] - place_ref[0] * stored
            mine = (row >= 0) & (row < stored)

            @pl.when(mine)
            def _():
                at = 0
                for ref, width in zip(refs, widths):
                    out[0, count, :, at : at + width] = ref[row]
                    at += width

            return count + mine.astype(jnp.int32)

        lax.fori_loop(0, batches, step, jnp.int32(0))

    return pl.pallas_call(
        kernel,
        out_shape=jax.ShapeDtypeStruct((replicas, capacity, rank, sum(widths)), BF16),
        grid=(replicas,),
        in_specs=[SMEM, SMEM] + [whole(t.shape) for t in tables],
        out_specs=pl.BlockSpec((1, capacity, rank, sum(widths)), lambda i: (i, 0, 0, 0)),
        compiler_params=PARAMS,
        name="pack",
    )(rows_all, place, *tables)


def partner_rows(rows, place, received):
    nearest = received[0]
    batches = rows.shape[0]

    def kernel(rows_ref, place_ref, *refs):
        out = refs[-1]

        @pl.loop(0, batches)
        def _(b):
            pick(rows_ref[b], place_ref, refs[:-1], lambda value: out.__setitem__(b, value))

    return pl.pallas_call(
        kernel,
        out_shape=jax.ShapeDtypeStruct((batches,) + nearest.shape[1:], BF16),
        in_specs=[SMEM, SMEM] + [VMEM] * len(received),
        out_specs=VMEM,
        compiler_params=PARAMS,
        name="partner_rows",
    )(rows, place, *received)


def pick(row, place_ref, refs, put):
    stored = refs[0].shape[0]
    me = place_ref[0]
    owner, at = row // stored, lax.rem(row, stored)
    apart = owner ^ me
    middle = (me == 1) | (me == 2)
    for ref, where in zip(
        refs,
        (
            apart == 1,
            middle & (apart == 3),
            middle & (apart == 2),
            jnp.logical_not(middle) & (apart == 2),
            jnp.logical_not(middle) & (apart == 3),
        ),
    ):

        @pl.when(where)
        def _():
            put(ref[at])


def low_rank_of_halves(attended, forks, own_rows, place, table, received, partner):
    rows, depth = attended.shape
    batches = own_rows.shape[0]
    stored, rank, _ = table.shape
    half = depth // 2

    def kernel(rows_ref, place_ref, a_ref, table_ref, *refs):
        partner_ref, o_ref, mine, other = refs[-4:]
        here = pl.multiple_of(place_ref[1] * half, half)
        there = pl.multiple_of((1 - place_ref[1]) * half, half)

        @pl.loop(0, batches)
        def _(b):
            row = rows_ref[b]
            own = row // stored == place_ref[0]
            at = lax.rem(row, stored)

            @pl.when(own)
            def _():
                mine[b] = table_ref[at, :, pl.ds(here, half)]
                other[b] = table_ref[at, :, pl.ds(there, half)]

            @pl.when(jnp.logical_not(own))
            def _():
                other[b] = partner_ref[b]

            pick(row, place_ref, refs[:-4], lambda value: mine.__setitem__(b, value))

        every = jnp.zeros((rows, batches * rank), F32)
        for at, selected in ((here, mine), (there, other)):
            every = every + lax.dot_general(
                a_ref[:, pl.ds(at, half)],
                selected[...].reshape(batches * rank, half),
                (((1,), (1,)), ((), ())),
                preferred_element_type=F32,
            )
        o_ref[...] = fold(every, rows, forks, batches, rank)

    return pl.pallas_call(
        kernel,
        out_shape=jax.ShapeDtypeStruct((rows, HD), F32),
        in_specs=[SMEM, SMEM] + [VMEM] * (3 + len(received)),
        out_specs=VMEM,
        scratch_shapes=[pltpu.VMEM((batches, rank, half), BF16)] * 2,
        compiler_params=PARAMS,
        name="low_rank",
    )(own_rows, place, attended, table, *received, partner)


def collect(rows_ref, stored, arrived_ref, selected):
    batches = selected.shape[0]
    for owner in range(arrived_ref.shape[0]):

        def step(b, count):
            row = rows_ref[b] - owner * stored
            there = (row >= 0) & (row < stored)

            @pl.when(there)
            def _():
                selected[b] = arrived_ref[owner, count]

            return count + there.astype(jnp.int32)

        lax.fori_loop(0, batches, step, jnp.int32(0))


def whole(shape):
    return pl.BlockSpec(shape, lambda i: (0,) * len(shape))


def columns(packed, width, block):
    shape = packed.shape[:-1] + (width,)
    return pl.BlockSpec(shape, lambda i: (0,) * (len(shape) - 1) + (block,))


def batch_mask(rows, forks, batches, rank):
    batch_forks = forks // batches
    row = lax.broadcasted_iota(jnp.int32, (rows, batches * rank), 0)
    column = lax.broadcasted_iota(jnp.int32, (rows, batches * rank), 1)
    return lax.rem(row, forks) // batch_forks == column // rank


def fold(every, rows, forks, batches, rank):
    every = jnp.where(batch_mask(rows, forks, batches, rank), every, 0.0)
    total = every[:, 0:HD]
    for c in range(1, batches * rank // HD):
        total = total + every[:, c * HD : (c + 1) * HD]
    return total


def low_rank(attended, forks, own_rows, stored, arrived):
    rows, depth = attended.shape
    batches = own_rows.shape[0]
    rank = arrived.shape[2]

    def kernel(rows_ref, a_ref, arrived_ref, o_ref, selected):
        collect(rows_ref, stored, arrived_ref, selected)
        every = lax.dot_general(
            a_ref[...],
            selected[...].reshape(batches * rank, depth),
            (((1,), (1,)), ((), ())),
            preferred_element_type=F32,
        )
        o_ref[...] = fold(every, rows, forks, batches, rank)

    return pl.pallas_call(
        kernel,
        out_shape=jax.ShapeDtypeStruct((rows, HD), F32),
        grid=(1,),
        in_specs=[SMEM, whole(attended.shape), columns(arrived, depth, (arrived.shape[3] - depth) // depth)],
        out_specs=whole((rows, HD)),
        scratch_shapes=[pltpu.VMEM((batches, rank, depth), BF16)],
        compiler_params=PARAMS,
        name="low_rank",
    )(own_rows, attended, arrived)


def finish(base, ranks, forks, own_rows, stored, arrived):
    rows, width = base.shape
    batches = own_rows.shape[0]
    rank = arrived.shape[2]
    tile = min(width, 1024)
    steps = rows // forks

    def kernel(rows_ref, base_ref, *rest):
        rank_refs = rest[:-3]
        arrived_ref, o_ref, selected = rest[-3:]
        collect(rows_ref, stored, arrived_ref, selected)
        total = rank_refs[0][...]
        for r in rank_refs[1:]:
            total = total + r[...]
        spread = jnp.concatenate([total] * (batches * rank // HD), axis=1)
        spread = jnp.where(batch_mask(rows, forks, batches, rank), spread, 0.0)
        high = spread.astype(BF16)
        low = (spread - high.astype(F32)).astype(BF16)
        up = selected[...].reshape(batches * rank, tile)
        out = jnp.dot(high, up, preferred_element_type=F32)
        out = out + jnp.dot(low, up, preferred_element_type=F32)
        out = out + base_ref[...]
        out = out.astype(BF16)
        for s in range(steps):
            o_ref[:, s, :] = out[s * forks : (s + 1) * forks, :]

    by_tile = pl.BlockSpec((rows, tile), lambda i: (0, i))
    return pl.pallas_call(
        kernel,
        out_shape=jax.ShapeDtypeStruct((forks, steps, width), BF16),
        grid=(width // tile,),
        in_specs=[SMEM, by_tile]
        + [whole(r.shape) for r in ranks]
        + [pl.BlockSpec(arrived.shape[:3] + (tile,), lambda i: (0, 0, 0, i))],
        out_specs=pl.BlockSpec((forks, steps, tile), lambda i: (0, 0, i)),
        scratch_shapes=[pltpu.VMEM((batches, rank, tile), BF16)],
        compiler_params=PARAMS,
        name="finish",
    )(own_rows, base, *ranks, arrived)


def lookup(wanted, adapter_table_row):
    matches = wanted[..., None] == jnp.arange(adapter_table_row.shape[0], dtype=jnp.int32)
    return jnp.sum(jnp.where(matches, adapter_table_row, 0), axis=-1)


def body(
    groups,
    replicas,
    chips,
    queries,
    recent_keys,
    recent_values,
    prefix_key_value,
    prefix_length_each,
    batch_adapter_index,
    adapter_table_row,
    down_weight_table,
    up_weight_table,
    output_weight,
):
    forks, steps, _ = queries.shape
    batches = batch_adapter_index.shape[0]
    capacity = max(2, 2 * batches // replicas)
    model_width = output_weight.shape[1]
    width = model_width // (2 * chips)
    replica = lax.axis_index("replica").astype(jnp.int32)
    tensor = lax.axis_index("tensor").astype(jnp.int32)
    chip, core = tensor // 2, lax.rem(tensor, 2)
    place = replica.reshape(1)

    own_rows = lookup(batch_adapter_index, adapter_table_row)
    by_halves = replicas == 4 and groups == 2
    stored = down_weight_table.shape[0]
    if by_halves:
        group = lax.axis_index("groups").astype(jnp.int32)
        place = jnp.stack([replica, group])
        half = down_weight_table.shape[2] // 2
        mine = lax.dynamic_slice_in_dim(down_weight_table, group * half, half, axis=2)
        nearest = lax.ppermute(mine, "replica", [(0, 1), (1, 0), (2, 3), (3, 2)])
        middle = lax.ppermute(mine, "replica", [(1, 2), (2, 1)])
        far = lax.ppermute(mine, "replica", [(0, 2), (3, 1)])
        onward = [(1, 0), (2, 3)]
        received = [nearest, middle, far, lax.ppermute(middle, "replica", onward), lax.ppermute(far, "replica", onward)]
        partner_named = lax.ppermute(own_rows, "groups", [(0, 1), (1, 0)])
        rows_all = jnp.stack(
            [own_rows]
            + [lax.ppermute(own_rows, "replica", [(z, z ^ d) for z in range(replicas)]) for d in range(1, replicas)]
        )
        parts = pack([up_weight_table], rows_all, place, capacity, True)
    else:
        rows_all = lax.all_gather(own_rows, "replica")
        parts = pack([up_weight_table, down_weight_table], rows_all, place, capacity, False)
    queries = lax.optimization_barrier((queries, parts))[0]
    arrived = lax.all_to_all(parts, "replica", 0, 0)

    lens = jnp.concatenate([prefix_length_each] * steps)[:, None]
    attended = attention(
        queries.transpose(1, 0, 2),
        recent_keys.transpose(1, 0, 2),
        recent_values.transpose(1, 0, 2),
        prefix_key_value,
        lens,
    )

    if by_halves:
        attended, *received[:3] = lax.optimization_barrier((attended, *received[:3]))

    swap = [(t, t ^ 1) for t in range(2 * chips)]

    def along(e):
        return [(t, (t + 2 * e) % (2 * chips)) for t in range(2 * chips)]

    order = list(range(1, chips)) + [0]
    starts = [lax.rem(chip + e, chips) * 2 for e in order]
    sums = []
    own_start = starts[-1]
    for e, g in zip(order[:-1], starts[:-1]):
        half = lax.ppermute(project(attended, output_weight, g + 1 - core, width, [], BF16), "tensor", swap)
        part = project(attended, output_weight, g + core, width, [], BF16)
        part = add(part, half)
        sums.append(lax.ppermute(part, "tensor", along(e)))
    own_attended = lax.optimization_barrier((attended, part))[0] if sums else attended
    half = lax.ppermute(project(own_attended, output_weight, own_start + 1 - core, width, [], BF16), "tensor", swap)
    base = project(own_attended, output_weight, own_start + core, width, [half] + sums, F32)

    if by_halves:
        partner = lax.ppermute(partner_rows(partner_named, place, received), "groups", [(0, 1), (1, 0)])
        rank_part = low_rank_of_halves(attended, forks, own_rows, place, down_weight_table, received, partner)
    else:
        rank_part = low_rank(attended, forks, own_rows, stored, arrived)
    ranks = [rank_part] + [
        lax.ppermute(rank_part, "tensor", [(t, t ^ e) for t in range(2 * chips)]) for e in range(1, 2 * chips)
    ]
    return finish(base, ranks, forks, own_rows, stored, arrived)


def solution(mesh):
    placed = (
        P(("groups", "replica"), None, "tensor"),
        P(("groups", "replica"), None, "tensor"),
        P(("groups", "replica"), None, "tensor"),
        P(("groups", "replica"), None, None, "tensor"),
        P(("groups", "replica")),
        P(("groups", "replica")),
        P("groups"),
        P("replica", None, "tensor"),
        P("replica", None, "tensor"),
        P("tensor", None),
    )
    return jax.shard_map(
        functools.partial(body, mesh.shape["groups"], mesh.shape["replica"], mesh.shape["tensor"] // 2),
        mesh=mesh,
        in_specs=placed,
        out_specs=P(("groups", "replica"), None, "tensor"),
        check_vma=False,
    )
```

```python
import functools
import math

import jax
import jax.numpy as jnp
from jax import lax
from jax.experimental import pallas as pl
from jax.experimental.pallas import tpu as pltpu
from jax.sharding import PartitionSpec as P

HD = 128
NEG = -1e30
LOG2_SCALE = math.log2(math.e) / math.sqrt(HD)
BF16, F32 = jnp.bfloat16, jnp.float32
VMEM = pl.BlockSpec(memory_space=pltpu.VMEM)
SMEM = pl.BlockSpec(memory_space=pltpu.SMEM)
SMALL_PARAMS = pltpu.CompilerParams(vmem_limit_bytes=20 * 1024 * 1024)
PARAMS = pltpu.CompilerParams(vmem_limit_bytes=58 * 1024 * 1024)


def attention_kernel(
    unit_heads, key_block, groups_ref, q_ref, rk_ref, rv_ref, kv_ref, lens_ref, w_ref, o_ref, *rest
):
    s_a, s_b, vaug, mx_a, mx_b, mb, acc, lensb, qs, w_buf, sems = rest[-11:]
    part_refs = rest[:-11]
    width_out = w_buf.shape[2]
    loads = [
        pltpu.make_async_copy(
            w_ref.at[:, pl.ds(pl.multiple_of(groups_ref[i] * width_out, width_out), width_out)],
            w_buf.at[i],
            sems.at[i],
        )
        for i in range(len(part_refs))
    ]
    for load in loads:
        load.start()
    steps, forks, width = q_ref.shape
    heads = width // HD
    heads_kv = rk_ref.shape[2] // HD
    group = heads // heads_kv
    head_rows = steps * forks
    rows = unit_heads * head_rows
    units = heads // unit_heads
    prefix = kv_ref.shape[2]
    longest = jnp.max(lens_ref[...])
    blocks = (longest + (key_block - 1)) // key_block
    lens = jnp.broadcast_to(lens_ref[...], (head_rows, HD))
    for i in range(unit_heads):
        lensb[i * head_rows : (i + 1) * head_rows, :] = lens
    for v in range(heads_kv):
        vaug[v, :, 0:HD] = kv_ref[0, 1, :, v * HD : (v + 1) * HD]
        vaug[v, :, HD : 2 * HD] = jnp.ones((prefix, HD), BF16)
    for h in range(heads):
        qs[h * head_rows : (h + 1) * head_rows, :] = q_ref[:, :, h * HD : (h + 1) * HD].reshape(head_rows, HD)
    score_refs, max_refs = (s_a, s_b), (mx_a, mx_b)

    def own_scores(u, t):
        parts = []
        for i in range(unit_heads):
            h = u * unit_heads + i
            v = h // group
            k = rk_ref[t, :, v * HD : (v + 1) * HD].astype(F32)
            for s in range(steps):
                if t <= s:
                    at = h * head_rows + s * forks
                    parts.append(jnp.sum(qs[at : at + forks, :].astype(F32) * k, axis=1, keepdims=True))
                else:
                    parts.append(jnp.full((forks, 1), NEG, F32))
        return jnp.concatenate(parts, axis=0)

    def score_block(u, j, s_ref, mx_ref):
        v = (u * unit_heads) // group
        keys = kv_ref[0, 0, pl.ds(pl.multiple_of(j * key_block, key_block), key_block), v * HD : (v + 1) * HD]
        s = lax.dot_general(
            qs[u * rows : (u + 1) * rows, :], keys, (((1,), (1,)), ((), ())), preferred_element_type=F32
        )
        top = mx_ref[...]
        left = lensb[...] - j * key_block
        lane = lax.broadcasted_iota(jnp.int32, (rows, HD), 1)
        for c in range(key_block // HD):
            part = jnp.where(lane + c * HD < left, s[:, c * HD : (c + 1) * HD], NEG)
            top = jnp.maximum(top, part)
            s_ref[j, :, c * HD : (c + 1) * HD] = part
        mx_ref[...] = top

    def value_block(u, j, s_ref):
        v = (u * unit_heads) // group
        top = mb[...]
        parts = [
            jnp.exp2((s_ref[j, :, c * HD : (c + 1) * HD] - top) * LOG2_SCALE).astype(BF16)
            for c in range(key_block // HD)
        ]
        values = vaug[v, pl.ds(pl.multiple_of(j * key_block, key_block), key_block), :]
        acc[...] += jnp.dot(jnp.concatenate(parts, axis=1), values, preferred_element_type=F32)

    for u in range(units + 1):
        done = u - 1
        if u < units:
            max_refs[u % 2][...] = jnp.full((rows, HD), NEG, F32)
        if u > 0:
            own = [own_scores(done, t) for t in range(steps)]
            top = jnp.max(max_refs[done % 2][...], axis=1, keepdims=True)
            for o in own:
                top = jnp.maximum(top, o)
            mb[...] = jnp.broadcast_to(top, (rows, HD))
            acc[...] = jnp.zeros_like(acc)

        @pl.loop(0, blocks)
        def _(j):
            if u < units:
                score_block(u, j, score_refs[u % 2], max_refs[u % 2])
            if u > 0:
                value_block(done, j, score_refs[done % 2])

        if u > 0:
            weights = [jnp.exp2((o - top) * LOG2_SCALE) for o in own]
            total = acc[:, HD : 2 * HD]
            for w in weights:
                total = total + w
            for i in range(unit_heads):
                h = done * unit_heads + i
                v = h // group
                at = slice(i * head_rows, (i + 1) * head_rows)
                mixed = acc[at, 0:HD]
                for t in range(steps):
                    value = rv_ref[t, :, v * HD : (v + 1) * HD].astype(F32)
                    value = jnp.concatenate([value] * steps, axis=0)
                    mixed = mixed + weights[t][at].astype(BF16).astype(F32) * value
                o_ref[:, h * HD : (h + 1) * HD] = (mixed / total[at]).astype(BF16)

    tile = 512
    for i, (load, part_ref) in enumerate(zip(loads, part_refs)):
        load.wait()
        for c in range(width_out // tile):
            at = slice(c * tile, (c + 1) * tile)
            part_ref[:, at] = jnp.dot(o_ref[...], w_buf[i, :, at], preferred_element_type=F32).astype(BF16)


def attention(q, rk, rv, kv, lens, weight, column_groups, out_width):
    steps, forks, width = q.shape
    prefix = kv.shape[2]
    heads_kv = rk.shape[2] // HD
    parts = column_groups.shape[0]
    unit_heads = 2
    key_block = prefix
    rows = unit_heads * steps * forks
    return pl.pallas_call(
        functools.partial(attention_kernel, unit_heads, key_block),
        out_shape=[jax.ShapeDtypeStruct((steps * forks, width), BF16)]
        + [jax.ShapeDtypeStruct((steps * forks, out_width), BF16)] * parts,
        in_specs=[SMEM] + [VMEM] * 5 + [pl.BlockSpec(memory_space=pl.ANY)],
        out_specs=[VMEM] * (1 + parts),
        scratch_shapes=[pltpu.VMEM((prefix // key_block, rows, key_block), F32)] * 2
        + [pltpu.VMEM((heads_kv, prefix, 2 * HD), BF16)]
        + [pltpu.VMEM((rows, HD), F32)] * 3
        + [
            pltpu.VMEM((rows, 2 * HD), F32),
            pltpu.VMEM((rows, HD), jnp.int32),
            pltpu.VMEM((width // HD * steps * forks, HD), BF16),
            pltpu.VMEM((parts, weight.shape[0], out_width), BF16),
            pltpu.SemaphoreType.DMA((parts,)),
        ],
        compiler_params=PARAMS,
        cost_estimate=pl.CostEstimate(flops=2 * 10**10, bytes_accessed=6 * 2**20, transcendentals=0),
        name="attention",
    )(column_groups, q, rk, rv, kv, lens, weight)


def project(attended, weight, column_group, width, add, dtype):
    rows, depth = attended.shape
    tile = 1024 if width % 1024 == 0 else width
    tiles = width // tile

    def kernel(group_ref, a_ref, w_ref, *rest):
        o_ref = rest[-1]
        part = jnp.dot(a_ref[...], w_ref[...], preferred_element_type=F32)
        for r in rest[:-1]:
            part = part + r[...].astype(F32)
        o_ref[...] = part.astype(o_ref.dtype)

    in_specs = [
        pl.BlockSpec((rows, depth), lambda i, g: (0, 0)),
        pl.BlockSpec((depth, tile), lambda i, g: (0, g[0] * tiles + i)),
    ]
    operands = [attended, weight]
    in_specs += [pl.BlockSpec((rows, tile), lambda i, g: (0, i))] * len(add)
    operands += add
    return pl.pallas_call(
        kernel,
        out_shape=jax.ShapeDtypeStruct((rows, width), dtype),
        grid_spec=pltpu.PrefetchScalarGridSpec(
            num_scalar_prefetch=1,
            grid=(tiles,),
            in_specs=in_specs,
            out_specs=pl.BlockSpec((rows, tile), lambda i, g: (0, i)),
        ),
        compiler_params=PARAMS,
        cost_estimate=pl.CostEstimate(
            flops=2 * rows * depth * width, bytes_accessed=2 * depth * width, transcendentals=0
        ),
        name="project",
    )(column_group.reshape(1), *operands)


def pack(tables, rows_all, place, capacity, relative):
    replicas, batches = rows_all.shape
    stored, rank, _ = tables[0].shape
    widths = [t.shape[2] for t in tables]

    def kernel(rows_ref, place_ref, *refs):
        out = refs[-1]
        to = pl.program_id(0)

        def step(b, count):
            row = rows_ref[to ^ place_ref[0] if relative else to, b] - place_ref[0] * stored
            mine = (row >= 0) & (row < stored)

            @pl.when(mine)
            def _():
                at = 0
                for ref, width in zip(refs, widths):
                    out[0, count, :, at : at + width] = ref[row]
                    at += width

            return count + mine.astype(jnp.int32)

        lax.fori_loop(0, batches, step, jnp.int32(0))

    return pl.pallas_call(
        kernel,
        out_shape=jax.ShapeDtypeStruct((replicas, capacity, rank, sum(widths)), BF16),
        grid=(replicas,),
        in_specs=[SMEM, SMEM] + [whole(t.shape) for t in tables],
        out_specs=pl.BlockSpec((1, capacity, rank, sum(widths)), lambda i: (i, 0, 0, 0)),
        compiler_params=PARAMS,
        name="pack",
    )(rows_all, place, *tables)


def partner_rows(rows, place, received):
    nearest = received[0]
    batches = rows.shape[0]

    def kernel(rows_ref, place_ref, *refs):
        out = refs[-1]

        @pl.loop(0, batches)
        def _(b):
            pick(rows_ref[b], place_ref, refs[:-1], lambda value: out.__setitem__(b, value))

    return pl.pallas_call(
        kernel,
        out_shape=jax.ShapeDtypeStruct((batches,) + nearest.shape[1:], BF16),
        in_specs=[SMEM, SMEM] + [VMEM] * len(received),
        out_specs=VMEM,
        compiler_params=PARAMS,
        name="partner_rows",
    )(rows, place, *received)


def pick(row, place_ref, refs, put):
    stored = refs[0].shape[0]
    me = place_ref[0]
    owner, at = row // stored, lax.rem(row, stored)
    apart = owner ^ me
    middle = (me == 1) | (me == 2)
    for ref, where in zip(
        refs,
        (
            apart == 1,
            middle & (apart == 3),
            middle & (apart == 2),
            jnp.logical_not(middle) & (apart == 2),
            jnp.logical_not(middle) & (apart == 3),
        ),
    ):

        @pl.when(where)
        def _():
            put(ref[at])


def low_rank_of_halves(attended, forks, own_rows, place, table, received, partner):
    rows, depth = attended.shape
    batches = own_rows.shape[0]
    stored, rank, _ = table.shape
    half = depth // 2

    def kernel(rows_ref, place_ref, a_ref, table_ref, *refs):
        partner_ref, o_ref, mine, other = refs[-4:]
        here = pl.multiple_of(place_ref[1] * half, half)
        there = pl.multiple_of((1 - place_ref[1]) * half, half)

        @pl.loop(0, batches)
        def _(b):
            row = rows_ref[b]
            own = row // stored == place_ref[0]
            at = lax.rem(row, stored)

            @pl.when(own)
            def _():
                mine[b] = table_ref[at, :, pl.ds(here, half)]
                other[b] = table_ref[at, :, pl.ds(there, half)]

            @pl.when(jnp.logical_not(own))
            def _():
                other[b] = partner_ref[b]

            pick(row, place_ref, refs[:-4], lambda value: mine.__setitem__(b, value))

        every = jnp.zeros((rows, batches * rank), F32)
        for at, selected in ((here, mine), (there, other)):
            every = every + lax.dot_general(
                a_ref[:, pl.ds(at, half)],
                selected[...].reshape(batches * rank, half),
                (((1,), (1,)), ((), ())),
                preferred_element_type=F32,
            )
        o_ref[...] = fold(every, rows, forks, batches, rank)

    return pl.pallas_call(
        kernel,
        out_shape=jax.ShapeDtypeStruct((rows, HD), F32),
        in_specs=[SMEM, SMEM] + [VMEM] * (3 + len(received)),
        out_specs=VMEM,
        scratch_shapes=[pltpu.VMEM((batches, rank, half), BF16)] * 2,
        compiler_params=PARAMS,
        name="low_rank",
    )(own_rows, place, attended, table, *received, partner)


def collect(rows_ref, stored, arrived_ref, selected):
    batches = selected.shape[0]
    for owner in range(arrived_ref.shape[0]):

        def step(b, count):
            row = rows_ref[b] - owner * stored
            there = (row >= 0) & (row < stored)

            @pl.when(there)
            def _():
                selected[b] = arrived_ref[owner, count]

            return count + there.astype(jnp.int32)

        lax.fori_loop(0, batches, step, jnp.int32(0))


def whole(shape):
    return pl.BlockSpec(shape, lambda i: (0,) * len(shape))


def columns(packed, width, block):
    shape = packed.shape[:-1] + (width,)
    return pl.BlockSpec(shape, lambda i: (0,) * (len(shape) - 1) + (block,))


def batch_mask(rows, forks, batches, rank):
    batch_forks = forks // batches
    row = lax.broadcasted_iota(jnp.int32, (rows, batches * rank), 0)
    column = lax.broadcasted_iota(jnp.int32, (rows, batches * rank), 1)
    return lax.rem(row, forks) // batch_forks == column // rank


def fold(every, rows, forks, batches, rank):
    every = jnp.where(batch_mask(rows, forks, batches, rank), every, 0.0)
    total = every[:, 0:HD]
    for c in range(1, batches * rank // HD):
        total = total + every[:, c * HD : (c + 1) * HD]
    return total


def low_rank(attended, forks, own_rows, stored, arrived):
    rows, depth = attended.shape
    batches = own_rows.shape[0]
    rank = arrived.shape[2]

    def kernel(rows_ref, a_ref, arrived_ref, o_ref, selected):
        collect(rows_ref, stored, arrived_ref, selected)
        every = lax.dot_general(
            a_ref[...],
            selected[...].reshape(batches * rank, depth),
            (((1,), (1,)), ((), ())),
            preferred_element_type=F32,
        )
        o_ref[...] = fold(every, rows, forks, batches, rank)

    return pl.pallas_call(
        kernel,
        out_shape=jax.ShapeDtypeStruct((rows, HD), F32),
        grid=(1,),
        in_specs=[SMEM, whole(attended.shape), columns(arrived, depth, (arrived.shape[3] - depth) // depth)],
        out_specs=whole((rows, HD)),
        scratch_shapes=[pltpu.VMEM((batches, rank, depth), BF16)],
        compiler_params=PARAMS,
        name="low_rank",
    )(own_rows, attended, arrived)


def finish(bases, ranks, forks, own_rows, stored, arrived):
    rows, width = bases[0].shape
    n_bases = len(bases)
    batches = own_rows.shape[0]
    rank = arrived.shape[2]
    tile = min(width, 1024)
    steps = rows // forks

    def kernel(rows_ref, *rest):
        base_refs, rank_refs = rest[:n_bases], rest[n_bases:-3]
        arrived_ref, o_ref, selected = rest[-3:]
        collect(rows_ref, stored, arrived_ref, selected)
        total = rank_refs[0][...]
        for r in rank_refs[1:]:
            total = total + r[...]
        spread = jnp.concatenate([total] * (batches * rank // HD), axis=1)
        spread = jnp.where(batch_mask(rows, forks, batches, rank), spread, 0.0)
        high = spread.astype(BF16)
        low = (spread - high.astype(F32)).astype(BF16)
        up = selected[...].reshape(batches * rank, tile)
        out = jnp.dot(high, up, preferred_element_type=F32)
        out = out + jnp.dot(low, up, preferred_element_type=F32)
        for r in base_refs:
            out = out + r[...].astype(F32)
        out = out.astype(BF16)
        for s in range(steps):
            o_ref[:, s, :] = out[s * forks : (s + 1) * forks, :]

    by_tile = pl.BlockSpec((rows, tile), lambda i: (0, i))
    return pl.pallas_call(
        kernel,
        out_shape=jax.ShapeDtypeStruct((forks, steps, width), BF16),
        grid=(width // tile,),
        in_specs=[SMEM]
        + [by_tile] * n_bases
        + [whole(r.shape) for r in ranks]
        + [pl.BlockSpec(arrived.shape[:3] + (tile,), lambda i: (0, 0, 0, i))],
        out_specs=pl.BlockSpec((forks, steps, tile), lambda i: (0, 0, i)),
        scratch_shapes=[pltpu.VMEM((batches, rank, tile), BF16)],
        compiler_params=SMALL_PARAMS,
        name="finish",
    )(own_rows, *bases, *ranks, arrived)


def lookup(wanted, adapter_table_row):
    matches = wanted[..., None] == jnp.arange(adapter_table_row.shape[0], dtype=jnp.int32)
    return jnp.sum(jnp.where(matches, adapter_table_row, 0), axis=-1)


def body(
    groups,
    replicas,
    chips,
    queries,
    recent_keys,
    recent_values,
    prefix_key_value,
    prefix_length_each,
    batch_adapter_index,
    adapter_table_row,
    down_weight_table,
    up_weight_table,
    output_weight,
):
    forks, steps, _ = queries.shape
    batches = batch_adapter_index.shape[0]
    capacity = max(2, 2 * batches // replicas)
    model_width = output_weight.shape[1]
    width = model_width // (2 * chips)
    replica = lax.axis_index("replica").astype(jnp.int32)
    tensor = lax.axis_index("tensor").astype(jnp.int32)
    chip, core = tensor // 2, lax.rem(tensor, 2)
    place = replica.reshape(1)

    own_rows = lookup(batch_adapter_index, adapter_table_row)
    by_halves = replicas == 4 and groups == 2
    stored = down_weight_table.shape[0]
    if by_halves:
        group = lax.axis_index("groups").astype(jnp.int32)
        place = jnp.stack([replica, group])
        half = down_weight_table.shape[2] // 2
        mine = lax.dynamic_slice_in_dim(down_weight_table, group * half, half, axis=2)
        nearest = lax.ppermute(mine, "replica", [(0, 1), (1, 0), (2, 3), (3, 2)])
        middle = lax.ppermute(mine, "replica", [(1, 2), (2, 1)])
        far = lax.ppermute(mine, "replica", [(0, 2), (3, 1)])
        onward = [(1, 0), (2, 3)]
        received = [nearest, middle, far, lax.ppermute(middle, "replica", onward), lax.ppermute(far, "replica", onward)]
        partner_named = lax.ppermute(own_rows, "groups", [(0, 1), (1, 0)])
        rows_all = jnp.stack(
            [own_rows]
            + [lax.ppermute(own_rows, "replica", [(z, z ^ d) for z in range(replicas)]) for d in range(1, replicas)]
        )
        parts = pack([up_weight_table], rows_all, place, capacity, True)
    else:
        rows_all = lax.all_gather(own_rows, "replica")
        parts = pack([up_weight_table, down_weight_table], rows_all, place, capacity, False)
    queries = lax.optimization_barrier((queries, parts))[0]
    arrived = lax.all_to_all(parts, "replica", 0, 0)

    lens = jnp.concatenate([prefix_length_each] * steps)[:, None]
    order = list(range(1, chips)) + [0]
    starts = [lax.rem(chip + e, chips) * 2 for e in order]
    first = [starts[0] + 1 - core, starts[0] + core, starts[-1] + 1 - core]
    attended, *parts = attention(
        queries.transpose(1, 0, 2),
        recent_keys.transpose(1, 0, 2),
        recent_values.transpose(1, 0, 2),
        prefix_key_value,
        lens,
        output_weight,
        jnp.stack(first),
        width,
    )
    if by_halves:
        attended, *rest = lax.optimization_barrier((attended, *parts, *received[:3]))
        parts, received[:3] = rest[: len(parts)], rest[len(parts) :]

    swap = [(t, t ^ 1) for t in range(2 * chips)]

    def along(e):
        return [(t, (t + 2 * e) % (2 * chips)) for t in range(2 * chips)]

    swapped = [lax.ppermute(p, "tensor", swap) for p in (parts[0], parts[2])]
    sums = []
    for i, (e, g) in enumerate(zip(order[:-1], starts[:-1])):
        if i == 0:
            half, part = swapped[0], parts[1]
        else:
            half = lax.ppermute(project(attended, output_weight, g + 1 - core, width, [], BF16), "tensor", swap)
            part = project(attended, output_weight, g + core, width, [], BF16)
        part = (part.astype(F32) + half.astype(F32)).astype(BF16)
        sums.append(lax.ppermute(part, "tensor", along(e)))
    last = lax.optimization_barrier((attended, part))[0]
    base = project(last, output_weight, starts[-1] + core, width, [swapped[1]], BF16)

    if by_halves:
        partner = lax.ppermute(partner_rows(partner_named, place, received), "groups", [(0, 1), (1, 0)])
        rank_part = low_rank_of_halves(attended, forks, own_rows, place, down_weight_table, received, partner)
    else:
        rank_part = low_rank(attended, forks, own_rows, stored, arrived)
    ranks = [rank_part] + [
        lax.ppermute(rank_part, "tensor", [(t, t ^ e) for t in range(2 * chips)]) for e in range(1, 2 * chips)
    ]
    return finish([base] + sums, ranks, forks, own_rows, stored, arrived)


def solution(mesh):
    placed = (
        P(("groups", "replica"), None, "tensor"),
        P(("groups", "replica"), None, "tensor"),
        P(("groups", "replica"), None, "tensor"),
        P(("groups", "replica"), None, None, "tensor"),
        P(("groups", "replica")),
        P(("groups", "replica")),
        P("groups"),
        P("replica", None, "tensor"),
        P("replica", None, "tensor"),
        P("tensor", None),
    )
    return jax.shard_map(
        functools.partial(body, mesh.shape["groups"], mesh.shape["replica"], mesh.shape["tensor"] // 2),
        mesh=mesh,
        in_specs=placed,
        out_specs=P(("groups", "replica"), None, "tensor"),
        check_vma=False,
    )
```

```python
import functools
import math

import jax
import jax.numpy as jnp
from jax import lax
from jax.experimental import pallas as pl
from jax.experimental.pallas import tpu as pltpu
from jax.sharding import PartitionSpec as P

HD = 128
NEG = -1e30
LOG2_SCALE = math.log2(math.e) / math.sqrt(HD)
BF16, F32 = jnp.bfloat16, jnp.float32
VMEM = pl.BlockSpec(memory_space=pltpu.VMEM)
SMEM = pl.BlockSpec(memory_space=pltpu.SMEM)
SMALL_PARAMS = pltpu.CompilerParams(vmem_limit_bytes=20 * 1024 * 1024)
PARAMS = pltpu.CompilerParams(vmem_limit_bytes=58 * 1024 * 1024)


def attention_kernel(
    unit_heads, key_block, groups_ref, q_ref, rk_ref, rv_ref, kv_ref, lens_ref, w_ref, o_ref, *rest
):
    s_a, s_b, vaug, mx_a, mx_b, mb, acc, lensb, qs, w_buf, sems = rest[-11:]
    part_refs = rest[:-11]
    width_out = w_buf.shape[2]
    loads = [
        pltpu.make_async_copy(
            w_ref.at[:, pl.ds(pl.multiple_of(groups_ref[i] * width_out, width_out), width_out)],
            w_buf.at[i],
            sems.at[i],
        )
        for i in range(len(part_refs))
    ]
    for load in loads:
        load.start()
    steps, forks, width = q_ref.shape
    heads = width // HD
    heads_kv = rk_ref.shape[2] // HD
    group = heads // heads_kv
    head_rows = steps * forks
    rows = unit_heads * head_rows
    units = heads // unit_heads
    prefix = kv_ref.shape[2]
    longest = jnp.max(lens_ref[...])
    blocks = (longest + (key_block - 1)) // key_block
    lens = jnp.broadcast_to(lens_ref[...], (head_rows, HD))
    for i in range(unit_heads):
        lensb[i * head_rows : (i + 1) * head_rows, :] = lens
    for v in range(heads_kv):
        vaug[v, :, 0:HD] = kv_ref[0, 1, :, v * HD : (v + 1) * HD]
        vaug[v, :, HD : 2 * HD] = jnp.ones((prefix, HD), BF16)
    for h in range(heads):
        qs[h * head_rows : (h + 1) * head_rows, :] = q_ref[:, :, h * HD : (h + 1) * HD].reshape(head_rows, HD)
    score_refs, max_refs = (s_a, s_b), (mx_a, mx_b)

    def own_scores(u, t):
        parts = []
        for i in range(unit_heads):
            h = u * unit_heads + i
            v = h // group
            k = rk_ref[t, :, v * HD : (v + 1) * HD].astype(F32)
            for s in range(steps):
                if t <= s:
                    at = h * head_rows + s * forks
                    parts.append(jnp.sum(qs[at : at + forks, :].astype(F32) * k, axis=1, keepdims=True))
                else:
                    parts.append(jnp.full((forks, 1), NEG, F32))
        return jnp.concatenate(parts, axis=0)

    def score_block(u, j, s_ref, mx_ref):
        v = (u * unit_heads) // group
        keys = kv_ref[0, 0, pl.ds(pl.multiple_of(j * key_block, key_block), key_block), v * HD : (v + 1) * HD]
        s = lax.dot_general(
            qs[u * rows : (u + 1) * rows, :], keys, (((1,), (1,)), ((), ())), preferred_element_type=F32
        )
        top = mx_ref[...]
        left = lensb[...] - j * key_block
        lane = lax.broadcasted_iota(jnp.int32, (rows, HD), 1)
        for c in range(key_block // HD):
            part = jnp.where(lane + c * HD < left, s[:, c * HD : (c + 1) * HD], NEG)
            top = jnp.maximum(top, part)
            s_ref[j, :, c * HD : (c + 1) * HD] = part
        mx_ref[...] = top

    def value_block(u, j, s_ref):
        v = (u * unit_heads) // group
        top = mb[...]
        parts = [
            jnp.exp2((s_ref[j, :, c * HD : (c + 1) * HD] - top) * LOG2_SCALE).astype(BF16)
            for c in range(key_block // HD)
        ]
        values = vaug[v, pl.ds(pl.multiple_of(j * key_block, key_block), key_block), :]
        acc[...] += jnp.dot(jnp.concatenate(parts, axis=1), values, preferred_element_type=F32)

    for u in range(units + 1):
        done = u - 1
        if u < units:
            max_refs[u % 2][...] = jnp.full((rows, HD), NEG, F32)
        if u > 0:
            own = [own_scores(done, t) for t in range(steps)]
            top = jnp.max(max_refs[done % 2][...], axis=1, keepdims=True)
            for o in own:
                top = jnp.maximum(top, o)
            mb[...] = jnp.broadcast_to(top, (rows, HD))
            acc[...] = jnp.zeros_like(acc)

        @pl.loop(0, blocks)
        def _(j):
            if u < units:
                score_block(u, j, score_refs[u % 2], max_refs[u % 2])
            if u > 0:
                value_block(done, j, score_refs[done % 2])

        if u > 0:
            weights = [jnp.exp2((o - top) * LOG2_SCALE) for o in own]
            total = acc[:, HD : 2 * HD]
            for w in weights:
                total = total + w
            for i in range(unit_heads):
                h = done * unit_heads + i
                v = h // group
                at = slice(i * head_rows, (i + 1) * head_rows)
                mixed = acc[at, 0:HD]
                for t in range(steps):
                    value = rv_ref[t, :, v * HD : (v + 1) * HD].astype(F32)
                    value = jnp.concatenate([value] * steps, axis=0)
                    mixed = mixed + weights[t][at].astype(BF16).astype(F32) * value
                o_ref[:, h * HD : (h + 1) * HD] = (mixed / total[at]).astype(BF16)

    tile = 512
    for i, (load, part_ref) in enumerate(zip(loads, part_refs)):
        load.wait()
        for c in range(width_out // tile):
            at = slice(c * tile, (c + 1) * tile)
            part_ref[:, at] = jnp.dot(o_ref[...], w_buf[i, :, at], preferred_element_type=F32).astype(BF16)


def attention(q, rk, rv, kv, lens, weight, column_groups, out_width):
    steps, forks, width = q.shape
    prefix = kv.shape[2]
    heads_kv = rk.shape[2] // HD
    parts = column_groups.shape[0]
    unit_heads = 2
    key_block = prefix
    rows = unit_heads * steps * forks
    return pl.pallas_call(
        functools.partial(attention_kernel, unit_heads, key_block),
        out_shape=[jax.ShapeDtypeStruct((steps * forks, width), BF16)]
        + [jax.ShapeDtypeStruct((steps * forks, out_width), BF16)] * parts,
        in_specs=[SMEM] + [VMEM] * 5 + [pl.BlockSpec(memory_space=pl.ANY)],
        out_specs=[VMEM] * (1 + parts),
        scratch_shapes=[pltpu.VMEM((prefix // key_block, rows, key_block), F32)] * 2
        + [pltpu.VMEM((heads_kv, prefix, 2 * HD), BF16)]
        + [pltpu.VMEM((rows, HD), F32)] * 3
        + [
            pltpu.VMEM((rows, 2 * HD), F32),
            pltpu.VMEM((rows, HD), jnp.int32),
            pltpu.VMEM((width // HD * steps * forks, HD), BF16),
            pltpu.VMEM((parts, weight.shape[0], out_width), BF16),
            pltpu.SemaphoreType.DMA((parts,)),
        ],
        compiler_params=PARAMS,
        cost_estimate=pl.CostEstimate(flops=2 * 10**10, bytes_accessed=6 * 2**20, transcendentals=0),
        name="attention",
    )(column_groups, q, rk, rv, kv, lens, weight)


def project(attended, weight, column_group, width, add, dtype):
    rows, depth = attended.shape
    tile = 1024 if width % 1024 == 0 else width
    tiles = width // tile

    def kernel(group_ref, a_ref, w_ref, *rest):
        o_ref = rest[-1]
        part = jnp.dot(a_ref[...], w_ref[...], preferred_element_type=F32)
        for r in rest[:-1]:
            part = part + r[...].astype(F32)
        o_ref[...] = part.astype(o_ref.dtype)

    in_specs = [
        pl.BlockSpec((rows, depth), lambda i, g: (0, 0)),
        pl.BlockSpec((depth, tile), lambda i, g: (0, g[0] * tiles + i)),
    ]
    operands = [attended, weight]
    in_specs += [pl.BlockSpec((rows, tile), lambda i, g: (0, i))] * len(add)
    operands += add
    return pl.pallas_call(
        kernel,
        out_shape=jax.ShapeDtypeStruct((rows, width), dtype),
        grid_spec=pltpu.PrefetchScalarGridSpec(
            num_scalar_prefetch=1,
            grid=(tiles,),
            in_specs=in_specs,
            out_specs=pl.BlockSpec((rows, tile), lambda i, g: (0, i)),
        ),
        compiler_params=PARAMS,
        cost_estimate=pl.CostEstimate(
            flops=2 * rows * depth * width, bytes_accessed=2 * depth * width, transcendentals=0
        ),
        name="project",
    )(column_group.reshape(1), *operands)


def pack(tables, rows_all, place, capacity, relative):
    replicas, batches = rows_all.shape
    stored, rank, _ = tables[0].shape
    widths = [t.shape[2] for t in tables]

    def kernel(rows_ref, place_ref, *refs):
        out = refs[-1]
        to = pl.program_id(0)

        def step(b, count):
            row = rows_ref[to ^ place_ref[0] if relative else to, b] - place_ref[0] * stored
            mine = (row >= 0) & (row < stored)

            @pl.when(mine)
            def _():
                at = 0
                for ref, width in zip(refs, widths):
                    out[0, count, :, at : at + width] = ref[row]
                    at += width

            return count + mine.astype(jnp.int32)

        lax.fori_loop(0, batches, step, jnp.int32(0))

    return pl.pallas_call(
        kernel,
        out_shape=jax.ShapeDtypeStruct((replicas, capacity, rank, sum(widths)), BF16),
        grid=(replicas,),
        in_specs=[SMEM, SMEM] + [whole(t.shape) for t in tables],
        out_specs=pl.BlockSpec((1, capacity, rank, sum(widths)), lambda i: (i, 0, 0, 0)),
        compiler_params=PARAMS,
        name="pack",
    )(rows_all, place, *tables)


def collect(rows_ref, stored, arrived_ref, selected):
    batches = selected.shape[0]
    for owner in range(arrived_ref.shape[0]):

        def step(b, count):
            row = rows_ref[b] - owner * stored
            there = (row >= 0) & (row < stored)

            @pl.when(there)
            def _():
                selected[b] = arrived_ref[owner, count]

            return count + there.astype(jnp.int32)

        lax.fori_loop(0, batches, step, jnp.int32(0))


def whole(shape):
    return pl.BlockSpec(shape, lambda i: (0,) * len(shape))


def columns(packed, width, block):
    shape = packed.shape[:-1] + (width,)
    return pl.BlockSpec(shape, lambda i: (0,) * (len(shape) - 1) + (block,))


def columns(packed, width, block):
    shape = packed.shape[:-1] + (width,)
    return pl.BlockSpec(shape, lambda i: (0,) * (len(shape) - 1) + (block,))


def batch_mask(rows, forks, batches, rank):
    batch_forks = forks // batches
    row = lax.broadcasted_iota(jnp.int32, (rows, batches * rank), 0)
    column = lax.broadcasted_iota(jnp.int32, (rows, batches * rank), 1)
    return lax.rem(row, forks) // batch_forks == column // rank


def fold(every, rows, forks, batches, rank):
    every = jnp.where(batch_mask(rows, forks, batches, rank), every, 0.0)
    total = every[:, 0:HD]
    for c in range(1, batches * rank // HD):
        total = total + every[:, c * HD : (c + 1) * HD]
    return total


def low_rank(attended, forks, own_rows, stored, arrived):
    rows, depth = attended.shape
    batches = own_rows.shape[0]
    rank = arrived.shape[2]

    def kernel(rows_ref, a_ref, arrived_ref, o_ref, selected):
        collect(rows_ref, stored, arrived_ref, selected)
        every = lax.dot_general(
            a_ref[...],
            selected[...].reshape(batches * rank, depth),
            (((1,), (1,)), ((), ())),
            preferred_element_type=F32,
        )
        o_ref[...] = fold(every, rows, forks, batches, rank)

    return pl.pallas_call(
        kernel,
        out_shape=jax.ShapeDtypeStruct((rows, HD), F32),
        grid=(1,),
        in_specs=[SMEM, whole(attended.shape), columns(arrived, depth, (arrived.shape[3] - depth) // depth)],
        out_specs=whole((rows, HD)),
        scratch_shapes=[pltpu.VMEM((batches, rank, depth), BF16)],
        compiler_params=PARAMS,
        name="low_rank",
    )(own_rows, attended, arrived)


def chosen(own_rows, stored, arrived, width):
    batches = own_rows.shape[0]
    rank = arrived.shape[2]

    def kernel(rows_ref, arrived_ref, o_ref):
        collect(rows_ref, stored, arrived_ref, o_ref)

    return pl.pallas_call(
        kernel,
        out_shape=jax.ShapeDtypeStruct((batches, rank, width), BF16),
        grid=(1,),
        in_specs=[SMEM, columns(arrived, width, 0)],
        out_specs=whole((batches, rank, width)),
        compiler_params=PARAMS,
        name="chosen",
    )(own_rows, arrived)


def finish(base, ranks, forks, up):
    rows, width = base.shape
    batches, rank, _ = up.shape
    tile = min(width, 1024)
    steps = rows // forks

    def kernel(base_ref, up_ref, *rest):
        rank_refs, o_ref = rest[:-1], rest[-1]
        total = rank_refs[0][...]
        for r in rank_refs[1:]:
            total = total + r[...]
        spread = jnp.concatenate([total] * (batches * rank // HD), axis=1)
        spread = jnp.where(batch_mask(rows, forks, batches, rank), spread, 0.0)
        high = spread.astype(BF16)
        low = (spread - high.astype(F32)).astype(BF16)
        columns = up_ref[...].reshape(batches * rank, tile)
        out = jnp.dot(high, columns, preferred_element_type=F32)
        out = out + jnp.dot(low, columns, preferred_element_type=F32)
        out = (out + base_ref[...].astype(F32)).astype(BF16)
        for s in range(steps):
            o_ref[:, s, :] = out[s * forks : (s + 1) * forks, :]

    return pl.pallas_call(
        kernel,
        out_shape=jax.ShapeDtypeStruct((forks, steps, width), BF16),
        grid=(width // tile,),
        in_specs=[
            pl.BlockSpec((rows, tile), lambda i: (0, i)),
            pl.BlockSpec((batches, rank, tile), lambda i: (0, 0, i)),
        ]
        + [whole(r.shape) for r in ranks],
        out_specs=pl.BlockSpec((forks, steps, tile), lambda i: (0, 0, i)),
        compiler_params=SMALL_PARAMS,
        name="finish",
    )(base, up, *ranks)


def lookup(wanted, adapter_table_row):
    matches = wanted[..., None] == jnp.arange(adapter_table_row.shape[0], dtype=jnp.int32)
    return jnp.sum(jnp.where(matches, adapter_table_row, 0), axis=-1)


def body(
    replicas,
    chips,
    queries,
    recent_keys,
    recent_values,
    prefix_key_value,
    prefix_length_each,
    batch_adapter_index,
    adapter_table_row,
    down_weight_table,
    up_weight_table,
    output_weight,
):
    forks, steps, _ = queries.shape
    batches = batch_adapter_index.shape[0]
    capacity = max(2, 2 * batches // replicas)
    model_width = output_weight.shape[1]
    width = model_width // (2 * chips)
    replica = lax.axis_index("replica").astype(jnp.int32)
    tensor = lax.axis_index("tensor").astype(jnp.int32)
    chip, core = tensor // 2, lax.rem(tensor, 2)
    place = replica.reshape(1)

    own_rows = lookup(batch_adapter_index, adapter_table_row)
    stored = down_weight_table.shape[0]
    by_xor = replicas == 4
    if by_xor:
        rows_all = jnp.stack(
            [own_rows]
            + [lax.ppermute(own_rows, "replica", [(z, z ^ d) for z in range(replicas)]) for d in range(1, replicas)]
        )
    else:
        rows_all = lax.all_gather(own_rows, "replica")
    packed = pack([up_weight_table, down_weight_table], rows_all, place, capacity, by_xor)
    arrived = lax.all_to_all(packed, "replica", 0, 0)

    lens = jnp.concatenate([prefix_length_each] * steps)[:, None]
    order = list(range(1, chips)) + [0]
    starts = [lax.rem(chip + e, chips) * 2 for e in order]
    first = [starts[0] + 1 - core, starts[0] + core, starts[-1] + 1 - core]
    first = lax.optimization_barrier((jnp.stack(first), packed))[0]
    attended, *parts = attention(
        queries.transpose(1, 0, 2),
        recent_keys.transpose(1, 0, 2),
        recent_values.transpose(1, 0, 2),
        prefix_key_value,
        lens,
        output_weight,
        first,
        width,
    )
    swap = [(t, t ^ 1) for t in range(2 * chips)]

    def along(e):
        return [(t, (t + 2 * e) % (2 * chips)) for t in range(2 * chips)]

    swapped = [lax.ppermute(p, "tensor", swap) for p in (parts[0], parts[2])]
    sums = []
    for i, (e, g) in enumerate(zip(order[:-1], starts[:-1])):
        if i == 0:
            half, part = swapped[0], parts[1]
        else:
            half = lax.ppermute(project(attended, output_weight, g + 1 - core, width, [], BF16), "tensor", swap)
            part = project(attended, output_weight, g + core, width, [], BF16)
        part = (part.astype(F32) + half.astype(F32)).astype(BF16)
        sums.append(lax.ppermute(part, "tensor", along(e)))
    last = lax.optimization_barrier((attended, part))[0]
    base = project(last, output_weight, starts[-1] + core, width, [swapped[1]] + sums, BF16)

    ready = lax.optimization_barrier((attended, base))[0]
    rank_part = low_rank(ready, forks, own_rows, stored, arrived)
    ranks = [rank_part] + [
        lax.ppermute(rank_part, "tensor", [(t, t ^ e) for t in range(2 * chips)]) for e in range(1, 2 * chips)
    ]
    up = chosen(own_rows, stored, arrived, width)
    return finish(base, ranks, forks, up)


def solution(mesh):
    placed = (
        P(("groups", "replica"), None, "tensor"),
        P(("groups", "replica"), None, "tensor"),
        P(("groups", "replica"), None, "tensor"),
        P(("groups", "replica"), None, None, "tensor"),
        P(("groups", "replica")),
        P(("groups", "replica")),
        P("groups"),
        P("replica", None, "tensor"),
        P("replica", None, "tensor"),
        P("tensor", None),
    )
    return jax.shard_map(
        functools.partial(body, mesh.shape["replica"], mesh.shape["tensor"] // 2),
        mesh=mesh,
        in_specs=placed,
        out_specs=P(("groups", "replica"), None, "tensor"),
        check_vma=False,
    )
```

```python
import functools
import math

import jax
import jax.numpy as jnp
from jax import lax
from jax.experimental import pallas as pl
from jax.experimental.pallas import tpu as pltpu
from jax.sharding import PartitionSpec as P

HD = 128
NEG = -1e30
LOG2_SCALE = math.log2(math.e) / math.sqrt(HD)
BF16, F32 = jnp.bfloat16, jnp.float32
VMEM = pl.BlockSpec(memory_space=pltpu.VMEM)
SMEM = pl.BlockSpec(memory_space=pltpu.SMEM)
SMALL_PARAMS = pltpu.CompilerParams(vmem_limit_bytes=20 * 1024 * 1024)
PARAMS = pltpu.CompilerParams(vmem_limit_bytes=58 * 1024 * 1024)


def attention_kernel(
    unit_heads, key_block, groups_ref, q_ref, rk_ref, rv_ref, kv_ref, lens_ref, w_ref, o_ref, *rest
):
    s_a, s_b, vaug, mx_a, mx_b, mb, acc, lensb, qs, w_buf, sems = rest[-11:]
    part_refs = rest[:-11]
    width_out = w_buf.shape[2]
    loads = [
        pltpu.make_async_copy(
            w_ref.at[:, pl.ds(pl.multiple_of(groups_ref[i] * width_out, width_out), width_out)],
            w_buf.at[i],
            sems.at[i],
        )
        for i in range(len(part_refs))
    ]
    for load in loads:
        load.start()
    steps, forks, width = q_ref.shape
    heads = width // HD
    heads_kv = rk_ref.shape[2] // HD
    group = heads // heads_kv
    head_rows = steps * forks
    rows = unit_heads * head_rows
    units = heads // unit_heads
    prefix = kv_ref.shape[2]
    longest = jnp.max(lens_ref[...])
    blocks = (longest + (key_block - 1)) // key_block
    lens = jnp.broadcast_to(lens_ref[...], (head_rows, HD))
    for i in range(unit_heads):
        lensb[i * head_rows : (i + 1) * head_rows, :] = lens
    for v in range(heads_kv):
        vaug[v, :, 0:HD] = kv_ref[0, 1, :, v * HD : (v + 1) * HD]
        vaug[v, :, HD : 2 * HD] = jnp.ones((prefix, HD), BF16)
    for h in range(heads):
        qs[h * head_rows : (h + 1) * head_rows, :] = q_ref[:, :, h * HD : (h + 1) * HD].reshape(head_rows, HD)
    score_refs, max_refs = (s_a, s_b), (mx_a, mx_b)

    def own_scores(u, t):
        parts = []
        for i in range(unit_heads):
            h = u * unit_heads + i
            v = h // group
            k = rk_ref[t, :, v * HD : (v + 1) * HD].astype(F32)
            for s in range(steps):
                if t <= s:
                    at = h * head_rows + s * forks
                    parts.append(jnp.sum(qs[at : at + forks, :].astype(F32) * k, axis=1, keepdims=True))
                else:
                    parts.append(jnp.full((forks, 1), NEG, F32))
        return jnp.concatenate(parts, axis=0)

    def score_block(u, j, s_ref, mx_ref):
        v = (u * unit_heads) // group
        keys = kv_ref[0, 0, pl.ds(pl.multiple_of(j * key_block, key_block), key_block), v * HD : (v + 1) * HD]
        s = lax.dot_general(
            qs[u * rows : (u + 1) * rows, :], keys, (((1,), (1,)), ((), ())), preferred_element_type=F32
        )
        top = mx_ref[...]
        left = lensb[...] - j * key_block
        lane = lax.broadcasted_iota(jnp.int32, (rows, HD), 1)
        for c in range(key_block // HD):
            part = jnp.where(lane + c * HD < left, s[:, c * HD : (c + 1) * HD], NEG)
            top = jnp.maximum(top, part)
            s_ref[j, :, c * HD : (c + 1) * HD] = part
        mx_ref[...] = top

    def value_block(u, j, s_ref):
        v = (u * unit_heads) // group
        top = mb[...]
        parts = [
            jnp.exp2((s_ref[j, :, c * HD : (c + 1) * HD] - top) * LOG2_SCALE).astype(BF16)
            for c in range(key_block // HD)
        ]
        values = vaug[v, pl.ds(pl.multiple_of(j * key_block, key_block), key_block), :]
        acc[...] += jnp.dot(jnp.concatenate(parts, axis=1), values, preferred_element_type=F32)

    for u in range(units + 1):
        done = u - 1
        if u < units:
            max_refs[u % 2][...] = jnp.full((rows, HD), NEG, F32)
        if u > 0:
            own = [own_scores(done, t) for t in range(steps)]
            top = jnp.max(max_refs[done % 2][...], axis=1, keepdims=True)
            for o in own:
                top = jnp.maximum(top, o)
            mb[...] = jnp.broadcast_to(top, (rows, HD))
            acc[...] = jnp.zeros_like(acc)

        @pl.loop(0, blocks)
        def _(j):
            if u < units:
                score_block(u, j, score_refs[u % 2], max_refs[u % 2])
            if u > 0:
                value_block(done, j, score_refs[done % 2])

        if u > 0:
            weights = [jnp.exp2((o - top) * LOG2_SCALE) for o in own]
            total = acc[:, HD : 2 * HD]
            for w in weights:
                total = total + w
            for i in range(unit_heads):
                h = done * unit_heads + i
                v = h // group
                at = slice(i * head_rows, (i + 1) * head_rows)
                mixed = acc[at, 0:HD]
                for t in range(steps):
                    value = rv_ref[t, :, v * HD : (v + 1) * HD].astype(F32)
                    value = jnp.concatenate([value] * steps, axis=0)
                    mixed = mixed + weights[t][at].astype(BF16).astype(F32) * value
                o_ref[:, h * HD : (h + 1) * HD] = (mixed / total[at]).astype(BF16)

    tile = 512
    for i, (load, part_ref) in enumerate(zip(loads, part_refs)):
        load.wait()
        for c in range(width_out // tile):
            at = slice(c * tile, (c + 1) * tile)
            part_ref[:, at] = jnp.dot(o_ref[...], w_buf[i, :, at], preferred_element_type=F32).astype(BF16)


def attention(q, rk, rv, kv, lens, weight, column_groups, out_width):
    steps, forks, width = q.shape
    prefix = kv.shape[2]
    heads_kv = rk.shape[2] // HD
    parts = column_groups.shape[0]
    unit_heads = 2
    key_block = prefix
    rows = unit_heads * steps * forks
    return pl.pallas_call(
        functools.partial(attention_kernel, unit_heads, key_block),
        out_shape=[jax.ShapeDtypeStruct((steps * forks, width), BF16)]
        + [jax.ShapeDtypeStruct((steps * forks, out_width), BF16)] * parts,
        in_specs=[SMEM] + [VMEM] * 5 + [pl.BlockSpec(memory_space=pl.ANY)],
        out_specs=[VMEM] * (1 + parts),
        scratch_shapes=[pltpu.VMEM((prefix // key_block, rows, key_block), F32)] * 2
        + [pltpu.VMEM((heads_kv, prefix, 2 * HD), BF16)]
        + [pltpu.VMEM((rows, HD), F32)] * 3
        + [
            pltpu.VMEM((rows, 2 * HD), F32),
            pltpu.VMEM((rows, HD), jnp.int32),
            pltpu.VMEM((width // HD * steps * forks, HD), BF16),
            pltpu.VMEM((parts, weight.shape[0], out_width), BF16),
            pltpu.SemaphoreType.DMA((parts,)),
        ],
        compiler_params=PARAMS,
        cost_estimate=pl.CostEstimate(flops=2 * 10**10, bytes_accessed=6 * 2**20, transcendentals=0),
        name="attention",
    )(column_groups, q, rk, rv, kv, lens, weight)


def project(attended, weight, column_group, width, add, dtype):
    rows, depth = attended.shape
    tile = 1024 if width % 1024 == 0 else width
    tiles = width // tile

    def kernel(group_ref, a_ref, w_ref, *rest):
        o_ref = rest[-1]
        part = jnp.dot(a_ref[...], w_ref[...], preferred_element_type=F32)
        for r in rest[:-1]:
            part = part + r[...].astype(F32)
        o_ref[...] = part.astype(o_ref.dtype)

    in_specs = [
        pl.BlockSpec((rows, depth), lambda i, g: (0, 0)),
        pl.BlockSpec((depth, tile), lambda i, g: (0, g[0] * tiles + i)),
    ]
    operands = [attended, weight]
    in_specs += [pl.BlockSpec((rows, tile), lambda i, g: (0, i))] * len(add)
    operands += add
    return pl.pallas_call(
        kernel,
        out_shape=jax.ShapeDtypeStruct((rows, width), dtype),
        grid_spec=pltpu.PrefetchScalarGridSpec(
            num_scalar_prefetch=1,
            grid=(tiles,),
            in_specs=in_specs,
            out_specs=pl.BlockSpec((rows, tile), lambda i, g: (0, i)),
        ),
        compiler_params=PARAMS,
        cost_estimate=pl.CostEstimate(
            flops=2 * rows * depth * width, bytes_accessed=2 * depth * width, transcendentals=0
        ),
        name="project",
    )(column_group.reshape(1), *operands)


def pack(tables, rows_all, place, capacity, relative):
    replicas, batches = rows_all.shape
    stored, rank, _ = tables[0].shape
    widths = [t.shape[2] for t in tables]

    def kernel(rows_ref, place_ref, *refs):
        out = refs[-1]
        to = pl.program_id(0)

        def step(b, count):
            row = rows_ref[to ^ place_ref[0] if relative else to, b] - place_ref[0] * stored
            mine = (row >= 0) & (row < stored)

            @pl.when(mine)
            def _():
                at = 0
                for ref, width in zip(refs, widths):
                    out[0, count, :, at : at + width] = ref[row]
                    at += width

            return count + mine.astype(jnp.int32)

        lax.fori_loop(0, batches, step, jnp.int32(0))

    return pl.pallas_call(
        kernel,
        out_shape=jax.ShapeDtypeStruct((replicas, capacity, rank, sum(widths)), BF16),
        grid=(replicas,),
        in_specs=[SMEM, SMEM] + [whole(t.shape) for t in tables],
        out_specs=pl.BlockSpec((1, capacity, rank, sum(widths)), lambda i: (i, 0, 0, 0)),
        compiler_params=PARAMS,
        name="pack",
    )(rows_all, place, *tables)


def collect(rows_ref, stored, arrived_ref, selected):
    batches = selected.shape[0]
    for owner in range(arrived_ref.shape[0]):

        def step(b, count):
            row = rows_ref[b] - owner * stored
            there = (row >= 0) & (row < stored)

            @pl.when(there)
            def _():
                selected[b] = arrived_ref[owner, count]

            return count + there.astype(jnp.int32)

        lax.fori_loop(0, batches, step, jnp.int32(0))


def whole(shape):
    return pl.BlockSpec(shape, lambda i: (0,) * len(shape))


def columns(packed, width, block):
    shape = packed.shape[:-1] + (width,)
    return pl.BlockSpec(shape, lambda i: (0,) * (len(shape) - 1) + (block,))


def columns(packed, width, block):
    shape = packed.shape[:-1] + (width,)
    return pl.BlockSpec(shape, lambda i: (0,) * (len(shape) - 1) + (block,))


def batch_mask(rows, forks, batches, rank):
    batch_forks = forks // batches
    row = lax.broadcasted_iota(jnp.int32, (rows, batches * rank), 0)
    column = lax.broadcasted_iota(jnp.int32, (rows, batches * rank), 1)
    return lax.rem(row, forks) // batch_forks == column // rank


def each_rank(batches, rank):
    k = lax.broadcasted_iota(jnp.int32, (rank, batches * rank), 0)
    column = lax.broadcasted_iota(jnp.int32, (rank, batches * rank), 1)
    return lax.rem(column, rank) == k


def fold(every, rows, forks, batches, rank):
    every = jnp.where(batch_mask(rows, forks, batches, rank), every, 0.0)
    return lax.dot_general(
        each_rank(batches, rank).astype(F32),
        every,
        (((1,), (1,)), ((), ())),
        precision=lax.Precision.HIGHEST,
        preferred_element_type=F32,
    )


def low_rank(attended, forks, own_rows, stored, arrived):
    rows, depth = attended.shape
    batches = own_rows.shape[0]
    rank = arrived.shape[2]

    def kernel(rows_ref, a_ref, arrived_ref, o_ref, selected):
        collect(rows_ref, stored, arrived_ref, selected)
        every = lax.dot_general(
            a_ref[...],
            selected[...].reshape(batches * rank, depth),
            (((1,), (1,)), ((), ())),
            preferred_element_type=F32,
        )
        o_ref[...] = fold(every, rows, forks, batches, rank)

    return pl.pallas_call(
        kernel,
        out_shape=jax.ShapeDtypeStruct((rank, rows), F32),
        grid=(1,),
        in_specs=[SMEM, whole(attended.shape), columns(arrived, depth, (arrived.shape[3] - depth) // depth)],
        out_specs=whole((rank, rows)),
        scratch_shapes=[pltpu.VMEM((batches, rank, depth), BF16)],
        compiler_params=PARAMS,
        name="low_rank",
    )(own_rows, attended, arrived)


def chosen(own_rows, stored, arrived, width):
    batches = own_rows.shape[0]
    rank = arrived.shape[2]
    tile = min(width, 1024)

    def kernel(rows_ref, arrived_ref, o_ref):
        collect(rows_ref, stored, arrived_ref, o_ref)

    return pl.pallas_call(
        kernel,
        out_shape=jax.ShapeDtypeStruct((batches, rank, width), BF16),
        grid=(width // tile,),
        in_specs=[SMEM, pl.BlockSpec(arrived.shape[:3] + (tile,), lambda i: (0, 0, 0, i))],
        out_specs=pl.BlockSpec((batches, rank, tile), lambda i: (0, 0, i)),
        compiler_params=PARAMS,
        name="chosen",
    )(own_rows, arrived)


def finish(base, ranks, forks, up):
    rows, width = base.shape
    batches, rank, _ = up.shape
    tile = min(width, 1024)
    steps = rows // forks

    def kernel(base_ref, up_ref, *rest):
        rank_refs, o_ref = rest[:-1], rest[-1]
        total = rank_refs[0][...]
        for r in rank_refs[1:]:
            total = total + r[...]
        total = total.T
        copies = each_rank(batches, rank).astype(BF16)
        mask = batch_mask(rows, forks, batches, rank)

        def spread(term):
            wide = jnp.dot(term, copies, preferred_element_type=F32)
            return jnp.where(mask, wide, 0.0).astype(BF16)

        first = total.astype(BF16)
        high = spread(first)
        low = spread((total - first.astype(F32)).astype(BF16))
        columns = up_ref[...].reshape(batches * rank, tile)
        out = jnp.dot(high, columns, preferred_element_type=F32)
        out = out + jnp.dot(low, columns, preferred_element_type=F32)
        out = (out + base_ref[...].astype(F32)).astype(BF16)
        for s in range(steps):
            o_ref[:, s, :] = out[s * forks : (s + 1) * forks, :]

    return pl.pallas_call(
        kernel,
        out_shape=jax.ShapeDtypeStruct((forks, steps, width), BF16),
        grid=(width // tile,),
        in_specs=[
            pl.BlockSpec((rows, tile), lambda i: (0, i)),
            pl.BlockSpec((batches, rank, tile), lambda i: (0, 0, i)),
        ]
        + [whole(r.shape) for r in ranks],
        out_specs=pl.BlockSpec((forks, steps, tile), lambda i: (0, 0, i)),
        compiler_params=SMALL_PARAMS,
        name="finish",
    )(base, up, *ranks)


def lookup(wanted, adapter_table_row):
    matches = wanted[..., None] == jnp.arange(adapter_table_row.shape[0], dtype=jnp.int32)
    return jnp.sum(jnp.where(matches, adapter_table_row, 0), axis=-1)


def body(
    replicas,
    chips,
    queries,
    recent_keys,
    recent_values,
    prefix_key_value,
    prefix_length_each,
    batch_adapter_index,
    adapter_table_row,
    down_weight_table,
    up_weight_table,
    output_weight,
):
    forks, steps, _ = queries.shape
    batches = batch_adapter_index.shape[0]
    capacity = max(2, 2 * batches // replicas)
    model_width = output_weight.shape[1]
    width = model_width // (2 * chips)
    replica = lax.axis_index("replica").astype(jnp.int32)
    tensor = lax.axis_index("tensor").astype(jnp.int32)
    chip, core = tensor // 2, lax.rem(tensor, 2)
    place = replica.reshape(1)

    own_rows = lookup(batch_adapter_index, adapter_table_row)
    stored = down_weight_table.shape[0]
    by_xor = replicas == 4
    if by_xor:
        rows_all = jnp.stack(
            [own_rows]
            + [lax.ppermute(own_rows, "replica", [(z, z ^ d) for z in range(replicas)]) for d in range(1, replicas)]
        )
    else:
        rows_all = lax.all_gather(own_rows, "replica")
    packed = pack([up_weight_table, down_weight_table], rows_all, place, capacity, by_xor)
    arrived = lax.all_to_all(packed, "replica", 0, 0)

    lens = jnp.concatenate([prefix_length_each] * steps)[:, None]
    order = list(range(1, chips)) + [0]
    starts = [lax.rem(chip + e, chips) * 2 for e in order]
    first = [starts[0] + 1 - core, starts[0] + core, starts[-1] + 1 - core]
    first = lax.optimization_barrier((jnp.stack(first), packed))[0]
    attended, *parts = attention(
        queries.transpose(1, 0, 2),
        recent_keys.transpose(1, 0, 2),
        recent_values.transpose(1, 0, 2),
        prefix_key_value,
        lens,
        output_weight,
        first,
        width,
    )
    swap = [(t, t ^ 1) for t in range(2 * chips)]

    def along(e):
        return [(t, (t + 2 * e) % (2 * chips)) for t in range(2 * chips)]

    swapped = [lax.ppermute(p, "tensor", swap) for p in (parts[0], parts[2])]
    sums = []
    for i, (e, g) in enumerate(zip(order[:-1], starts[:-1])):
        if i == 0:
            half, part = swapped[0], parts[1]
        else:
            half = lax.ppermute(project(attended, output_weight, g + 1 - core, width, [], BF16), "tensor", swap)
            part = project(attended, output_weight, g + core, width, [], BF16)
        part = (part.astype(F32) + half.astype(F32)).astype(BF16)
        sums.append(lax.ppermute(part, "tensor", along(e)))
    last = lax.optimization_barrier((attended, part))[0]
    base = project(last, output_weight, starts[-1] + core, width, [swapped[1]] + sums, BF16)

    ready = lax.optimization_barrier((attended, base))[0]
    rank_part = low_rank(ready, forks, own_rows, stored, arrived)
    ranks = [rank_part] + [
        lax.ppermute(rank_part, "tensor", [(t, t ^ e) for t in range(2 * chips)]) for e in range(1, 2 * chips)
    ]
    up = chosen(own_rows, stored, arrived, width)
    return finish(base, ranks, forks, up)


def solution(mesh):
    placed = (
        P(("groups", "replica"), None, "tensor"),
        P(("groups", "replica"), None, "tensor"),
        P(("groups", "replica"), None, "tensor"),
        P(("groups", "replica"), None, None, "tensor"),
        P(("groups", "replica")),
        P(("groups", "replica")),
        P("groups"),
        P("replica", None, "tensor"),
        P("replica", None, "tensor"),
        P("tensor", None),
    )
    return jax.shard_map(
        functools.partial(body, mesh.shape["replica"], mesh.shape["tensor"] // 2),
        mesh=mesh,
        in_specs=placed,
        out_specs=P(("groups", "replica"), None, "tensor"),
        check_vma=False,
    )
```

```python
import functools
import math

import jax
import jax.numpy as jnp
from jax import lax
from jax.experimental import pallas as pl
from jax.experimental.pallas import tpu as pltpu
from jax.sharding import PartitionSpec as P

HD = 128
NEG = -1e30
LOG2_SCALE = math.log2(math.e) / math.sqrt(HD)
BF16, F32 = jnp.bfloat16, jnp.float32
VMEM = pl.BlockSpec(memory_space=pltpu.VMEM)
SMEM = pl.BlockSpec(memory_space=pltpu.SMEM)
SMALL_PARAMS = pltpu.CompilerParams(vmem_limit_bytes=20 * 1024 * 1024)
PARAMS = pltpu.CompilerParams(vmem_limit_bytes=58 * 1024 * 1024)


def attention_kernel(
    unit_heads, key_block, groups_ref, q_ref, rk_ref, rv_ref, kv_ref, lens_ref, w_ref, o_ref, *rest
):
    s_a, s_b, vaug, mx_a, mx_b, mb, acc, lensb, qs, w_buf, sems = rest[-11:]
    part_refs = rest[:-11]
    width_out = w_buf.shape[2]
    loads = [
        pltpu.make_async_copy(
            w_ref.at[:, pl.ds(pl.multiple_of(groups_ref[i] * width_out, width_out), width_out)],
            w_buf.at[i],
            sems.at[i],
        )
        for i in range(len(part_refs))
    ]
    for load in loads:
        load.start()
    steps, forks, width = q_ref.shape
    heads = width // HD
    heads_kv = rk_ref.shape[2] // HD
    group = heads // heads_kv
    head_rows = steps * forks
    rows = unit_heads * head_rows
    units = heads // unit_heads
    prefix = kv_ref.shape[2]
    longest = jnp.max(lens_ref[...])
    blocks = (longest + (key_block - 1)) // key_block
    lens = jnp.broadcast_to(lens_ref[...], (head_rows, HD))
    for i in range(unit_heads):
        lensb[i * head_rows : (i + 1) * head_rows, :] = lens
    for v in range(heads_kv):
        vaug[v, :, 0:HD] = kv_ref[0, 1, :, v * HD : (v + 1) * HD]
        vaug[v, :, HD : 2 * HD] = jnp.ones((prefix, HD), BF16)
    for h in range(heads):
        qs[h * head_rows : (h + 1) * head_rows, :] = q_ref[:, :, h * HD : (h + 1) * HD].reshape(head_rows, HD)
    score_refs, max_refs = (s_a, s_b), (mx_a, mx_b)

    def own_scores(u, t):
        parts = []
        for i in range(unit_heads):
            h = u * unit_heads + i
            v = h // group
            k = rk_ref[t, :, v * HD : (v + 1) * HD].astype(F32)
            for s in range(steps):
                if t <= s:
                    at = h * head_rows + s * forks
                    parts.append(jnp.sum(qs[at : at + forks, :].astype(F32) * k, axis=1, keepdims=True))
                else:
                    parts.append(jnp.full((forks, 1), NEG, F32))
        return jnp.concatenate(parts, axis=0)

    def score_block(u, j, s_ref, mx_ref):
        v = (u * unit_heads) // group
        keys = kv_ref[0, 0, pl.ds(pl.multiple_of(j * key_block, key_block), key_block), v * HD : (v + 1) * HD]
        s = lax.dot_general(
            qs[u * rows : (u + 1) * rows, :], keys, (((1,), (1,)), ((), ())), preferred_element_type=F32
        )
        top = mx_ref[...]
        left = lensb[...] - j * key_block
        lane = lax.broadcasted_iota(jnp.int32, (rows, HD), 1)
        for c in range(key_block // HD):
            part = jnp.where(lane + c * HD < left, s[:, c * HD : (c + 1) * HD], NEG)
            top = jnp.maximum(top, part)
            s_ref[j, :, c * HD : (c + 1) * HD] = part
        mx_ref[...] = top

    def value_block(u, j, s_ref):
        v = (u * unit_heads) // group
        top = mb[...]
        parts = [
            jnp.exp2((s_ref[j, :, c * HD : (c + 1) * HD] - top) * LOG2_SCALE).astype(BF16)
            for c in range(key_block // HD)
        ]
        values = vaug[v, pl.ds(pl.multiple_of(j * key_block, key_block), key_block), :]
        acc[...] += jnp.dot(jnp.concatenate(parts, axis=1), values, preferred_element_type=F32)

    for u in range(units + 1):
        done = u - 1
        if u < units:
            max_refs[u % 2][...] = jnp.full((rows, HD), NEG, F32)
        if u > 0:
            own = [own_scores(done, t) for t in range(steps)]
            top = jnp.max(max_refs[done % 2][...], axis=1, keepdims=True)
            for o in own:
                top = jnp.maximum(top, o)
            mb[...] = jnp.broadcast_to(top, (rows, HD))
            acc[...] = jnp.zeros_like(acc)

        @pl.loop(0, blocks)
        def _(j):
            if u < units:
                score_block(u, j, score_refs[u % 2], max_refs[u % 2])
            if u > 0:
                value_block(done, j, score_refs[done % 2])

        if u > 0:
            weights = [jnp.exp2((o - top) * LOG2_SCALE) for o in own]
            total = acc[:, HD : 2 * HD]
            for w in weights:
                total = total + w
            for i in range(unit_heads):
                h = done * unit_heads + i
                v = h // group
                at = slice(i * head_rows, (i + 1) * head_rows)
                mixed = acc[at, 0:HD]
                for t in range(steps):
                    value = rv_ref[t, :, v * HD : (v + 1) * HD].astype(F32)
                    value = jnp.concatenate([value] * steps, axis=0)
                    mixed = mixed + weights[t][at].astype(BF16).astype(F32) * value
                o_ref[:, h * HD : (h + 1) * HD] = (mixed / total[at]).astype(BF16)

    tile = 512
    for i, (load, part_ref) in enumerate(zip(loads, part_refs)):
        load.wait()
        for c in range(width_out // tile):
            at = slice(c * tile, (c + 1) * tile)
            part_ref[:, at] = jnp.dot(o_ref[...], w_buf[i, :, at], preferred_element_type=F32).astype(BF16)


def attention(q, rk, rv, kv, lens, weight, column_groups, out_width):
    steps, forks, width = q.shape
    prefix = kv.shape[2]
    heads_kv = rk.shape[2] // HD
    parts = column_groups.shape[0]
    unit_heads = 2
    key_block = prefix
    rows = unit_heads * steps * forks
    return pl.pallas_call(
        functools.partial(attention_kernel, unit_heads, key_block),
        out_shape=[jax.ShapeDtypeStruct((steps * forks, width), BF16)]
        + [jax.ShapeDtypeStruct((steps * forks, out_width), BF16)] * parts,
        in_specs=[SMEM] + [VMEM] * 5 + [pl.BlockSpec(memory_space=pl.ANY)],
        out_specs=[VMEM] * (1 + parts),
        scratch_shapes=[pltpu.VMEM((prefix // key_block, rows, key_block), F32)] * 2
        + [pltpu.VMEM((heads_kv, prefix, 2 * HD), BF16)]
        + [pltpu.VMEM((rows, HD), F32)] * 3
        + [
            pltpu.VMEM((rows, 2 * HD), F32),
            pltpu.VMEM((rows, HD), jnp.int32),
            pltpu.VMEM((width // HD * steps * forks, HD), BF16),
            pltpu.VMEM((parts, weight.shape[0], out_width), BF16),
            pltpu.SemaphoreType.DMA((parts,)),
        ],
        compiler_params=PARAMS,
        cost_estimate=pl.CostEstimate(flops=2 * 10**10, bytes_accessed=6 * 2**20, transcendentals=0),
        name="attention",
    )(column_groups, q, rk, rv, kv, lens, weight)


def project(attended, weight, column_group, width, add, dtype):
    rows, depth = attended.shape
    tile = 1024 if width % 1024 == 0 else width
    tiles = width // tile

    def kernel(group_ref, a_ref, w_ref, *rest):
        o_ref = rest[-1]
        part = jnp.dot(a_ref[...], w_ref[...], preferred_element_type=F32)
        for r in rest[:-1]:
            part = part + r[...].astype(F32)
        o_ref[...] = part.astype(o_ref.dtype)

    in_specs = [
        pl.BlockSpec((rows, depth), lambda i, g: (0, 0)),
        pl.BlockSpec((depth, tile), lambda i, g: (0, g[0] * tiles + i)),
    ]
    operands = [attended, weight]
    in_specs += [pl.BlockSpec((rows, tile), lambda i, g: (0, i))] * len(add)
    operands += add
    return pl.pallas_call(
        kernel,
        out_shape=jax.ShapeDtypeStruct((rows, width), dtype),
        grid_spec=pltpu.PrefetchScalarGridSpec(
            num_scalar_prefetch=1,
            grid=(tiles,),
            in_specs=in_specs,
            out_specs=pl.BlockSpec((rows, tile), lambda i, g: (0, i)),
        ),
        compiler_params=PARAMS,
        cost_estimate=pl.CostEstimate(
            flops=2 * rows * depth * width, bytes_accessed=2 * depth * width, transcendentals=0
        ),
        name="project",
    )(column_group.reshape(1), *operands)


def pack(tables, rows_all, place, capacity, relative):
    replicas, batches = rows_all.shape
    stored, rank, _ = tables[0].shape
    widths = [t.shape[2] for t in tables]

    def kernel(rows_ref, place_ref, *refs):
        out = refs[-1]
        to = pl.program_id(0)

        def step(b, count):
            row = rows_ref[to ^ place_ref[0] if relative else to, b] - place_ref[0] * stored
            mine = (row >= 0) & (row < stored)

            @pl.when(mine)
            def _():
                at = 0
                for ref, width in zip(refs, widths):
                    out[0, count, :, at : at + width] = ref[row]
                    at += width

            return count + mine.astype(jnp.int32)

        lax.fori_loop(0, batches, step, jnp.int32(0))

    return pl.pallas_call(
        kernel,
        out_shape=jax.ShapeDtypeStruct((replicas, capacity, rank, sum(widths)), BF16),
        grid=(replicas,),
        in_specs=[SMEM, SMEM] + [whole(t.shape) for t in tables],
        out_specs=pl.BlockSpec((1, capacity, rank, sum(widths)), lambda i: (i, 0, 0, 0)),
        compiler_params=PARAMS,
        name="pack",
    )(rows_all, place, *tables)


def collect(rows_ref, stored, arrived_ref, start, selected, sems):
    batches, _, width = selected.shape
    at = pl.ds(start, width)
    for owner in range(arrived_ref.shape[0]):

        def step(b, count):
            row = rows_ref[b] - owner * stored
            there = (row >= 0) & (row < stored)

            @pl.when(there)
            def _():
                pltpu.make_async_copy(arrived_ref.at[owner, count, :, at], selected.at[b], sems.at[b]).start()

            return count + there.astype(jnp.int32)

        lax.fori_loop(0, batches, step, jnp.int32(0))

    @pl.loop(0, batches)
    def _(b):
        pltpu.make_async_copy(arrived_ref.at[0, 0, :, at], selected.at[b], sems.at[b]).wait()


def whole(shape):
    return pl.BlockSpec(shape, lambda i: (0,) * len(shape))


def batch_mask(rows, forks, batches, rank):
    batch_forks = forks // batches
    row = lax.broadcasted_iota(jnp.int32, (rows, batches * rank), 0)
    column = lax.broadcasted_iota(jnp.int32, (rows, batches * rank), 1)
    return lax.rem(row, forks) // batch_forks == column // rank


def each_rank(batches, rank):
    k = lax.broadcasted_iota(jnp.int32, (rank, batches * rank), 0)
    column = lax.broadcasted_iota(jnp.int32, (rank, batches * rank), 1)
    return lax.rem(column, rank) == k


def fold(every, rows, forks, batches, rank):
    every = jnp.where(batch_mask(rows, forks, batches, rank), every, 0.0)
    return lax.dot_general(
        each_rank(batches, rank).astype(F32),
        every,
        (((1,), (1,)), ((), ())),
        precision=lax.Precision.HIGHEST,
        preferred_element_type=F32,
    )


def low_rank(attended, forks, own_rows, stored, arrived):
    rows, depth = attended.shape
    batches = own_rows.shape[0]
    rank = arrived.shape[2]

    def kernel(rows_ref, a_ref, arrived_ref, o_ref, selected, sems):
        collect(rows_ref, stored, arrived_ref, arrived.shape[3] - depth, selected, sems)
        every = lax.dot_general(
            a_ref[...],
            selected[...].reshape(batches * rank, depth),
            (((1,), (1,)), ((), ())),
            preferred_element_type=F32,
        )
        o_ref[...] = fold(every, rows, forks, batches, rank)

    return pl.pallas_call(
        kernel,
        out_shape=jax.ShapeDtypeStruct((rank, rows), F32),
        in_specs=[SMEM, VMEM, pl.BlockSpec(memory_space=pl.ANY)],
        out_specs=VMEM,
        scratch_shapes=[pltpu.VMEM((batches, rank, depth), BF16), pltpu.SemaphoreType.DMA((batches,))],
        compiler_params=PARAMS,
        name="low_rank",
    )(own_rows, attended, arrived)


def chosen(own_rows, stored, arrived, width):
    batches = own_rows.shape[0]
    rank = arrived.shape[2]

    def kernel(rows_ref, arrived_ref, o_ref, sems):
        collect(rows_ref, stored, arrived_ref, 0, o_ref, sems)

    return pl.pallas_call(
        kernel,
        out_shape=jax.ShapeDtypeStruct((batches, rank, width), BF16),
        in_specs=[SMEM, pl.BlockSpec(memory_space=pl.ANY)],
        out_specs=VMEM,
        scratch_shapes=[pltpu.SemaphoreType.DMA((batches,))],
        compiler_params=PARAMS,
        name="chosen",
    )(own_rows, arrived)


def finish(base, ranks, forks, up):
    rows, width = base.shape
    batches, rank, _ = up.shape
    tile = min(width, 1024)
    steps = rows // forks

    def kernel(base_ref, up_ref, *rest):
        rank_refs, o_ref = rest[:-1], rest[-1]
        total = rank_refs[0][...]
        for r in rank_refs[1:]:
            total = total + r[...]
        total = total.T
        copies = each_rank(batches, rank).astype(BF16)
        mask = batch_mask(rows, forks, batches, rank)

        def spread(term):
            wide = jnp.dot(term, copies, preferred_element_type=F32)
            return jnp.where(mask, wide, 0.0).astype(BF16)

        first = total.astype(BF16)
        high = spread(first)
        low = spread((total - first.astype(F32)).astype(BF16))
        columns = up_ref[...].reshape(batches * rank, tile)
        out = jnp.dot(high, columns, preferred_element_type=F32)
        out = out + jnp.dot(low, columns, preferred_element_type=F32)
        out = (out + base_ref[...].astype(F32)).astype(BF16)
        for s in range(steps):
            o_ref[:, s, :] = out[s * forks : (s + 1) * forks, :]

    return pl.pallas_call(
        kernel,
        out_shape=jax.ShapeDtypeStruct((forks, steps, width), BF16),
        grid=(width // tile,),
        in_specs=[
            pl.BlockSpec((rows, tile), lambda i: (0, i)),
            pl.BlockSpec((batches, rank, tile), lambda i: (0, 0, i)),
        ]
        + [whole(r.shape) for r in ranks],
        out_specs=pl.BlockSpec((forks, steps, tile), lambda i: (0, 0, i)),
        compiler_params=SMALL_PARAMS,
        name="finish",
    )(base, up, *ranks)


def lookup(wanted, adapter_table_row):
    matches = wanted[..., None] == jnp.arange(adapter_table_row.shape[0], dtype=jnp.int32)
    return jnp.sum(jnp.where(matches, adapter_table_row, 0), axis=-1)


def body(
    replicas,
    chips,
    queries,
    recent_keys,
    recent_values,
    prefix_key_value,
    prefix_length_each,
    batch_adapter_index,
    adapter_table_row,
    down_weight_table,
    up_weight_table,
    output_weight,
):
    forks, steps, _ = queries.shape
    batches = batch_adapter_index.shape[0]
    capacity = max(2, 2 * batches // replicas)
    model_width = output_weight.shape[1]
    width = model_width // (2 * chips)
    replica = lax.axis_index("replica").astype(jnp.int32)
    tensor = lax.axis_index("tensor").astype(jnp.int32)
    chip, core = tensor // 2, lax.rem(tensor, 2)
    place = replica.reshape(1)

    own_rows = lookup(batch_adapter_index, adapter_table_row)
    stored = down_weight_table.shape[0]
    by_xor = replicas == 4
    if by_xor:
        rows_all = jnp.stack(
            [own_rows]
            + [lax.ppermute(own_rows, "replica", [(z, z ^ d) for z in range(replicas)]) for d in range(1, replicas)]
        )
    else:
        rows_all = lax.all_gather(own_rows, "replica")
    packed = pack([up_weight_table, down_weight_table], rows_all, place, capacity, by_xor)
    arrived = lax.all_to_all(packed, "replica", 0, 0)

    lens = jnp.concatenate([prefix_length_each] * steps)[:, None]
    order = list(range(1, chips)) + [0]
    starts = [lax.rem(chip + e, chips) * 2 for e in order]
    first = [starts[0] + 1 - core, starts[0] + core, starts[-1] + 1 - core]
    first = lax.optimization_barrier((jnp.stack(first), packed))[0]
    attended, *parts = attention(
        queries.transpose(1, 0, 2),
        recent_keys.transpose(1, 0, 2),
        recent_values.transpose(1, 0, 2),
        prefix_key_value,
        lens,
        output_weight,
        first,
        width,
    )
    swap = [(t, t ^ 1) for t in range(2 * chips)]

    def along(e):
        return [(t, (t + 2 * e) % (2 * chips)) for t in range(2 * chips)]

    swapped = [lax.ppermute(p, "tensor", swap) for p in (parts[0], parts[2])]
    sums = []
    for i, (e, g) in enumerate(zip(order[:-1], starts[:-1])):
        if i == 0:
            half, part = swapped[0], parts[1]
        else:
            half = lax.ppermute(project(attended, output_weight, g + 1 - core, width, [], BF16), "tensor", swap)
            part = project(attended, output_weight, g + core, width, [], BF16)
        part = (part.astype(F32) + half.astype(F32)).astype(BF16)
        sums.append(lax.ppermute(part, "tensor", along(e)))
    last = lax.optimization_barrier((attended, part))[0]
    base = project(last, output_weight, starts[-1] + core, width, [swapped[1]] + sums, BF16)

    ready = lax.optimization_barrier((attended, base))[0]
    rank_part = low_rank(ready, forks, own_rows, stored, arrived)
    ranks = [rank_part] + [
        lax.ppermute(rank_part, "tensor", [(t, t ^ e) for t in range(2 * chips)]) for e in range(1, 2 * chips)
    ]
    up = chosen(own_rows, stored, arrived, width)
    return finish(base, ranks, forks, up)


def solution(mesh):
    placed = (
        P(("groups", "replica"), None, "tensor"),
        P(("groups", "replica"), None, "tensor"),
        P(("groups", "replica"), None, "tensor"),
        P(("groups", "replica"), None, None, "tensor"),
        P(("groups", "replica")),
        P(("groups", "replica")),
        P("groups"),
        P("replica", None, "tensor"),
        P("replica", None, "tensor"),
        P("tensor", None),
    )
    return jax.shard_map(
        functools.partial(body, mesh.shape["replica"], mesh.shape["tensor"] // 2),
        mesh=mesh,
        in_specs=placed,
        out_specs=P(("groups", "replica"), None, "tensor"),
        check_vma=False,
    )
```

```python
import functools
import math

import jax
import jax.numpy as jnp
from jax import lax
from jax.experimental import pallas as pl
from jax.experimental.pallas import tpu as pltpu
from jax.sharding import PartitionSpec as P

HD = 128
NEG = -1e30
LOG2_SCALE = math.log2(math.e) / math.sqrt(HD)
BF16, F32 = jnp.bfloat16, jnp.float32
VMEM = pl.BlockSpec(memory_space=pltpu.VMEM)
SMEM = pl.BlockSpec(memory_space=pltpu.SMEM)
SMALL_PARAMS = pltpu.CompilerParams(vmem_limit_bytes=20 * 1024 * 1024)
PARAMS = pltpu.CompilerParams(vmem_limit_bytes=58 * 1024 * 1024)


def attention_kernel(
    unit_heads, key_block, groups_ref, q_ref, rk_ref, rv_ref, kv_ref, lens_ref, w_ref, o_ref, *rest
):
    s_a, s_b, vaug, mx_a, mx_b, mb, acc, lensb, qs, w_buf, sems = rest[-11:]
    part_refs = rest[:-11]
    width_out = w_buf.shape[2]
    loads = [
        pltpu.make_async_copy(
            w_ref.at[:, pl.ds(pl.multiple_of(groups_ref[i] * width_out, width_out), width_out)],
            w_buf.at[i],
            sems.at[i],
        )
        for i in range(len(part_refs))
    ]
    for load in loads:
        load.start()
    steps, forks, width = q_ref.shape
    heads = width // HD
    heads_kv = rk_ref.shape[2] // HD
    group = heads // heads_kv
    head_rows = steps * forks
    rows = unit_heads * head_rows
    units = heads // unit_heads
    prefix = kv_ref.shape[2]
    longest = jnp.max(lens_ref[...])
    blocks = (longest + (key_block - 1)) // key_block
    lens = jnp.broadcast_to(lens_ref[...], (head_rows, HD))
    for i in range(unit_heads):
        lensb[i * head_rows : (i + 1) * head_rows, :] = lens
    for v in range(heads_kv):
        vaug[v, :, 0:HD] = kv_ref[0, 1, :, v * HD : (v + 1) * HD]
        vaug[v, :, HD : 2 * HD] = jnp.ones((prefix, HD), BF16)
    for h in range(heads):
        qs[h * head_rows : (h + 1) * head_rows, :] = q_ref[:, :, h * HD : (h + 1) * HD].reshape(head_rows, HD)
    score_refs, max_refs = (s_a, s_b), (mx_a, mx_b)

    def own_scores(u, t):
        parts = []
        for i in range(unit_heads):
            h = u * unit_heads + i
            v = h // group
            k = rk_ref[t, :, v * HD : (v + 1) * HD].astype(F32)
            for s in range(steps):
                if t <= s:
                    at = h * head_rows + s * forks
                    parts.append(jnp.sum(qs[at : at + forks, :].astype(F32) * k, axis=1, keepdims=True))
                else:
                    parts.append(jnp.full((forks, 1), NEG, F32))
        return jnp.concatenate(parts, axis=0)

    def score_block(u, j, s_ref, mx_ref):
        v = (u * unit_heads) // group
        keys = kv_ref[0, 0, pl.ds(pl.multiple_of(j * key_block, key_block), key_block), v * HD : (v + 1) * HD]
        s = lax.dot_general(
            qs[u * rows : (u + 1) * rows, :], keys, (((1,), (1,)), ((), ())), preferred_element_type=F32
        )
        top = mx_ref[...]
        left = lensb[...] - j * key_block
        lane = lax.broadcasted_iota(jnp.int32, (rows, HD), 1)
        for c in range(key_block // HD):
            part = jnp.where(lane + c * HD < left, s[:, c * HD : (c + 1) * HD], NEG)
            top = jnp.maximum(top, part)
            s_ref[j, :, c * HD : (c + 1) * HD] = part
        mx_ref[...] = top

    def value_block(u, j, s_ref):
        v = (u * unit_heads) // group
        top = mb[...]
        parts = [
            jnp.exp2((s_ref[j, :, c * HD : (c + 1) * HD] - top) * LOG2_SCALE).astype(BF16)
            for c in range(key_block // HD)
        ]
        values = vaug[v, pl.ds(pl.multiple_of(j * key_block, key_block), key_block), :]
        acc[...] += jnp.dot(jnp.concatenate(parts, axis=1), values, preferred_element_type=F32)

    for u in range(units + 1):
        done = u - 1
        if u < units:
            max_refs[u % 2][...] = jnp.full((rows, HD), NEG, F32)
        if u > 0:
            own = [own_scores(done, t) for t in range(steps)]
            top = jnp.max(max_refs[done % 2][...], axis=1, keepdims=True)
            for o in own:
                top = jnp.maximum(top, o)
            mb[...] = jnp.broadcast_to(top, (rows, HD))
            acc[...] = jnp.zeros_like(acc)

        @pl.loop(0, blocks)
        def _(j):
            if u < units:
                score_block(u, j, score_refs[u % 2], max_refs[u % 2])
            if u > 0:
                value_block(done, j, score_refs[done % 2])

        if u > 0:
            weights = [jnp.exp2((o - top) * LOG2_SCALE) for o in own]
            total = acc[:, HD : 2 * HD]
            for w in weights:
                total = total + w
            for i in range(unit_heads):
                h = done * unit_heads + i
                v = h // group
                at = slice(i * head_rows, (i + 1) * head_rows)
                mixed = acc[at, 0:HD]
                for t in range(steps):
                    value = rv_ref[t, :, v * HD : (v + 1) * HD].astype(F32)
                    value = jnp.concatenate([value] * steps, axis=0)
                    mixed = mixed + weights[t][at].astype(BF16).astype(F32) * value
                o_ref[:, h * HD : (h + 1) * HD] = (mixed / total[at]).astype(BF16)

    tile = 512
    for i, (load, part_ref) in enumerate(zip(loads, part_refs)):
        load.wait()
        for c in range(width_out // tile):
            at = slice(c * tile, (c + 1) * tile)
            part_ref[:, at] = jnp.dot(o_ref[...], w_buf[i, :, at], preferred_element_type=F32).astype(BF16)


def attention(q, rk, rv, kv, lens, weight, column_groups, out_width):
    steps, forks, width = q.shape
    prefix = kv.shape[2]
    heads_kv = rk.shape[2] // HD
    parts = column_groups.shape[0]
    unit_heads = 2
    key_block = prefix
    rows = unit_heads * steps * forks
    return pl.pallas_call(
        functools.partial(attention_kernel, unit_heads, key_block),
        out_shape=[jax.ShapeDtypeStruct((steps * forks, width), BF16)]
        + [jax.ShapeDtypeStruct((steps * forks, out_width), BF16)] * parts,
        in_specs=[SMEM] + [VMEM] * 5 + [pl.BlockSpec(memory_space=pl.ANY)],
        out_specs=[VMEM] * (1 + parts),
        scratch_shapes=[pltpu.VMEM((prefix // key_block, rows, key_block), F32)] * 2
        + [pltpu.VMEM((heads_kv, prefix, 2 * HD), BF16)]
        + [pltpu.VMEM((rows, HD), F32)] * 3
        + [
            pltpu.VMEM((rows, 2 * HD), F32),
            pltpu.VMEM((rows, HD), jnp.int32),
            pltpu.VMEM((width // HD * steps * forks, HD), BF16),
            pltpu.VMEM((parts, weight.shape[0], out_width), BF16),
            pltpu.SemaphoreType.DMA((parts,)),
        ],
        compiler_params=PARAMS,
        cost_estimate=pl.CostEstimate(flops=2 * 10**10, bytes_accessed=6 * 2**20, transcendentals=0),
        name="attention",
    )(column_groups, q, rk, rv, kv, lens, weight)


def project(attended, weight, column_group, width, add, dtype):
    rows, depth = attended.shape
    tile = 1024 if width % 1024 == 0 else width
    tiles = width // tile

    def kernel(group_ref, a_ref, w_ref, *rest):
        o_ref = rest[-1]
        part = jnp.dot(a_ref[...], w_ref[...], preferred_element_type=F32)
        for r in rest[:-1]:
            part = part + r[...].astype(F32)
        o_ref[...] = part.astype(o_ref.dtype)

    in_specs = [
        pl.BlockSpec((rows, depth), lambda i, g: (0, 0)),
        pl.BlockSpec((depth, tile), lambda i, g: (0, g[0] * tiles + i)),
    ]
    operands = [attended, weight]
    in_specs += [pl.BlockSpec((rows, tile), lambda i, g: (0, i))] * len(add)
    operands += add
    return pl.pallas_call(
        kernel,
        out_shape=jax.ShapeDtypeStruct((rows, width), dtype),
        grid_spec=pltpu.PrefetchScalarGridSpec(
            num_scalar_prefetch=1,
            grid=(tiles,),
            in_specs=in_specs,
            out_specs=pl.BlockSpec((rows, tile), lambda i, g: (0, i)),
        ),
        compiler_params=PARAMS,
        cost_estimate=pl.CostEstimate(
            flops=2 * rows * depth * width, bytes_accessed=2 * depth * width, transcendentals=0
        ),
        name="project",
    )(column_group.reshape(1), *operands)


def pack(tables, rows_all, place, capacity, relative):
    replicas, batches = rows_all.shape
    stored, rank, _ = tables[0].shape
    widths = [t.shape[2] for t in tables]

    def kernel(rows_ref, place_ref, *refs):
        out = refs[-1]
        to = pl.program_id(0)

        def step(b, count):
            row = rows_ref[to ^ place_ref[0] if relative else to, b] - place_ref[0] * stored
            mine = (row >= 0) & (row < stored)

            @pl.when(mine)
            def _():
                at = 0
                for ref, width in zip(refs, widths):
                    out[0, count, :, at : at + width] = ref[row]
                    at += width

            return count + mine.astype(jnp.int32)

        lax.fori_loop(0, batches, step, jnp.int32(0))

    return pl.pallas_call(
        kernel,
        out_shape=jax.ShapeDtypeStruct((replicas, capacity, rank, sum(widths)), BF16),
        grid=(replicas,),
        in_specs=[SMEM, SMEM] + [whole(t.shape) for t in tables],
        out_specs=pl.BlockSpec((1, capacity, rank, sum(widths)), lambda i: (i, 0, 0, 0)),
        compiler_params=PARAMS,
        name="pack",
    )(rows_all, place, *tables)


def collect(rows_ref, stored, arrived_ref, start, selected, sems):
    batches, _, width = selected.shape
    at = pl.ds(start, width)
    for owner in range(arrived_ref.shape[0]):

        def step(b, count):
            row = rows_ref[b] - owner * stored
            there = (row >= 0) & (row < stored)

            @pl.when(there)
            def _():
                pltpu.make_async_copy(arrived_ref.at[owner, count, :, at], selected.at[b], sems.at[b]).start()

            return count + there.astype(jnp.int32)

        lax.fori_loop(0, batches, step, jnp.int32(0))

    @pl.loop(0, batches)
    def _(b):
        pltpu.make_async_copy(arrived_ref.at[0, 0, :, at], selected.at[b], sems.at[b]).wait()


def whole(shape):
    return pl.BlockSpec(shape, lambda i: (0,) * len(shape))


def batch_mask(rows, forks, batches, rank):
    batch_forks = forks // batches
    row = lax.broadcasted_iota(jnp.int32, (rows, batches * rank), 0)
    column = lax.broadcasted_iota(jnp.int32, (rows, batches * rank), 1)
    return lax.rem(row, forks) // batch_forks == column // rank


def each_rank(batches, rank):
    k = lax.broadcasted_iota(jnp.int32, (rank, batches * rank), 0)
    column = lax.broadcasted_iota(jnp.int32, (rank, batches * rank), 1)
    return lax.rem(column, rank) == k


def fold(every, rows, forks, batches, rank):
    every = jnp.where(batch_mask(rows, forks, batches, rank), every, 0.0)
    return lax.dot_general(
        each_rank(batches, rank).astype(F32),
        every,
        (((1,), (1,)), ((), ())),
        precision=lax.Precision.HIGHEST,
        preferred_element_type=F32,
    )


def low_rank(attended, forks, own_rows, stored, arrived):
    rows, depth = attended.shape
    batches = own_rows.shape[0]
    rank = arrived.shape[2]

    def kernel(rows_ref, a_ref, arrived_ref, o_ref, selected, sems):
        collect(rows_ref, stored, arrived_ref, arrived.shape[3] - depth, selected, sems)
        every = lax.dot_general(
            a_ref[...],
            selected[...].reshape(batches * rank, depth),
            (((1,), (1,)), ((), ())),
            preferred_element_type=F32,
        )
        o_ref[...] = fold(every, rows, forks, batches, rank)

    return pl.pallas_call(
        kernel,
        out_shape=jax.ShapeDtypeStruct((rank, rows), F32),
        in_specs=[SMEM, VMEM, pl.BlockSpec(memory_space=pl.ANY)],
        out_specs=VMEM,
        scratch_shapes=[pltpu.VMEM((batches, rank, depth), BF16), pltpu.SemaphoreType.DMA((batches,))],
        compiler_params=SMALL_PARAMS,
        name="low_rank",
    )(own_rows, attended, arrived)


def chosen(own_rows, stored, arrived, width):
    batches = own_rows.shape[0]
    rank = arrived.shape[2]

    def kernel(rows_ref, arrived_ref, o_ref, sems):
        collect(rows_ref, stored, arrived_ref, 0, o_ref, sems)

    return pl.pallas_call(
        kernel,
        out_shape=jax.ShapeDtypeStruct((batches, rank, width), BF16),
        in_specs=[SMEM, pl.BlockSpec(memory_space=pl.ANY)],
        out_specs=VMEM,
        scratch_shapes=[pltpu.SemaphoreType.DMA((batches,))],
        compiler_params=SMALL_PARAMS,
        name="chosen",
    )(own_rows, arrived)


def finish(base, ranks, forks, up):
    rows, width = base.shape
    batches, rank, _ = up.shape
    tile = min(width, 1024)
    steps = rows // forks

    def kernel(base_ref, up_ref, *rest):
        rank_refs, o_ref = rest[:-1], rest[-1]
        total = rank_refs[0][...]
        for r in rank_refs[1:]:
            total = total + r[...]
        total = total.T
        copies = each_rank(batches, rank).astype(BF16)
        mask = batch_mask(rows, forks, batches, rank)

        def spread(term):
            wide = jnp.dot(term, copies, preferred_element_type=F32)
            return jnp.where(mask, wide, 0.0).astype(BF16)

        first = total.astype(BF16)
        high = spread(first)
        low = spread((total - first.astype(F32)).astype(BF16))
        columns = up_ref[...].reshape(batches * rank, tile)
        out = jnp.dot(high, columns, preferred_element_type=F32)
        out = out + jnp.dot(low, columns, preferred_element_type=F32)
        out = (out + base_ref[...].astype(F32)).astype(BF16)
        for s in range(steps):
            o_ref[:, s, :] = out[s * forks : (s + 1) * forks, :]

    return pl.pallas_call(
        kernel,
        out_shape=jax.ShapeDtypeStruct((forks, steps, width), BF16),
        grid=(width // tile,),
        in_specs=[
            pl.BlockSpec((rows, tile), lambda i: (0, i)),
            pl.BlockSpec((batches, rank, tile), lambda i: (0, 0, i)),
        ]
        + [whole(r.shape) for r in ranks],
        out_specs=pl.BlockSpec((forks, steps, tile), lambda i: (0, 0, i)),
        compiler_params=SMALL_PARAMS,
        name="finish",
    )(base, up, *ranks)


def lookup(wanted, adapter_table_row):
    matches = wanted[..., None] == jnp.arange(adapter_table_row.shape[0], dtype=jnp.int32)
    return jnp.sum(jnp.where(matches, adapter_table_row, 0), axis=-1)


def body(
    replicas,
    chips,
    queries,
    recent_keys,
    recent_values,
    prefix_key_value,
    prefix_length_each,
    batch_adapter_index,
    adapter_table_row,
    down_weight_table,
    up_weight_table,
    output_weight,
):
    forks, steps, _ = queries.shape
    batches = batch_adapter_index.shape[0]
    capacity = max(2, 2 * batches // replicas)
    model_width = output_weight.shape[1]
    width = model_width // (2 * chips)
    replica = lax.axis_index("replica").astype(jnp.int32)
    tensor = lax.axis_index("tensor").astype(jnp.int32)
    chip, core = tensor // 2, lax.rem(tensor, 2)
    place = replica.reshape(1)

    own_rows = lookup(batch_adapter_index, adapter_table_row)
    stored = down_weight_table.shape[0]
    by_xor = replicas == 4
    if by_xor:
        rows_all = jnp.stack(
            [own_rows]
            + [lax.ppermute(own_rows, "replica", [(z, z ^ d) for z in range(replicas)]) for d in range(1, replicas)]
        )
    else:
        rows_all = lax.all_gather(own_rows, "replica")
    packed = pack([up_weight_table, down_weight_table], rows_all, place, capacity, by_xor)
    arrived = lax.all_to_all(packed, "replica", 0, 0)

    lens = jnp.concatenate([prefix_length_each] * steps)[:, None]
    order = list(range(1, chips)) + [0]
    starts = [lax.rem(chip + e, chips) * 2 for e in order]
    first = [starts[0] + 1 - core, starts[0] + core, starts[-1] + 1 - core]
    first = lax.optimization_barrier((jnp.stack(first), packed))[0]
    attended, *parts = attention(
        queries.transpose(1, 0, 2),
        recent_keys.transpose(1, 0, 2),
        recent_values.transpose(1, 0, 2),
        prefix_key_value,
        lens,
        output_weight,
        first,
        width,
    )
    swap = [(t, t ^ 1) for t in range(2 * chips)]

    def along(e):
        return [(t, (t + 2 * e) % (2 * chips)) for t in range(2 * chips)]

    swapped = [lax.ppermute(p, "tensor", swap) for p in (parts[0], parts[2])]
    sums = []
    for i, (e, g) in enumerate(zip(order[:-1], starts[:-1])):
        if i == 0:
            half, part = swapped[0], parts[1]
        else:
            half = lax.ppermute(project(attended, output_weight, g + 1 - core, width, [], BF16), "tensor", swap)
            part = project(attended, output_weight, g + core, width, [], BF16)
        part = (part.astype(F32) + half.astype(F32)).astype(BF16)
        sums.append(lax.ppermute(part, "tensor", along(e)))
    last = lax.optimization_barrier((attended, part))[0]
    base = project(last, output_weight, starts[-1] + core, width, [swapped[1]] + sums, BF16)

    ready = lax.optimization_barrier((attended, base))[0]
    rank_part = low_rank(ready, forks, own_rows, stored, arrived)
    ranks = [rank_part] + [
        lax.ppermute(rank_part, "tensor", [(t, t ^ e) for t in range(2 * chips)]) for e in range(1, 2 * chips)
    ]
    up = chosen(own_rows, stored, arrived, width)
    return finish(base, ranks, forks, up)


def solution(mesh):
    placed = (
        P(("groups", "replica"), None, "tensor"),
        P(("groups", "replica"), None, "tensor"),
        P(("groups", "replica"), None, "tensor"),
        P(("groups", "replica"), None, None, "tensor"),
        P(("groups", "replica")),
        P(("groups", "replica")),
        P("groups"),
        P("replica", None, "tensor"),
        P("replica", None, "tensor"),
        P("tensor", None),
    )
    return jax.shard_map(
        functools.partial(body, mesh.shape["replica"], mesh.shape["tensor"] // 2),
        mesh=mesh,
        in_specs=placed,
        out_specs=P(("groups", "replica"), None, "tensor"),
        check_vma=False,
    )
```
